128 devices in a mesh: qrow: 16 (over z, y), kcol: 8 (over x, core).
Axes of the slice: x: 4, y: 4, z: 4, core: 2. Of those that a mesh axis runs over, the one named last changes fastest.
Arguments:
- features: bfloat16 [16384, 1024], P(('qrow', 'kcol')), may hold values from -24 to 24
- node_ids: int32 [16384], P(('qrow', 'kcol')), may hold values from 0 to 511
- token_embed: bfloat16 [512, 1024], replicated, may hold values from -3 to 3
- w_query: bfloat16 [1024, 1024], replicated, may hold values from -0.1875 to 0.1875
- w_key: bfloat16 [1024, 1024], replicated, may hold values from -0.1875 to 0.1875
- w_value: bfloat16 [1024, 1024], replicated, may hold values from -0.1875 to 0.1875
- w_out: bfloat16 [1024, 1024], replicated, may hold values from -0.1875 to 0.1875
- slopes: float32 [16], replicated, may hold values from 1 to 3
- chan_scale: float32 [64], replicated, may hold values from -6 to 6
- chan_shift: float32 [64], replicated, may hold values from -4 to 4
- edge_proj: bfloat16 [64, 32], replicated, may hold values from -0.75 to 0.75
- edge_value: bfloat16 [128, 8, 4, 128, 128], P('qrow', 'kcol'), may hold values from -4 to 240
- key_index: int32 [128, 8, 4], P('qrow', 'kcol'), may hold values from 0 to 15
- counts: int32 [128, 8], P('qrow', 'kcol'), may hold values from 0 to 4, as said below
- w_up: bfloat16 [1024, 4096], P(None, 'qrow'), may hold values from -0.1875 to 0.1875
- w_down: bfloat16 [4096, 1024], P('qrow'), may hold values from -0.09375 to 0.09375
Outputs:
- output: bfloat16 [16384, 1024], P(('qrow', 'kcol'))
The draws below stay inside these ranges and needn't reach their ends.
Inputs may be any that keep to these rules, and one draw needn't show every extreme that they name: counts[g, c] is 1 or more in the column c = (g % 8), so every query node has a live tile.
All inputs are finite; a program needn't handle non-finite values.
Results may differ from the reference program's by a relative error of at most 0.013.
Values may be sent and summed in bfloat16 or wider, within the bound.
No kernel may reach another device: no remote copies, remote signals or barrier semaphores. Data moves between devices by JAX's collectives and lax.ppermute only.
A program may use at most 192 MiB of HBM per device.

```python
import math
import jax
import jax.numpy as jnp
import numpy as np
from jax import lax

D = 1024
HEADS = 16
FF = 4096
EC = 64
VOCAB = 512
BLK = 128
NODE_DEV = 128
KCAP = 4
BPD = 1
QB_ROW = 8
KB_COL = 16
NODES = 16384
QBLOCKS = 128
N_QROW = 16
N_KCOL = 8


def tile_lists(key):
    key = jax.random.fold_in(key, 101)
    key_count, key_pick, key_perm = jax.random.split(key, 3)
    block_ids = jnp.arange(QBLOCKS, dtype=jnp.int32)
    local_ids = block_ids % QB_ROW
    diag_col = local_ids // BPD
    diag_blk = block_ids // QB_ROW * BPD + local_ids % BPD
    column = jnp.arange(N_KCOL, dtype=jnp.int32)
    own_col = column[None, :] == diag_col[:, None]
    live_draw = jax.random.randint(key_count, (QBLOCKS, N_KCOL), 0, KCAP + 1)
    live_draw = jnp.where(own_col, jnp.maximum(live_draw, 1), live_draw)
    chosen = jax.random.randint(key_pick, (), 0, QBLOCKS * N_KCOL)
    flat_ids = jnp.arange(QBLOCKS * N_KCOL, dtype=jnp.int32).reshape(QBLOCKS, N_KCOL)
    live_draw = jnp.where(flat_ids == chosen, KCAP, live_draw)
    perm_keys = jax.random.split(key_perm, QBLOCKS * N_KCOL)
    orders = jax.vmap(lambda one_key: jax.random.permutation(one_key, KB_COL))(perm_keys).reshape(QBLOCKS, N_KCOL, KB_COL)
    rank_of = jnp.argsort(orders, axis=-1, stable=True).astype(jnp.int32)
    blocks = jnp.arange(KB_COL, dtype=jnp.int32)
    diag_first = own_col[:, :, None] & (blocks[None, None, :] == diag_blk[:, None, None])
    rank_of = jnp.where(diag_first, -1, rank_of)
    picked = jnp.argsort(rank_of, axis=-1, stable=True)[:, :, :KCAP].astype(jnp.int32)
    return (live_draw.astype(jnp.int32), picked)


def draw_key_index(key, part):
    return tile_lists(key)[1]


def draw_counts(key, part):
    return tile_lists(key)[0]


def draw_features(key, part):
    key = jax.random.fold_in(key, 3)
    key_noise, key_rows, key_cols = jax.random.split(key, 3)
    log_low = math.log(0.3)
    log_high = math.log(3.0)
    row_scale = jnp.exp(jax.random.uniform(key_rows, (NODES, 1), jnp.float32, log_low, log_high))
    col_scale = jnp.exp(jax.random.uniform(key_cols, (1, D), jnp.float32, log_low, log_high))
    noise = jax.random.normal(key_noise, (NODES, D), jnp.float32)
    return jnp.clip(0.5 * noise * row_scale * col_scale, -24.0, 24.0).astype(jnp.bfloat16)


def draw_edge_value(key, part):
    key = jax.random.fold_in(key, 7)
    key_base = jax.random.fold_in(key, 0)
    full_shape = (QBLOCKS, N_KCOL, KCAP, BLK, BLK)
    drawn_value = jnp.clip(jax.random.normal(key_base, full_shape, jnp.float32), -4.0, 4.0)
    return drawn_value.astype(jnp.bfloat16)


def plant(array, rng, least, high):
    longest = array.shape.index(max(array.shape))
    spots = []
    for shift in (0, 1):
        where = [jax.random.randint(jax.random.fold_in(rng, axis), (), 0, length) for axis, length in enumerate(array.shape)]
        where[longest] = (where[longest] + shift) % array.shape[longest]
        spots.append(tuple(where))
    return array.at[spots[0]].set(least).at[spots[1]].set(high)


def block_scale(own_key, dims, pieces, low, top_value):
    gain, own = 1.0, jax.random.fold_in(own_key, 6)
    for dim, shards_of in pieces:
        draws = jnp.exp(jax.random.uniform(jax.random.fold_in(own, dim), (shards_of,), jnp.float32, low / len(pieces), top_value / len(pieces)))
        gain = gain * jnp.repeat(draws, dims[dim] // shards_of).reshape([-1 if axis == dim else 1 for axis in range(len(dims))])
    return gain


def cumulative_ranks(count, skew):
    portions = [(1 << 20) // math.isqrt(rank ** skew) + 1 for rank in range(1, count + 1)]
    scale = 1 + sum(portions) // (1 << 30)
    return np.cumsum(np.array([max(1, weight // scale) for weight in portions]))


def ranked(rng, shape, count, skew):
    table = cumulative_ranks(count, skew)
    ticket = jax.random.randint(jax.random.fold_in(rng, 1), shape, 0, int(table[count - 1]))
    rank = jnp.searchsorted(jnp.asarray(table, jnp.int32), ticket, side="right")
    return jax.random.permutation(jax.random.fold_in(rng, 2), count)[rank].astype(jnp.int32)


def scatter_about(key, extent, deviation, reach, shards=(), held_as=jnp.bfloat16):
    level = block_scale(key, extent, shards, -0.22, 0.18) if shards else 1.0
    drawn = jax.random.normal(key, extent, jnp.float32) * deviation * level
    return jnp.minimum(jnp.maximum(drawn, -reach), reach).astype(held_as)


def setup_inputs(seed: int = 0) -> dict:
    key_of = jax.random.split(jax.random.key(seed), 17)
    return {
        "features": draw_features(jax.random.fold_in(key_of[16], 71), 0),
        "node_ids": plant(ranked(key_of[1], (NODES,), VOCAB, 2), jax.random.fold_in(key_of[1], 3), 0, VOCAB - 1).astype(jnp.int32),
        "token_embed": scatter_about(key_of[2], (VOCAB, D), 0.5, 3.0),
        "w_query": scatter_about(key_of[3], (D, D), D ** -0.5, 0.1875),
        "w_key": scatter_about(key_of[4], (D, D), D ** -0.5, 0.1875),
        "w_value": scatter_about(key_of[5], (D, D), D ** -0.5, 0.1875),
        "w_out": scatter_about(key_of[6], (D, D), D ** -0.5, 0.1875),
        "slopes": jnp.clip(jnp.exp(jax.random.uniform(key_of[7], (HEADS,), jnp.float32, math.log(1.0), math.log(3.0))), 1.0, 3.0),
        "chan_scale": scatter_about(key_of[8], (EC,), 2.0, 6.0, (), jnp.float32),
        "chan_shift": scatter_about(key_of[9], (EC,), 1.0, 4.0, (), jnp.float32),
        "edge_proj": scatter_about(key_of[10], (EC, 2 * HEADS), EC ** -0.5, 0.75),
        "edge_value": draw_edge_value(jax.random.fold_in(key_of[16], 71), 0),
        "key_index": draw_key_index(jax.random.fold_in(key_of[16], 71), 0),
        "counts": draw_counts(jax.random.fold_in(key_of[16], 71), 0),
        "w_up": scatter_about(key_of[14], (D, FF), D ** -0.5, 0.1875, ((1, 16),)),
        "w_down": scatter_about(key_of[15], (FF, D), FF ** -0.5, 0.09375, ((0, 16),)),
    }


NEG_FILL = -1e+30

def layer_norm(values):
    average = lax.optimization_barrier(jnp.mean(values, axis=-1, keepdims=True))
    centered = values - average
    spread = lax.optimization_barrier(jnp.mean(centered * centered, axis=-1, keepdims=True))
    return centered * lax.rsqrt(spread + 1e-05)

def tile_step(carried, queries, key_tiles, value_tiles, edge_tile, live_rows, slopes, chan_scale, chan_shift, edge_proj):
    run_max, run_sum, run_num = carried
    block_total, tile_rows, model_width = queries.shape
    head_count = slopes.shape[0]
    head_dim = model_width // head_count
    edge_f = edge_tile.astype(jnp.float32)
    channels = jax.nn.sigmoid(edge_f[:, None] * chan_scale[None, :, None, None] + chan_shift[None, :, None, None]).astype(jnp.bfloat16)
    edge_terms = jnp.einsum('aeij,eh->ahij', channels.astype(jnp.float32), edge_proj.astype(jnp.float32))
    bias_part = edge_terms[:, :head_count]
    gate_part = jax.nn.sigmoid(edge_terms[:, head_count:])
    query_heads = queries.reshape(block_total, tile_rows, head_count, head_dim).astype(jnp.float32)
    key_heads = key_tiles.reshape(block_total, tile_rows, head_count, head_dim).astype(jnp.float32)
    value_heads = value_tiles.reshape(block_total, tile_rows, head_count, head_dim).astype(jnp.float32)
    scores = jnp.einsum('aihd,ajhd->ahij', query_heads, key_heads) * head_dim ** (-0.5)
    scores = scores + bias_part + slopes[None, :, None, None] * edge_f[:, None]
    live_mask = live_rows[:, None, None, None]
    scores = jnp.where(live_mask, scores, NEG_FILL)
    new_max = jnp.maximum(run_max, lax.optimization_barrier(jnp.max(scores, axis=-1)))
    factor = jnp.exp(run_max - new_max)
    exp_scores = jnp.exp(scores - new_max[..., None]) * live_mask.astype(jnp.float32)
    run_sum = run_sum * factor + lax.optimization_barrier(jnp.sum(exp_scores, axis=-1))
    gated = (exp_scores * gate_part).astype(jnp.bfloat16)
    contrib = jnp.einsum('ahij,ajhd->aihd', gated.astype(jnp.float32), value_heads)
    run_num = run_num * jnp.swapaxes(factor, 1, 2)[..., None] + contrib
    return (new_max, run_sum, run_num)

def reference(features, node_ids, token_embed, w_query, w_key, w_value, w_out, slopes, chan_scale, chan_shift, edge_proj, edge_value, key_index, counts, w_up, w_down):
    embedded = features.astype(jnp.float32) + token_embed[node_ids].astype(jnp.float32)
    normed = layer_norm(embedded).astype(jnp.bfloat16)
    query_all = jnp.dot(normed, w_query, preferred_element_type=jnp.float32).astype(jnp.bfloat16)
    key_all = jnp.dot(normed, w_key, preferred_element_type=jnp.float32).astype(jnp.bfloat16)
    value_all = jnp.dot(normed, w_value, preferred_element_type=jnp.float32).astype(jnp.bfloat16)
    head_count = slopes.shape[0]
    query_grid = query_all.reshape(N_QROW, QB_ROW, BLK, D)
    key_grid = key_all.reshape(N_QROW, N_KCOL, NODE_DEV, D)
    value_grid = value_all.reshape(N_QROW, N_KCOL, NODE_DEV, D)
    edge_grid = edge_value.reshape(N_QROW, QB_ROW, N_KCOL, KCAP, BLK, BLK)
    index_grid = key_index.reshape(N_QROW, QB_ROW, N_KCOL, KCAP)
    count_grid = counts.reshape(N_QROW, QB_ROW, N_KCOL)

    def one_row(packed):
        queries, edge_cells, indices, live_counts = packed

        def visit_tile(step_idx, carried):
            column = step_idx // KCAP
            slot_pos = step_idx % KCAP
            col_keys = lax.dynamic_index_in_dim(key_grid, column, 1, keepdims=False).reshape(KB_COL, BLK, D)
            col_values = lax.dynamic_index_in_dim(value_grid, column, 1, keepdims=False).reshape(KB_COL, BLK, D)
            edge_cell = lax.dynamic_index_in_dim(edge_cells, column, 1, keepdims=False)
            edge_tile = lax.dynamic_index_in_dim(edge_cell, slot_pos, 1, keepdims=False)
            index_cell = lax.dynamic_index_in_dim(indices, column, 1, keepdims=False)
            picked = lax.dynamic_index_in_dim(index_cell, slot_pos, 1, keepdims=False)
            count_cell = lax.dynamic_index_in_dim(live_counts, column, 1, keepdims=False)
            live_rows = count_cell > slot_pos
            return tile_step(carried, queries, col_keys[picked], col_values[picked], edge_tile, live_rows, slopes, chan_scale, chan_shift, edge_proj)
        initial = (jnp.full((QB_ROW, head_count, BLK), NEG_FILL, jnp.float32), jnp.zeros((QB_ROW, head_count, BLK), jnp.float32), jnp.zeros((QB_ROW, BLK, head_count, D // head_count), jnp.float32))
        row_top, row_total, numerators = lax.fori_loop(0, N_KCOL * KCAP, visit_tile, initial)
        attended = numerators / jnp.swapaxes(row_total, 1, 2)[..., None]
        return attended.reshape(QB_ROW * BLK, D)
    attended = lax.map(one_row, (query_grid, edge_grid, index_grid, count_grid)).reshape(NODES, D).astype(jnp.bfloat16)
    residual = embedded + jnp.dot(attended, w_out, preferred_element_type=jnp.float32)
    normed_two = layer_norm(residual).astype(jnp.bfloat16)
    hidden = jax.nn.gelu(jnp.dot(normed_two, w_up, preferred_element_type=jnp.float32), approximate=False).astype(jnp.bfloat16)
    return (residual + jnp.dot(hidden, w_down, preferred_element_type=jnp.float32)).astype(jnp.bfloat16)
```

```python
import jax
import jax.numpy as jnp
from jax import lax
from jax.experimental import pallas as pl
from jax.experimental.pallas import tpu as pltpu
from jax.sharding import PartitionSpec as P

NEG_FILL = -1e30
VMEM_BYTES = 56 * 1024 * 1024


def layer_norm(values):
    average = jnp.mean(values, axis=-1, keepdims=True)
    centered = values - average
    spread = jnp.mean(centered * centered, axis=-1, keepdims=True)
    return centered * lax.rsqrt(spread + 1e-05)


def edge_kernel(
    tile_of,
    slot_of,
    live_of,
    slopes,
    offsets,
    edge_ref,
    mix_ref,
    scale_ref,
    shift_ref,
    base_ref,
    gate_ref,
    edge_t,
    chans,
):
    step = pl.program_id(0)
    heads = base_ref.shape[1]
    rows, lanes = edge_t.shape
    channel_count = scale_ref.shape[0]

    @pl.when(live_of[step] > 0)
    def _():
        edge_t[...] = edge_ref[0].astype(jnp.float32).T
        scale = scale_ref[...]
        shift = shift_ref[...]
        for part in range(rows // 16):
            slot = part % 2
            for half in range(2):
                for within in range(8):
                    row = part * 16 + half * 8 + within
                    line = jnp.broadcast_to(edge_t[row : row + 1, :], scale.shape)
                    pre = (line * scale + shift).astype(jnp.bfloat16)
                    chans[
                        slot,
                        within * channel_count : (within + 1) * channel_count,
                        half * lanes : (half + 1) * lanes,
                    ] = jnp.tanh(pre)
            terms = jnp.dot(mix_ref[...], chans[slot], preferred_element_type=jnp.float32)
            low = edge_t[part * 16 : part * 16 + 8, :]
            high = edge_t[part * 16 + 8 : part * 16 + 16, :]
            for head in range(heads):
                block = terms[head * 8 : head * 8 + 8]
                base_ref[0, head, part * 16 : part * 16 + 8, :] = block[:, :lanes] + (
                    low * slopes[head] + offsets[head]
                )
                base_ref[0, head, part * 16 + 8 : part * 16 + 16, :] = block[:, lanes:] + (
                    high * slopes[head] + offsets[head]
                )
                gate_block = terms[(heads + head) * 8 : (heads + head) * 8 + 8]
                both = jnp.concatenate([gate_block[:, :lanes], gate_block[:, lanes:]], axis=0)
                gate_ref[0, head, part * 16 : part * 16 + 16, :] = (
                    0.5 + 0.5 * jnp.tanh(both + offsets[heads + head])
                ).astype(jnp.bfloat16)


def edge_stage(tile_of, slot_of, live_of, slopes, offsets, edges, mix, scale, shift):
    tiles, rows, lanes = edges.shape
    heads = slopes.shape[0]
    grid_spec = pltpu.PrefetchScalarGridSpec(
        num_scalar_prefetch=5,
        grid=(tiles,),
        in_specs=[
            pl.BlockSpec((1, rows, lanes), lambda s, tile, *_: (tile[s], 0, 0)),
            pl.BlockSpec(mix.shape, lambda s, *_: (0, 0)),
            pl.BlockSpec(scale.shape, lambda s, *_: (0, 0)),
            pl.BlockSpec(shift.shape, lambda s, *_: (0, 0)),
        ],
        out_specs=[
            pl.BlockSpec((1, heads, rows, lanes), lambda s, tile, slot, *_: (slot[s], 0, 0, 0)),
            pl.BlockSpec((1, heads, rows, lanes), lambda s, tile, slot, *_: (slot[s], 0, 0, 0)),
        ],
        scratch_shapes=[
            pltpu.VMEM((rows, lanes), jnp.float32),
            pltpu.VMEM((2, mix.shape[1], 2 * lanes), jnp.bfloat16),
        ],
    )
    return pl.pallas_call(
        edge_kernel,
        grid_spec=grid_spec,
        out_shape=[
            jax.ShapeDtypeStruct((tiles, heads, rows, lanes), jnp.float32),
            jax.ShapeDtypeStruct((tiles, heads, rows, lanes), jnp.bfloat16),
        ],
        compiler_params=pltpu.CompilerParams(vmem_limit_bytes=VMEM_BYTES),
        cost_estimate=pl.CostEstimate(
            flops=tiles * 2 * rows * lanes * 64 * 256,
            bytes_accessed=tiles * rows * lanes * heads * 6,
            transcendentals=tiles * rows * lanes * 80,
        ),
        name="edge_terms",
    )(tile_of, slot_of, live_of, slopes, offsets, edges, mix, scale, shift)


def attend_kernel(
    slot_of,
    block_of,
    key_of,
    live_of,
    first_of,
    last_of,
    base_ref,
    gate_ref,
    key_ref,
    value_ref,
    query_ref,
    num_ref,
    stat_ref,
    query_pairs,
    acc,
    tops,
    totals,
):
    step = pl.program_id(0)
    heads = base_ref.shape[1]
    rows = base_ref.shape[2]
    lanes = base_ref.shape[3]
    head_dim = acc.shape[0] // heads

    @pl.when(first_of[step] > 0)
    def _():
        block = block_of[step]
        acc[...] = jnp.zeros_like(acc)
        tops[...] = jnp.full_like(tops, NEG_FILL)
        totals[...] = jnp.zeros_like(totals)
        blank = jnp.zeros((head_dim, lanes), jnp.bfloat16)
        for pair in range(heads // 2):
            upper = query_ref[block, pair * 2 * head_dim : (pair * 2 + 1) * head_dim, :]
            lower = query_ref[block, (pair * 2 + 1) * head_dim : (pair * 2 + 2) * head_dim, :]
            query_pairs[pair, :head_dim, :lanes] = upper
            query_pairs[pair, :head_dim, lanes:] = blank
            query_pairs[pair, head_dim:, :lanes] = blank
            query_pairs[pair, head_dim:, lanes:] = lower

    @pl.when(live_of[step] > 0)
    def _():
        key_block = key_of[step]
        for pair in range(heads // 2):
            width = 2 * head_dim
            keys = key_ref[key_block, :, pair * width : (pair + 1) * width]
            both = jnp.dot(keys, query_pairs[pair], preferred_element_type=jnp.float32)
            for side in range(2):
                head = pair * 2 + side
                span = slice(head * head_dim, (head + 1) * head_dim)
                scores = both[:, side * lanes : (side + 1) * lanes] + base_ref[0, head]
                old_top = tops[head : head + 1, :]
                new_top = jnp.maximum(old_top, jnp.max(scores, axis=0, keepdims=True))
                factor = jnp.exp(old_top - new_top)
                weights = jnp.exp(scores - new_top)
                totals[head : head + 1, :] = totals[head : head + 1, :] * factor + jnp.sum(
                    weights, axis=0, keepdims=True
                )
                tops[head : head + 1, :] = new_top
                gated = (weights * gate_ref[0, head].astype(jnp.float32)).astype(jnp.bfloat16)
                part = jnp.dot(
                    value_ref[key_block, span, :], gated, preferred_element_type=jnp.float32
                )
                acc[span, :] = acc[span, :] * factor + part

    @pl.when(last_of[step] > 0)
    def _():
        for head in range(heads):
            span = slice(head * head_dim, (head + 1) * head_dim)
            total = totals[head : head + 1, :]
            inverse = jnp.where(total > 0.0, 1.0 / jnp.where(total > 0.0, total, 1.0), 0.0)
            num_ref[0, span, :] = (acc[span, :] * inverse).astype(num_ref.dtype)
        stat_ref[0, :heads, :] = tops[...]
        stat_ref[0, heads:, :] = totals[...]


def attend_stage(lists, base, gate, keys, values, queries):
    block_total, width, lanes = queries.shape
    tiles, heads, rows, _ = base.shape
    whole = lambda array: pl.BlockSpec(
        array.shape, lambda s, *_: (0,) * array.ndim, pipeline_mode=pl.Buffered(1)
    )
    grid_spec = pltpu.PrefetchScalarGridSpec(
        num_scalar_prefetch=6,
        grid=(tiles,),
        in_specs=[
            pl.BlockSpec((1, heads, rows, lanes), lambda s, slot, *_: (slot[s], 0, 0, 0)),
            pl.BlockSpec((1, heads, rows, lanes), lambda s, slot, *_: (slot[s], 0, 0, 0)),
            whole(keys),
            whole(values),
            whole(queries),
        ],
        out_specs=[
            pl.BlockSpec((1, width, lanes), lambda s, slot, block, *_: (block[s], 0, 0)),
            pl.BlockSpec((1, 2 * heads, lanes), lambda s, slot, block, *_: (block[s], 0, 0)),
        ],
        scratch_shapes=[
            pltpu.VMEM((heads // 2, 2 * width // heads, 2 * lanes), jnp.bfloat16),
            pltpu.VMEM((width, lanes), jnp.float32),
            pltpu.VMEM((heads, lanes), jnp.float32),
            pltpu.VMEM((heads, lanes), jnp.float32),
        ],
    )
    return pl.pallas_call(
        attend_kernel,
        grid_spec=grid_spec,
        out_shape=[
            jax.ShapeDtypeStruct((block_total, width, lanes), jnp.bfloat16),
            jax.ShapeDtypeStruct((block_total, 2 * heads, lanes), jnp.float32),
        ],
        compiler_params=pltpu.CompilerParams(vmem_limit_bytes=VMEM_BYTES),
        cost_estimate=pl.CostEstimate(
            flops=tiles * 4 * rows * lanes * width,
            bytes_accessed=tiles * rows * lanes * heads * 6,
            transcendentals=tiles * rows * lanes * heads,
        ),
        name="attend",
    )(*lists, base, gate, keys, values, queries)


def step_lists(cell_counts, cell_index):
    block_total, slot_count = cell_index.shape
    total = block_total * slot_count
    slots = jnp.arange(slot_count, dtype=jnp.int32)[None, :]
    visits = jnp.maximum(cell_counts, 1)[:, None]
    used = (slots < visits).reshape(total)
    order = jnp.arange(total, dtype=jnp.int32)
    place = jnp.sum((used[None, :] & (order[None, :] < order[:, None])).astype(jnp.int32), axis=1)
    steps = jnp.sum(used.astype(jnp.int32))
    slot_of = jnp.minimum(order, steps - 1)
    chosen = used[None, :] & (place[None, :] == slot_of[:, None])
    fresh = (order < steps).astype(jnp.int32)
    pick = lambda values: jnp.sum(
        jnp.where(chosen, values.reshape(1, total).astype(jnp.int32), 0), axis=1
    )
    blocks = jnp.broadcast_to(
        jnp.arange(block_total, dtype=jnp.int32)[:, None], (block_total, slot_count)
    )
    tile_of = pick(order)
    block_of = pick(blocks)
    key_of = pick(cell_index)
    live_of = pick(slots < cell_counts[:, None]) * fresh
    first_of = pick(jnp.broadcast_to(slots == 0, (block_total, slot_count))) * fresh
    last_of = pick(slots == visits - 1) * fresh
    return tile_of, slot_of, block_of, key_of, live_of, first_of, last_of


def mix_matrix(edge_proj, heads):
    channel_count, outs = edge_proj.shape
    factors = jnp.where(jnp.arange(outs) < heads, 0.5, 0.25).astype(jnp.bfloat16)
    scaled = (edge_proj * factors[None, :]).T
    eye = jnp.eye(8, dtype=jnp.bfloat16)
    mixed = scaled[:, None, None, :] * eye[None, :, :, None]
    offsets = jnp.sum(scaled.astype(jnp.float32), axis=1)
    return mixed.reshape(outs * 8, 8 * channel_count), offsets


def local(
    features,
    node_ids,
    token_embed,
    w_query,
    w_key,
    w_value,
    w_out,
    slopes,
    chan_scale,
    chan_shift,
    edge_proj,
    edge_value,
    key_index,
    counts,
    w_up,
    w_down,
):
    node_dev, width = features.shape
    vocab_size = token_embed.shape[0]
    heads = slopes.shape[0]
    head_dim = width // heads
    rows = edge_value.shape[-1]
    one_hot = (
        node_ids[:, None] == lax.broadcasted_iota(jnp.int32, (node_dev, vocab_size), 1)
    ).astype(jnp.bfloat16)
    embedded = features.astype(jnp.float32) + jnp.dot(
        one_hot, token_embed, preferred_element_type=jnp.float32
    )
    normed = layer_norm(embedded).astype(jnp.bfloat16)
    row_nodes = lax.all_gather(normed, "kcol", axis=0)
    column_nodes = lax.all_gather(normed, "qrow", axis=0)
    up_all = lax.all_gather(w_up, "qrow", axis=0)
    down_all = lax.all_gather(w_down, "qrow", axis=0)

    tile_of, slot_of, block_of, key_of, live_of, first_of, last_of = step_lists(
        counts[:, 0], key_index[:, 0]
    )
    mix, offsets = mix_matrix(edge_proj, heads)
    spread = lambda vector: jnp.broadcast_to((0.5 * vector)[:, None], (vector.shape[0], rows))
    base, gate = edge_stage(
        tile_of,
        slot_of,
        live_of,
        slopes,
        offsets,
        edge_value.reshape(-1, rows, rows),
        mix,
        spread(chan_scale),
        spread(chan_shift),
    )
    queries = (
        jnp.einsum("kd,gnk->gdn", w_query, row_nodes, preferred_element_type=jnp.float32).astype(
            jnp.bfloat16
        )
        * jnp.bfloat16(head_dim ** (-0.5))
    )
    keys = jnp.einsum(
        "gnk,kd->gnd", column_nodes, w_key, preferred_element_type=jnp.float32
    ).astype(jnp.bfloat16)
    values = jnp.einsum(
        "kd,gnk->gdn", w_value, column_nodes, preferred_element_type=jnp.float32
    ).astype(jnp.bfloat16)
    partial, stats = attend_stage(
        (slot_of, block_of, key_of, live_of, first_of, last_of), base, gate, keys, values, queries
    )
    partial = lax.all_to_all(partial, "kcol", 0, 0, tiled=True)
    stats = lax.all_to_all(stats, "kcol", 0, 0, tiled=True)
    tops, totals = stats[:, :heads], stats[:, heads:]
    shares = totals * jnp.exp(tops - jnp.max(tops, axis=0, keepdims=True))
    shares = shares / jnp.sum(shares, axis=0, keepdims=True)
    attended = jnp.sum(
        partial.astype(jnp.float32).reshape(-1, heads, head_dim, rows) * shares[:, :, None, :],
        axis=0,
    )
    attended = attended.reshape(width, rows).T.astype(jnp.bfloat16)
    residual = embedded + jnp.dot(attended, w_out, preferred_element_type=jnp.float32)
    normed_two = layer_norm(residual).astype(jnp.bfloat16)
    hidden = jax.nn.gelu(
        jnp.einsum("nk,skf->snf", normed_two, up_all, preferred_element_type=jnp.float32),
        approximate=False,
    ).astype(jnp.bfloat16)
    ffn = jnp.einsum("snf,sfd->nd", hidden, down_all, preferred_element_type=jnp.float32)
    return (residual + ffn).astype(jnp.bfloat16)


def solution(mesh):
    placed = (
        P(("qrow", "kcol"), None),
        P(("qrow", "kcol")),
        P(),
        P(),
        P(),
        P(),
        P(),
        P(),
        P(),
        P(),
        P(),
        P("qrow", "kcol", None, None, None),
        P("qrow", "kcol", None),
        P("qrow", "kcol"),
        P(None, "qrow"),
        P("qrow", None),
    )
    return jax.shard_map(
        local, mesh=mesh, in_specs=placed, out_specs=P(("qrow", "kcol"), None), check_vma=False
    )
```

```python
import functools

import jax
import jax.numpy as jnp
from jax import lax
from jax.experimental import pallas as pl
from jax.experimental.pallas import tpu as pltpu
from jax.sharding import PartitionSpec as P

NEG_FILL = -1e30
CUTS = (6, 11, 22)
EDGE_VMEM = 56 * 1024 * 1024
ATTEND_VMEM = 56 * 1024 * 1024
TAIL_VMEM = 24 * 1024 * 1024


def layer_norm(values):
    average = jnp.mean(values, axis=-1, keepdims=True)
    centered = values - average
    spread = jnp.mean(centered * centered, axis=-1, keepdims=True)
    return centered * lax.rsqrt(spread + 1e-05)


def list_kernel(counts_ref, index_ref, place_ref, lists_ref):
    block_total, slot_count = index_ref.shape
    total = block_total * slot_count
    row_hi, row_lo, col_hi, col_lo = place_ref[0], place_ref[1], place_ref[2], place_ref[3]

    def relative(theirs, ours):
        gap = (theirs - ours + 4) & 3
        return jnp.where(gap == 0, 0, jnp.where(gap == 3, 1, gap + 1))

    filled = jnp.int32(0)
    for block in range(block_total):
        count = counts_ref[block, 0]
        other = jnp.where(col_lo == block % 2, 0, 4)
        partner = other + relative(jnp.int32(block // 2), col_hi)
        visits = jnp.maximum(count, 1)
        for slot in range(slot_count):

            @pl.when(slot < visits)
            def _(at=filled, block=block, slot=slot, partner=partner, count=count, visits=visits):
                key_block = index_ref[block, slot]
                lists_ref[0, at] = jnp.int32(block * slot_count + slot)
                lists_ref[1, at] = at
                lists_ref[2, at] = partner
                lists_ref[3, at] = 4 * relative(key_block >> 2, row_hi) + relative(
                    key_block & 3, row_lo
                )
                lists_ref[4, at] = (slot < count).astype(jnp.int32)
                lists_ref[5, at] = jnp.int32(slot == 0)
                lists_ref[6, at] = (visits == slot + 1).astype(jnp.int32)

            filled = filled + (slot < visits).astype(jnp.int32)

    @pl.loop(0, total)
    def _(step):
        @pl.when(step >= filled)
        def _():
            for row in range(4):
                lists_ref[row, step] = lists_ref[row, filled - 1]
            for row in range(4, 7):
                lists_ref[row, step] = jnp.int32(0)


def list_stage(counts, index, place):
    scalars = pl.BlockSpec(memory_space=pltpu.SMEM)
    return pl.pallas_call(
        list_kernel,
        in_specs=[scalars] * 3,
        out_specs=scalars,
        out_shape=jax.ShapeDtypeStruct((8, index.shape[0] * index.shape[1]), jnp.int32),
        name="lists",
    )(counts, index, place)


def edge_kernel(start, lists, offsets, edge_ref, mix_ref, scale_ref, shift_ref, *rest):
    bias_ref, gate_ref, edge_t, chans = rest[-4:]
    step = pl.program_id(0) + start
    heads = bias_ref.shape[1]
    rows, lanes = edge_t.shape
    channel_count = scale_ref.shape[0]

    @pl.when(lists[4, step] > 0)
    def _():
        edge_t[...] = edge_ref[0].astype(jnp.float32).T
        scale = scale_ref[...]
        shift = shift_ref[...]
        for part in range(rows // 16):
            slot = part % 2
            for half in range(2):
                for within in range(8):
                    row = part * 16 + half * 8 + within
                    line = jnp.broadcast_to(edge_t[row : row + 1, :], scale.shape)
                    pre = (line * scale + shift).astype(jnp.bfloat16)
                    chans[
                        slot,
                        within * channel_count : (within + 1) * channel_count,
                        half * lanes : (half + 1) * lanes,
                    ] = jnp.tanh(pre)
            terms = jnp.dot(mix_ref[...], chans[slot], preferred_element_type=jnp.float32)
            span = slice(part * 16, part * 16 + 16)
            for head in range(heads):
                block = terms[head * 8 : head * 8 + 8]
                both = jnp.concatenate([block[:, :lanes], block[:, lanes:]], axis=0)
                bias_ref[0, head, span, :] = both.astype(jnp.bfloat16)
                block = terms[(heads + head) * 8 : (heads + head) * 8 + 8]
                both = jnp.concatenate([block[:, :lanes], block[:, lanes:]], axis=0)
                gate_ref[0, head, span, :] = (
                    0.5 + 0.5 * jnp.tanh(both + offsets[heads + head])
                ).astype(jnp.bfloat16)


def edge_stage(start, stop, lists, offsets, edges, mix, scale, shift, heads, held):
    tiles, rows, lanes = edges.shape
    out = pl.BlockSpec((1, heads, rows, lanes), lambda s, lists, *_: (jnp.maximum(lists[1, s + start], start), 0, 0, 0))
    grid_spec = pltpu.PrefetchScalarGridSpec(
        num_scalar_prefetch=2,
        grid=(stop - start,),
        in_specs=[
            pl.BlockSpec((1, rows, lanes), lambda s, lists, *_: (lists[0, s + start], 0, 0)),
            pl.BlockSpec(mix.shape, lambda s, *_: (0, 0)),
            pl.BlockSpec(scale.shape, lambda s, *_: (0, 0)),
            pl.BlockSpec(shift.shape, lambda s, *_: (0, 0)),
        ]
        + [pl.BlockSpec(memory_space=pl.ANY)] * len(held),
        out_specs=[out, out],
        scratch_shapes=[
            pltpu.VMEM((rows, lanes), jnp.float32),
            pltpu.VMEM((2, mix.shape[1], 2 * lanes), jnp.bfloat16),
        ],
    )
    count = stop - start
    return pl.pallas_call(
        functools.partial(edge_kernel, start),
        grid_spec=grid_spec,
        out_shape=[jax.ShapeDtypeStruct((tiles, heads, rows, lanes), jnp.bfloat16)] * 2,
        input_output_aliases={6: 0, 7: 1} if held else {},
        compiler_params=pltpu.CompilerParams(vmem_limit_bytes=EDGE_VMEM),
        cost_estimate=pl.CostEstimate(
            flops=count * 2 * rows * lanes * 64 * 256 * 2,
            bytes_accessed=count * rows * lanes * heads * 4,
            transcendentals=count * rows * lanes * 80,
        ),
        name="edge_terms",
    )(lists, offsets, edges, mix, scale, shift, *held)


def attend_kernel(
    lists,
    slopes,
    offsets,
    edge_ref,
    bias_ref,
    gate_ref,
    key_ref,
    value_ref,
    query_ref,
    num_ref,
    stat_ref,
    query_pairs,
    acc,
    tops,
    totals,
):
    step = pl.program_id(0)
    heads, rows, lanes = bias_ref.shape[1:]
    head_dim = acc.shape[0] // heads

    @pl.when(lists[5, step] > 0)
    def _():
        block = lists[2, step]
        acc[...] = jnp.zeros_like(acc)
        tops[...] = jnp.full_like(tops, NEG_FILL)
        totals[...] = jnp.zeros_like(totals)
        blank = jnp.zeros((head_dim, lanes), jnp.bfloat16)
        for pair in range(heads // 2):
            upper = query_ref[block, pair * 2 * head_dim : (pair * 2 + 1) * head_dim, :]
            lower = query_ref[block, (pair * 2 + 1) * head_dim : (pair * 2 + 2) * head_dim, :]
            query_pairs[pair, :head_dim, :lanes] = upper
            query_pairs[pair, :head_dim, lanes:] = blank
            query_pairs[pair, head_dim:, :lanes] = blank
            query_pairs[pair, head_dim:, lanes:] = lower

    @pl.when(lists[4, step] > 0)
    def _():
        key_block = lists[3, step]
        edge_t = edge_ref[0].astype(jnp.float32).T
        for pair in range(heads // 2):
            width = 2 * head_dim
            keys = key_ref[key_block, :, pair * width : (pair + 1) * width]
            both = jnp.dot(keys, query_pairs[pair], preferred_element_type=jnp.float32)
            for side in range(2):
                head = pair * 2 + side
                span = slice(head * head_dim, (head + 1) * head_dim)
                scores = both[:, side * lanes : (side + 1) * lanes] + (
                    bias_ref[0, head].astype(jnp.float32) + (edge_t * slopes[head] + offsets[head])
                )
                old_top = tops[head : head + 1, :]
                new_top = jnp.maximum(old_top, jnp.max(scores, axis=0, keepdims=True))
                factor = jnp.exp(old_top - new_top)
                weights = jnp.exp(scores - new_top)
                totals[head : head + 1, :] = totals[head : head + 1, :] * factor + jnp.sum(
                    weights, axis=0, keepdims=True
                )
                tops[head : head + 1, :] = new_top
                gated = (weights * gate_ref[0, head].astype(jnp.float32)).astype(jnp.bfloat16)
                part = jnp.dot(
                    value_ref[key_block, span, :], gated, preferred_element_type=jnp.float32
                )
                acc[span, :] = acc[span, :] * factor + part

    @pl.when(lists[6, step] > 0)
    def _():
        for head in range(heads):
            span = slice(head * head_dim, (head + 1) * head_dim)
            total = totals[head : head + 1, :]
            inverse = jnp.where(total > 0.0, 1.0 / jnp.where(total > 0.0, total, 1.0), 0.0)
            num_ref[0, span, :] = (acc[span, :] * inverse).astype(num_ref.dtype)
        stat_ref[0, :heads, :] = tops[...]
        stat_ref[0, heads:, :] = totals[...]


def attend_stage(lists, slopes, offsets, edges, bias, gate, keys, values, queries):
    block_total, width, lanes = queries.shape
    tiles, heads, rows, _ = bias.shape
    whole = lambda array: pl.BlockSpec(
        array.shape, lambda s, *_: (0,) * array.ndim, pipeline_mode=pl.Buffered(1)
    )
    edge_block = pl.BlockSpec((1, heads, rows, lanes), lambda s, lists, *_: (lists[1, s], 0, 0, 0))
    grid_spec = pltpu.PrefetchScalarGridSpec(
        num_scalar_prefetch=3,
        grid=(tiles,),
        in_specs=[
            pl.BlockSpec((1, rows, lanes), lambda s, lists, *_: (lists[0, s], 0, 0)),
            edge_block,
            edge_block,
            whole(keys),
            whole(values),
            whole(queries),
        ],
        out_specs=[
            pl.BlockSpec((1, width, lanes), lambda s, lists, *_: (lists[2, s], 0, 0)),
            pl.BlockSpec((1, 2 * heads, lanes), lambda s, lists, *_: (lists[2, s], 0, 0)),
        ],
        scratch_shapes=[
            pltpu.VMEM((heads // 2, 2 * width // heads, 2 * lanes), jnp.bfloat16),
            pltpu.VMEM((width, lanes), jnp.float32),
            pltpu.VMEM((heads, lanes), jnp.float32),
            pltpu.VMEM((heads, lanes), jnp.float32),
        ],
    )
    return pl.pallas_call(
        attend_kernel,
        grid_spec=grid_spec,
        out_shape=[
            jax.ShapeDtypeStruct((block_total, width, lanes), jnp.bfloat16),
            jax.ShapeDtypeStruct((block_total, 2 * heads, lanes), jnp.float32),
        ],
        compiler_params=pltpu.CompilerParams(vmem_limit_bytes=ATTEND_VMEM),
        cost_estimate=pl.CostEstimate(
            flops=tiles * 16 * rows * lanes * width,
            bytes_accessed=tiles * rows * lanes * heads * 4,
            transcendentals=tiles * rows * lanes * heads,
        ),
        name="attend",
    )(lists, slopes, offsets, edges, bias, gate, keys, values, queries)


def merge_parts(parts, stats, heads):
    top = stats[0][:heads]
    for stat in stats[1:]:
        top = jnp.maximum(top, stat[:heads])
    shares = [stat[heads:] * jnp.exp(stat[:heads] - top) for stat in stats]
    total = sum(shares[1:], shares[0])
    live = total > 0.0
    inverse = jnp.where(live, 1.0 / jnp.where(live, total, 1.0), 0.0)
    return top, total, [share * inverse for share in shares]


def merge_kernel(own_ref, other_ref, own_stat, other_stat, num_ref, stat_ref):
    heads = own_stat.shape[1] // 2
    head_dim = own_ref.shape[1] // heads
    top, total, shares = merge_parts(None, [own_stat[0], other_stat[0]], heads)
    for head in range(heads):
        span = slice(head * head_dim, (head + 1) * head_dim)
        num_ref[0, span, :] = (
            own_ref[0, span, :].astype(jnp.float32) * shares[0][head : head + 1]
            + other_ref[0, span, :].astype(jnp.float32) * shares[1][head : head + 1]
        ).astype(num_ref.dtype)
    stat_ref[0, :heads, :] = top
    stat_ref[0, heads:, :] = total


def merge_stage(own, other, own_stat, other_stat):
    count, width, lanes = other.shape
    stat_rows = other_stat.shape[1]
    block = pl.BlockSpec((1, width, lanes), lambda s: (s, 0, 0))
    stat = pl.BlockSpec((1, stat_rows, lanes), lambda s: (s, 0, 0))
    return pl.pallas_call(
        merge_kernel,
        grid=(count,),
        in_specs=[block, block, stat, stat],
        out_specs=[block, stat],
        out_shape=[
            jax.ShapeDtypeStruct((count, width, lanes), jnp.bfloat16),
            jax.ShapeDtypeStruct((count, stat_rows, lanes), jnp.float32),
        ],
        name="merge",
    )(own, other, own_stat, other_stat)


def tail_kernel(
    core,
    part_0,
    part_1,
    part_2,
    part_3,
    stat_0,
    stat_1,
    stat_2,
    stat_3,
    embedded_ref,
    out_ref,
    own_ref,
    other_ref,
    final_ref,
    attended,
    residual,
    normed,
    acc,
):
    step = pl.program_id(0)

    @pl.when(step == 0)
    def _():
        heads = stat_0.shape[1] // 2
        head_dim = attended.shape[0] // heads
        parts = [part_0, part_1, part_2, part_3]
        stats = [stat[0] for stat in (stat_0, stat_1, stat_2, stat_3)]
        _, _, shares = merge_parts(None, stats, heads)
        for head in range(heads):
            span = slice(head * head_dim, (head + 1) * head_dim)
            merged = parts[0][0, span, :].astype(jnp.float32) * shares[0][head : head + 1]
            for part, share in zip(parts[1:], shares[1:]):
                merged = merged + part[0, span, :].astype(jnp.float32) * share[head : head + 1]
            attended[span, :] = merged
        rows = attended[...].T.astype(jnp.bfloat16)
        values = embedded_ref[...] + jnp.dot(
            rows, out_ref[...], preferred_element_type=jnp.float32
        )
        residual[...] = values
        normed[...] = layer_norm(values).astype(jnp.bfloat16)
        acc[...] = jnp.zeros_like(acc)

    def feed(up_ref, down_ref):
        pre = jnp.dot(normed[...], up_ref[0], preferred_element_type=jnp.float32)
        hidden = (0.5 * pre * (1.0 + lax.erf(pre * (0.5**0.5)))).astype(jnp.bfloat16)
        span = hidden.shape[1]
        for piece in range(acc.shape[1] // span):
            cut = slice(piece * span, (piece + 1) * span)
            acc[:, cut] += jnp.dot(hidden, down_ref[0, cut, :], preferred_element_type=jnp.float32)

    @pl.when(core[0] == 0)
    def _():
        feed(own_ref, other_ref)

    @pl.when(core[0] != 0)
    def _():
        feed(other_ref, own_ref)

    @pl.when(step == pl.num_programs(0) - 1)
    def _():
        final_ref[...] = (residual[...] + acc[...]).astype(final_ref.dtype)


def tail_stage(core, parts, stats, embedded, w_out, own, other):
    shards, width, span = own.shape
    rows = embedded.shape[0]
    lanes = parts[0].shape[2]
    part = pl.BlockSpec((1, width, lanes), lambda s, *_: (0, 0, 0))
    stat = pl.BlockSpec((1, stats[0].shape[1], lanes), lambda s, *_: (0, 0, 0))
    weight = pl.BlockSpec((1, width, span), lambda s, *_: (s, 0, 0))
    flat = lambda array: pl.BlockSpec(array.shape, lambda s, *_: (0, 0))
    grid_spec = pltpu.PrefetchScalarGridSpec(
        num_scalar_prefetch=1,
        grid=(shards,),
        in_specs=[part] * 4 + [stat] * 4 + [flat(embedded), flat(w_out), weight, weight],
        out_specs=pl.BlockSpec((rows, width), lambda s, *_: (0, 0)),
        scratch_shapes=[
            pltpu.VMEM((width, lanes), jnp.float32),
            pltpu.VMEM((rows, width), jnp.float32),
            pltpu.VMEM((rows, width), jnp.bfloat16),
            pltpu.VMEM((rows, width), jnp.float32),
        ],
    )
    return pl.pallas_call(
        tail_kernel,
        grid_spec=grid_spec,
        out_shape=jax.ShapeDtypeStruct((rows, width), jnp.bfloat16),
        compiler_params=pltpu.CompilerParams(vmem_limit_bytes=TAIL_VMEM),
        cost_estimate=pl.CostEstimate(
            flops=4 * rows * width * span * shards,
            bytes_accessed=2 * shards * width * span * 2,
            transcendentals=rows * span * shards,
        ),
        name="tail",
    )(core, *parts, *stats, embedded, w_out, own, other)


def mix_matrix(edge_proj, heads):
    channel_count, outs = edge_proj.shape
    factors = jnp.where(jnp.arange(outs) < heads, 0.5, 0.25).astype(jnp.bfloat16)
    scaled = (edge_proj * factors[None, :]).T
    eye = jnp.eye(8, dtype=jnp.bfloat16)
    mixed = scaled[:, None, None, :] * eye[None, :, :, None]
    offsets = jnp.sum(scaled.astype(jnp.float32), axis=1)
    return mixed.reshape(outs * 8, 8 * channel_count), offsets


def shift_low(value, by):
    return lax.ppermute(value, "qrow", [(i, (i & 12) | ((i + by) & 3)) for i in range(16)])


def shift_high(value, by):
    return lax.ppermute(value, "qrow", [(i, (i + 4 * by) & 15) for i in range(16)])


def shift_chip(value, by):
    return lax.ppermute(value, "kcol", [(i, (i + 2 * by) & 7) for i in range(8)])


def after(value, others):
    return lax.optimization_barrier((value, others))[0]


def swap_core(value):
    return lax.ppermute(value, "kcol", [(i, i ^ 1) for i in range(8)])


def local(
    features,
    node_ids,
    token_embed,
    w_query,
    w_key,
    w_value,
    w_out,
    slopes,
    chan_scale,
    chan_shift,
    edge_proj,
    edge_value,
    key_index,
    counts,
    w_up,
    w_down,
):
    node_dev, width = features.shape
    vocab_size = token_embed.shape[0]
    heads = slopes.shape[0]
    head_dim = width // heads
    rows = edge_value.shape[-1]
    row_at = lax.axis_index("qrow")
    col_at = lax.axis_index("kcol")
    core = col_at & 1

    span = w_up.shape[1]
    down_stack = jnp.concatenate(
        [w_down[:, cut : cut + span] for cut in range(0, width, span)], axis=0
    )
    own_weights = lax.all_gather(jnp.where(core == 0, w_up, down_stack), "qrow", axis=0)

    one_hot = (
        node_ids[:, None] == lax.broadcasted_iota(jnp.int32, (node_dev, vocab_size), 1)
    ).astype(jnp.bfloat16)
    embedded = features.astype(jnp.float32) + jnp.dot(
        one_hot, token_embed, preferred_element_type=jnp.float32
    )
    normed = layer_norm(embedded).astype(jnp.bfloat16)

    half = node_dev // 2
    first = [normed[:half], normed[half:]]
    axes = [(shift_low, shift_high), (shift_high, shift_low)]
    near = [[move[0](part, 1), move[0](part, -1)] for part, move in zip(first, axes)]
    row_near = [shift_chip(normed, 1)]

    lists = list_stage(
        counts, key_index[:, 0], jnp.stack([row_at >> 2, row_at & 3, col_at >> 1, core])
    )
    mix, offsets = mix_matrix(edge_proj, heads)
    spread = lambda vector: jnp.broadcast_to((0.5 * vector)[:, None], (vector.shape[0], rows))
    edges = edge_value.reshape(-1, rows, rows)
    scale, shift = spread(chan_scale), spread(chan_shift)

    def edge_part(start, stop, held, others):
        pinned = after(lists, others)
        return edge_stage(start, stop, pinned, offsets, edges, mix, scale, shift, heads, held)

    held = edge_part(0, CUTS[0], (), normed)
    far = [
        [move[0](pair[0][: half // 2], 1), move[0](pair[1][half // 2 :], -1)]
        for pair, move in zip(near, axes)
    ]
    held = edge_part(CUTS[0], CUTS[1], held, (near, row_near))
    row_near.append(shift_chip(after(normed, near), -1))
    lines = [
        jnp.concatenate([part, *pair, *ends], axis=0) for part, pair, ends in zip(first, near, far)
    ]
    near = [[move[1](line, 1), move[1](line, -1)] for line, move in zip(lines, axes)]
    held = edge_part(CUTS[1], CUTS[2], held, (far, row_near))
    row_near.append(shift_chip(after(normed, far), 2))
    cut = 2 * half
    far = [
        [move[1](pair[0][:cut], 1), move[1](pair[1][cut:], -1)] for pair, move in zip(near, axes)
    ]
    bias, gate = edge_part(CUTS[2], edges.shape[0], held, (near, row_near))
    row_own = jnp.concatenate([normed, *row_near], axis=0)
    row_other = swap_core(row_own)
    planes = [
        jnp.concatenate([line, *pair, *ends], axis=0).reshape(4, 4, half, width)
        for line, pair, ends in zip(lines, near, far)
    ]
    column_nodes = jnp.concatenate([planes[0], jnp.swapaxes(planes[1], 0, 1)], axis=2).reshape(
        16, node_dev, width
    )
    row_nodes = jnp.concatenate([row_own, row_other], axis=0).reshape(
        8, node_dev, width
    )
    queries = (
        jnp.einsum("kd,gnk->gdn", w_query, row_nodes, preferred_element_type=jnp.float32).astype(
            jnp.bfloat16
        )
        * jnp.bfloat16(head_dim ** (-0.5))
    )
    keys = jnp.einsum(
        "gnk,kd->gnd", column_nodes, w_key, preferred_element_type=jnp.float32
    ).astype(jnp.bfloat16)
    values = jnp.einsum(
        "kd,gnk->gdn", w_value, column_nodes, preferred_element_type=jnp.float32
    ).astype(jnp.bfloat16)
    part, stat = attend_stage(lists, slopes, offsets, edges, bias, gate, keys, values, queries)
    own_weights, part = lax.optimization_barrier((own_weights, part))
    other_weights = swap_core(own_weights)
    part, stat = merge_stage(part, swap_core(part[4:]), stat, swap_core(stat[4:]))
    parts, stats = [part], [stat]
    for at, step in ((1, -1), (2, 1), (3, 2)):
        parts.append(shift_chip(part[at : at + 1], step))
        stats.append(shift_chip(stat[at : at + 1], step))
    return tail_stage(
        core.reshape(1), parts, stats, embedded, w_out, own_weights, other_weights
    )


def solution(mesh):
    placed = (
        P(("qrow", "kcol"), None),
        P(("qrow", "kcol")),
        P(),
        P(),
        P(),
        P(),
        P(),
        P(),
        P(),
        P(),
        P(),
        P("qrow", "kcol", None, None, None),
        P("qrow", "kcol", None),
        P("qrow", "kcol"),
        P(None, "qrow"),
        P("qrow", None),
    )
    return jax.shard_map(
        local, mesh=mesh, in_specs=placed, out_specs=P(("qrow", "kcol"), None), check_vma=False
    )
```

```python
import functools

import jax
import jax.numpy as jnp
from jax import lax
from jax.experimental import pallas as pl
from jax.experimental.pallas import tpu as pltpu
from jax.sharding import PartitionSpec as P

NEG_FILL = -1e30
TOP_PIECES = 3
TOTAL_PIECES = 3
EDGE_VMEM = 56 * 1024 * 1024
ATTEND_VMEM = 56 * 1024 * 1024
TAIL_VMEM = 24 * 1024 * 1024


def layer_norm(values):
    average = jnp.mean(values, axis=-1, keepdims=True)
    centered = values - average
    spread = jnp.mean(centered * centered, axis=-1, keepdims=True)
    return centered * lax.rsqrt(spread + 1e-05)


def list_kernel(counts_ref, index_ref, place_ref, lists_ref):
    block_total, slot_count = index_ref.shape
    total = block_total * slot_count
    chip, core = place_ref[0], place_ref[1]

    def relative(theirs, ours):
        gap = (theirs - ours + 4) & 3
        return jnp.where(gap == 0, 0, jnp.where(gap == 3, 1, gap + 1))

    filled = jnp.int32(0)
    for block in range(block_total):
        count = counts_ref[block, 0]
        partner = jnp.where(core == block % 2, 0, 4) + relative(jnp.int32(block // 2), chip)
        visits = jnp.maximum(count, 1)
        for slot in range(slot_count):

            @pl.when(slot < visits)
            def _(at=filled, block=block, slot=slot, partner=partner, count=count, visits=visits):
                key_block = index_ref[block, slot]
                lists_ref[0, at] = jnp.int32(block * slot_count + slot)
                lists_ref[1, at] = at
                lists_ref[2, at] = jnp.int32(block)
                lists_ref[3, at] = key_block
                lists_ref[4, at] = (slot < count).astype(jnp.int32)
                lists_ref[5, at] = jnp.int32(slot == 0)
                lists_ref[6, at] = (visits == slot + 1).astype(jnp.int32)
                lists_ref[7, at] = partner

            filled = filled + (slot < visits).astype(jnp.int32)

    @pl.loop(0, total)
    def _(step):
        @pl.when(step >= filled)
        def _():
            for row in range(4):
                lists_ref[row, step] = lists_ref[row, filled - 1]
            for row in range(4, 7):
                lists_ref[row, step] = jnp.int32(0)
            lists_ref[7, step] = lists_ref[7, filled - 1]


def list_stage(counts, index, place):
    scalars = pl.BlockSpec(memory_space=pltpu.SMEM)
    return pl.pallas_call(
        list_kernel,
        in_specs=[scalars] * 3,
        out_specs=scalars,
        out_shape=jax.ShapeDtypeStruct((8, index.shape[0] * index.shape[1]), jnp.int32),
        name="lists",
    )(counts, index, place)


def edge_kernel(
    lists, offsets, edge_ref, mix_ref, scale_ref, shift_ref, bias_ref, gate_ref, edge_t, chans
):
    step = pl.program_id(0)
    heads = bias_ref.shape[1]
    rows, lanes = edge_t.shape
    channel_count = scale_ref.shape[0]

    @pl.when(lists[4, step] > 0)
    def _():
        edge_t[...] = edge_ref[0].astype(jnp.float32).T
        scale = scale_ref[...]
        shift = shift_ref[...]
        for part in range(rows // 16):
            slot = part % 2
            for half in range(2):
                for within in range(8):
                    row = part * 16 + half * 8 + within
                    line = jnp.broadcast_to(edge_t[row : row + 1, :], scale.shape)
                    pre = (line * scale + shift).astype(jnp.bfloat16)
                    chans[
                        slot,
                        within * channel_count : (within + 1) * channel_count,
                        half * lanes : (half + 1) * lanes,
                    ] = jnp.tanh(pre)
            terms = jnp.dot(mix_ref[...], chans[slot], preferred_element_type=jnp.float32)
            span = slice(part * 16, part * 16 + 16)
            for head in range(heads):
                block = terms[head * 8 : head * 8 + 8]
                both = jnp.concatenate([block[:, :lanes], block[:, lanes:]], axis=0)
                bias_ref[0, head, span, :] = both.astype(jnp.bfloat16)
                block = terms[(heads + head) * 8 : (heads + head) * 8 + 8]
                both = jnp.concatenate([block[:, :lanes], block[:, lanes:]], axis=0)
                gate_ref[0, head, span, :] = (
                    0.5 + 0.5 * jnp.tanh(both + offsets[heads + head])
                ).astype(jnp.bfloat16)


def edge_stage(lists, offsets, edges, mix, scale, shift, heads):
    tiles, rows, lanes = edges.shape
    out = pl.BlockSpec((1, heads, rows, lanes), lambda s, lists, *_: (lists[1, s], 0, 0, 0))
    grid_spec = pltpu.PrefetchScalarGridSpec(
        num_scalar_prefetch=2,
        grid=(tiles,),
        in_specs=[
            pl.BlockSpec((1, rows, lanes), lambda s, lists, *_: (lists[0, s], 0, 0)),
            pl.BlockSpec(mix.shape, lambda s, *_: (0, 0)),
            pl.BlockSpec(scale.shape, lambda s, *_: (0, 0)),
            pl.BlockSpec(shift.shape, lambda s, *_: (0, 0)),
        ],
        out_specs=[out, out],
        scratch_shapes=[
            pltpu.VMEM((rows, lanes), jnp.float32),
            pltpu.VMEM((2, mix.shape[1], 2 * lanes), jnp.bfloat16),
        ],
    )
    return pl.pallas_call(
        edge_kernel,
        grid_spec=grid_spec,
        out_shape=[jax.ShapeDtypeStruct((tiles, heads, rows, lanes), jnp.bfloat16)] * 2,
        compiler_params=pltpu.CompilerParams(vmem_limit_bytes=EDGE_VMEM),
        cost_estimate=pl.CostEstimate(
            flops=tiles * 2 * rows * lanes * 64 * 256 * 2,
            bytes_accessed=tiles * rows * lanes * heads * 4,
            transcendentals=tiles * rows * lanes * 80,
        ),
        name="edge_terms",
    )(lists, offsets, edges, mix, scale, shift)


def attend_kernel(
    lists,
    slopes,
    offsets,
    edge_ref,
    bias_ref,
    gate_ref,
    key_ref,
    value_ref,
    query_ref,
    num_ref,
    query_pairs,
    acc,
    tops,
    totals,
):
    step = pl.program_id(0)
    heads, rows, lanes = bias_ref.shape[1:]
    head_dim = acc.shape[0] // heads

    @pl.when(lists[5, step] > 0)
    def _():
        block = lists[7, step]
        acc[...] = jnp.zeros_like(acc)
        tops[...] = jnp.full_like(tops, NEG_FILL)
        totals[...] = jnp.zeros_like(totals)
        blank = jnp.zeros((head_dim, lanes), jnp.bfloat16)
        for pair in range(heads // 2):
            upper = query_ref[block, pair * 2 * head_dim : (pair * 2 + 1) * head_dim, :]
            lower = query_ref[block, (pair * 2 + 1) * head_dim : (pair * 2 + 2) * head_dim, :]
            query_pairs[pair, :head_dim, :lanes] = upper
            query_pairs[pair, :head_dim, lanes:] = blank
            query_pairs[pair, head_dim:, :lanes] = blank
            query_pairs[pair, head_dim:, lanes:] = lower

    @pl.when(lists[4, step] > 0)
    def _():
        key_block = lists[3, step]
        edge_t = edge_ref[0].astype(jnp.float32).T
        for pair in range(heads // 2):
            width = 2 * head_dim
            keys = key_ref[key_block, :, pair * width : (pair + 1) * width]
            both = jnp.dot(keys, query_pairs[pair], preferred_element_type=jnp.float32)
            for side in range(2):
                head = pair * 2 + side
                span = slice(head * head_dim, (head + 1) * head_dim)
                scores = both[:, side * lanes : (side + 1) * lanes] + (
                    bias_ref[0, head].astype(jnp.float32) + (edge_t * slopes[head] + offsets[head])
                )
                old_top = tops[head : head + 1, :]
                new_top = jnp.maximum(old_top, jnp.max(scores, axis=0, keepdims=True))
                factor = jnp.exp(old_top - new_top)
                weights = jnp.exp(scores - new_top)
                totals[head : head + 1, :] = totals[head : head + 1, :] * factor + jnp.sum(
                    weights, axis=0, keepdims=True
                )
                tops[head : head + 1, :] = new_top
                gated = (weights * gate_ref[0, head].astype(jnp.float32)).astype(jnp.bfloat16)
                part = jnp.dot(
                    value_ref[key_block, span, :], gated, preferred_element_type=jnp.float32
                )
                acc[span, :] = acc[span, :] * factor + part

    @pl.when(lists[6, step] > 0)
    def _():
        for head in range(heads):
            span = slice(head * head_dim, (head + 1) * head_dim)
            total = totals[head : head + 1, :]
            inverse = jnp.where(total > 0.0, 1.0 / jnp.where(total > 0.0, total, 1.0), 0.0)
            num_ref[0, span, :] = (acc[span, :] * inverse).astype(num_ref.dtype)
        at = acc.shape[0]
        rest = tops[...]
        for _ in range(TOP_PIECES):
            piece = rest.astype(num_ref.dtype)
            num_ref[0, at : at + heads, :] = piece
            rest = rest - piece.astype(jnp.float32)
            at += heads
        rest = totals[...]
        for _ in range(TOTAL_PIECES):
            piece = rest.astype(num_ref.dtype)
            num_ref[0, at : at + heads, :] = piece
            rest = rest - piece.astype(jnp.float32)
            at += heads


def attend_stage(lists, slopes, offsets, edges, bias, gate, keys, values, queries):
    block_total, width, lanes = queries.shape
    tiles, heads, rows, _ = bias.shape
    packed = width + heads * (TOP_PIECES + TOTAL_PIECES)
    whole = lambda array: pl.BlockSpec(
        array.shape, lambda s, *_: (0,) * array.ndim, pipeline_mode=pl.Buffered(1)
    )
    edge_block = pl.BlockSpec((1, heads, rows, lanes), lambda s, lists, *_: (lists[1, s], 0, 0, 0))
    grid_spec = pltpu.PrefetchScalarGridSpec(
        num_scalar_prefetch=3,
        grid=(tiles,),
        in_specs=[
            pl.BlockSpec((1, rows, lanes), lambda s, lists, *_: (lists[0, s], 0, 0)),
            edge_block,
            edge_block,
            whole(keys),
            whole(values),
            whole(queries),
        ],
        out_specs=pl.BlockSpec((1, packed, lanes), lambda s, lists, *_: (lists[2, s], 0, 0)),
        scratch_shapes=[
            pltpu.VMEM((heads // 2, 2 * width // heads, 2 * lanes), jnp.bfloat16),
            pltpu.VMEM((width, lanes), jnp.float32),
            pltpu.VMEM((heads, lanes), jnp.float32),
            pltpu.VMEM((heads, lanes), jnp.float32),
        ],
    )
    return pl.pallas_call(
        attend_kernel,
        grid_spec=grid_spec,
        out_shape=jax.ShapeDtypeStruct((block_total, packed, lanes), jnp.bfloat16),
        compiler_params=pltpu.CompilerParams(vmem_limit_bytes=ATTEND_VMEM),
        cost_estimate=pl.CostEstimate(
            flops=tiles * 16 * rows * lanes * width,
            bytes_accessed=tiles * rows * lanes * heads * 4,
            transcendentals=tiles * rows * lanes * heads,
        ),
        name="attend",
    )(lists, slopes, offsets, edges, bias, gate, keys, values, queries)


def join_kernel(parts_ref, embedded_ref, out_ref, residual, normed, attended):
    width = attended.shape[0]
    count = parts_ref.shape[0]
    heads = (parts_ref.shape[1] - width) // (TOP_PIECES + TOTAL_PIECES)
    head_dim = width // heads

    def rejoin(part, first, pieces):
        whole = jnp.zeros((heads, attended.shape[1]), jnp.float32)
        for piece in range(pieces):
            at = width + (first + piece) * heads
            whole = whole + parts_ref[part, at : at + heads, :].astype(jnp.float32)
        return whole

    tops = [rejoin(part, 0, TOP_PIECES) for part in range(count)]
    top = functools.reduce(jnp.maximum, tops)
    shares = [
        rejoin(part, TOP_PIECES, TOTAL_PIECES) * jnp.exp(tops[part] - top)
        for part in range(count)
    ]
    inverse = 1.0 / functools.reduce(jnp.add, shares)
    shares = [share * inverse for share in shares]
    for head in range(heads):
        span = slice(head * head_dim, (head + 1) * head_dim)
        merged = jnp.zeros((head_dim, attended.shape[1]), jnp.float32)
        for part in range(count):
            merged = merged + parts_ref[part, span, :].astype(jnp.float32) * (
                shares[part][head : head + 1]
            )
        attended[span, :] = merged
    rows = attended[...].T.astype(jnp.bfloat16)
    values = embedded_ref[...] + jnp.dot(
        rows, out_ref[...], preferred_element_type=jnp.float32
    )
    residual[...] = values
    normed[...] = layer_norm(values).astype(jnp.bfloat16)


def join_stage(parts, embedded, w_out):
    rows, width = embedded.shape
    return pl.pallas_call(
        join_kernel,
        out_shape=[
            jax.ShapeDtypeStruct((rows, width), jnp.float32),
            jax.ShapeDtypeStruct((rows, width), jnp.bfloat16),
        ],
        scratch_shapes=[pltpu.VMEM((width, parts.shape[2]), jnp.float32)],
        compiler_params=pltpu.CompilerParams(vmem_limit_bytes=TAIL_VMEM),
        name="join",
    )(parts, embedded, w_out)


def feed_kernel(own_ref, other_ref, weight_ref, own_sum, other_sum, normed, acc):
    step = pl.program_id(0)
    rows, width = own_ref.shape
    shards, depth, span = weight_ref.shape
    tall = depth // 2
    units = span // 2

    @pl.when(step == 0)
    def _():
        normed[:rows, :] = own_ref[...]
        normed[rows:, :] = other_ref[...]
        acc[...] = jnp.zeros_like(acc)

    pre = jnp.zeros((2 * rows, shards * units), jnp.float32)
    for piece in range(width // tall):
        up = jnp.concatenate(
            [
                weight_ref[shard, :tall, piece * units : (piece + 1) * units]
                for shard in range(shards)
            ],
            axis=1,
        )
        pre = pre + jnp.dot(
            normed[:, piece * tall : (piece + 1) * tall], up, preferred_element_type=jnp.float32
        )
    hidden = (0.5 * pre * (1.0 + lax.erf(pre * (0.5**0.5)))).astype(jnp.bfloat16)
    for piece in range(width // span):
        down = jnp.concatenate(
            [
                weight_ref[shard, tall + piece * units : tall + (piece + 1) * units, :]
                for shard in range(shards)
            ],
            axis=0,
        )
        acc[:, piece * span : (piece + 1) * span] += jnp.dot(
            hidden, down, preferred_element_type=jnp.float32
        )

    @pl.when(step == pl.num_programs(0) - 1)
    def _():
        own_sum[...] = acc[:rows, :]
        other_sum[...] = acc[rows:, :]


def feed_stage(own, other, weights):
    shards, depth, span = weights.shape
    rows, width = own.shape
    group = 2
    flat = pl.BlockSpec((rows, width), lambda s: (0, 0))
    return pl.pallas_call(
        feed_kernel,
        grid=(shards // group,),
        in_specs=[flat, flat, pl.BlockSpec((group, depth, span), lambda s: (s, 0, 0))],
        out_specs=[flat, flat],
        out_shape=[jax.ShapeDtypeStruct((rows, width), jnp.float32)] * 2,
        scratch_shapes=[
            pltpu.VMEM((2 * rows, width), jnp.bfloat16),
            pltpu.VMEM((2 * rows, width), jnp.float32),
        ],
        compiler_params=pltpu.CompilerParams(vmem_limit_bytes=TAIL_VMEM),
        name="feed",
    )(own, other, weights)


def half_weights(w_up, w_down, core):
    width, span = w_up.shape
    units = span // 2
    up = lax.dynamic_slice_in_dim(w_up, core * units, units, 1)
    down = lax.dynamic_slice_in_dim(w_down, core * units, units, 0)
    tall = width // 2
    top = jnp.concatenate([up[:tall], up[tall:]], axis=1)
    return jnp.concatenate(
        [top] + [down[:, cut : cut + span] for cut in range(0, width, span)], axis=0
    )


def mix_matrix(edge_proj, heads):
    channel_count, outs = edge_proj.shape
    factors = jnp.where(jnp.arange(outs) < heads, 0.5, 0.25).astype(jnp.bfloat16)
    scaled = (edge_proj * factors[None, :]).T
    eye = jnp.eye(8, dtype=jnp.bfloat16)
    mixed = scaled[:, None, None, :] * eye[None, :, :, None]
    offsets = jnp.sum(scaled.astype(jnp.float32), axis=1)
    return mixed.reshape(outs * 8, 8 * channel_count), offsets


def shift_chip(value, by):
    return lax.ppermute(value, "kcol", [(i, (i + 2 * by) & 7) for i in range(8)])


def after(value, others):
    return lax.optimization_barrier((value, others))[0]


def swap_core(value):
    return lax.ppermute(value, "kcol", [(i, i ^ 1) for i in range(8)])


def local(
    features,
    node_ids,
    token_embed,
    w_query,
    w_key,
    w_value,
    w_out,
    slopes,
    chan_scale,
    chan_shift,
    edge_proj,
    edge_value,
    key_index,
    counts,
    w_up,
    w_down,
):
    node_dev, width = features.shape
    vocab_size = token_embed.shape[0]
    heads = slopes.shape[0]
    head_dim = width // heads
    rows = edge_value.shape[-1]
    col_at = lax.axis_index("kcol")
    core = col_at & 1
    one_hot = (
        node_ids[:, None] == lax.broadcasted_iota(jnp.int32, (node_dev, vocab_size), 1)
    ).astype(jnp.bfloat16)
    embedded = features.astype(jnp.float32) + jnp.dot(
        one_hot, token_embed, preferred_element_type=jnp.float32
    )
    normed = layer_norm(embedded).astype(jnp.bfloat16)

    column_nodes = lax.all_gather(normed, "qrow", axis=0)
    row_own = jnp.stack([normed] + [shift_chip(normed, by) for by in (1, -1, 2)])
    row_other = swap_core(row_own)

    weights = half_weights(w_up, w_down, core)

    lists = list_stage(counts, key_index[:, 0], jnp.stack([col_at >> 1, core]))
    mix, offsets = mix_matrix(edge_proj, heads)
    spread = lambda vector: jnp.broadcast_to((0.5 * vector)[:, None], (vector.shape[0], rows))
    edges = edge_value.reshape(-1, rows, rows)
    bias, gate = edge_stage(
        after(lists, row_other), offsets, edges, mix, spread(chan_scale), spread(chan_shift), heads
    )
    row_nodes = jnp.concatenate([row_own, row_other], axis=0)
    column_nodes, weights, bias = lax.optimization_barrier((column_nodes, weights, bias))
    weights = lax.all_gather(weights, "qrow", axis=0)
    queries = (
        jnp.einsum("kd,gnk->gdn", w_query, row_nodes, preferred_element_type=jnp.float32).astype(
            jnp.bfloat16
        )
        * jnp.bfloat16(head_dim ** (-0.5))
    )
    keys = jnp.einsum(
        "gnk,kd->gnd", column_nodes, w_key, preferred_element_type=jnp.float32
    ).astype(jnp.bfloat16)
    values = jnp.einsum(
        "kd,gnk->gdn", w_value, column_nodes, preferred_element_type=jnp.float32
    ).astype(jnp.bfloat16)
    parts = attend_stage(lists, slopes, offsets, edges, bias, gate, keys, values, queries)
    parts = lax.all_to_all(parts, "kcol", 0, 0, tiled=True)
    residual, normed_two = join_stage(parts, embedded, w_out)
    weights, normed_two = lax.optimization_barrier((weights, normed_two))
    own_sum, other_sum = feed_stage(normed_two, swap_core(normed_two), weights)
    return (residual + (own_sum + swap_core(other_sum))).astype(jnp.bfloat16)


def solution(mesh):
    placed = (
        P(("qrow", "kcol"), None),
        P(("qrow", "kcol")),
        P(),
        P(),
        P(),
        P(),
        P(),
        P(),
        P(),
        P(),
        P(),
        P("qrow", "kcol", None, None, None),
        P("qrow", "kcol", None),
        P("qrow", "kcol"),
        P(None, "qrow"),
        P("qrow", None),
    )
    return jax.shard_map(
        local, mesh=mesh, in_specs=placed, out_specs=P(("qrow", "kcol"), None), check_vma=False
    )
```

```python
import functools

import jax
import jax.numpy as jnp
from jax import lax
from jax.experimental import pallas as pl
from jax.experimental.pallas import tpu as pltpu
from jax.sharding import PartitionSpec as P

NEG_FILL = -1e30
TOP_PIECES = 3
TOTAL_PIECES = 3
EDGE_VMEM = 56 * 1024 * 1024
ATTEND_VMEM = 56 * 1024 * 1024
TAIL_VMEM = 24 * 1024 * 1024


def layer_norm(values):
    average = jnp.mean(values, axis=-1, keepdims=True)
    centered = values - average
    spread = jnp.mean(centered * centered, axis=-1, keepdims=True)
    return centered * lax.rsqrt(spread + 1e-05)


def list_kernel(counts_ref, index_ref, place_ref, lists_ref):
    block_total, slot_count = index_ref.shape
    total = block_total * slot_count
    chip, core = place_ref[0], place_ref[1]

    def relative(theirs, ours):
        gap = (theirs - ours + 4) & 3
        return jnp.where(gap == 0, 0, jnp.where(gap == 3, 1, gap + 1))

    filled = jnp.int32(0)
    for block in range(block_total):
        count = counts_ref[block, 0]
        partner = jnp.where(core == block % 2, 0, 4) + relative(jnp.int32(block // 2), chip)
        visits = jnp.maximum(count, 1)
        for slot in range(slot_count):

            @pl.when(slot < visits)
            def _(at=filled, block=block, slot=slot, partner=partner, count=count, visits=visits):
                key_block = index_ref[block, slot]
                lists_ref[0, at] = jnp.int32(block * slot_count + slot)
                lists_ref[1, at] = at
                lists_ref[2, at] = jnp.int32(block)
                lists_ref[3, at] = key_block
                lists_ref[4, at] = (slot < count).astype(jnp.int32)
                lists_ref[5, at] = jnp.int32(slot == 0)
                lists_ref[6, at] = (visits == slot + 1).astype(jnp.int32)
                lists_ref[7, at] = partner

            filled = filled + (slot < visits).astype(jnp.int32)

    @pl.loop(0, total)
    def _(step):
        @pl.when(step >= filled)
        def _():
            for row in range(4):
                lists_ref[row, step] = lists_ref[row, filled - 1]
            for row in range(4, 7):
                lists_ref[row, step] = jnp.int32(0)
            lists_ref[7, step] = lists_ref[7, filled - 1]


def list_stage(counts, index, place):
    scalars = pl.BlockSpec(memory_space=pltpu.SMEM)
    return pl.pallas_call(
        list_kernel,
        in_specs=[scalars] * 3,
        out_specs=scalars,
        out_shape=jax.ShapeDtypeStruct((8, index.shape[0] * index.shape[1]), jnp.int32),
        name="lists",
    )(counts, index, place)


def edge_kernel(
    lists, offsets, edge_ref, mix_ref, scale_ref, shift_ref, bias_ref, gate_ref, edge_t
):
    step = pl.program_id(0)
    heads = bias_ref.shape[1]
    rows, lanes = edge_t.shape

    @pl.when(lists[4, step] > 0)
    def _():
        edge_t[...] = edge_ref[0].astype(jnp.float32).T
        scale = scale_ref[...]
        shift = shift_ref[...]

        def channels(row):
            line = jnp.broadcast_to(edge_t[row : row + 1, :], scale.shape)
            return jnp.tanh((line * scale + shift).astype(jnp.bfloat16))

        def build(part):
            return jnp.concatenate(
                [
                    jnp.concatenate(
                        [channels(part * 16 + half * 8 + within) for within in range(8)], axis=0
                    )
                    for half in range(2)
                ],
                axis=1,
            )

        for part in range(rows // 16):
            terms = jnp.dot(mix_ref[...], build(part), preferred_element_type=jnp.float32)
            span = slice(part * 16, part * 16 + 16)
            for head in range(heads):
                block = terms[head * 8 : head * 8 + 8]
                both = jnp.concatenate([block[:, :lanes], block[:, lanes:]], axis=0)
                bias_ref[0, head, span, :] = both.astype(jnp.bfloat16)
                block = terms[(heads + head) * 8 : (heads + head) * 8 + 8]
                both = jnp.concatenate([block[:, :lanes], block[:, lanes:]], axis=0)
                gate_ref[0, head, span, :] = (
                    0.5 + 0.5 * jnp.tanh(both + offsets[heads + head])
                ).astype(jnp.bfloat16)


def edge_stage(lists, offsets, edges, mix, scale, shift, heads):
    tiles, rows, lanes = edges.shape
    out = pl.BlockSpec((1, heads, rows, lanes), lambda s, lists, *_: (lists[1, s], 0, 0, 0))
    grid_spec = pltpu.PrefetchScalarGridSpec(
        num_scalar_prefetch=2,
        grid=(tiles,),
        in_specs=[
            pl.BlockSpec((1, rows, lanes), lambda s, lists, *_: (lists[0, s], 0, 0)),
            pl.BlockSpec(mix.shape, lambda s, *_: (0, 0)),
            pl.BlockSpec(scale.shape, lambda s, *_: (0, 0)),
            pl.BlockSpec(shift.shape, lambda s, *_: (0, 0)),
        ],
        out_specs=[out, out],
        scratch_shapes=[
            pltpu.VMEM((rows, lanes), jnp.float32),
        ],
    )
    return pl.pallas_call(
        edge_kernel,
        grid_spec=grid_spec,
        out_shape=[jax.ShapeDtypeStruct((tiles, heads, rows, lanes), jnp.bfloat16)] * 2,
        compiler_params=pltpu.CompilerParams(vmem_limit_bytes=EDGE_VMEM),
        cost_estimate=pl.CostEstimate(
            flops=tiles * 2 * rows * lanes * 64 * 256 * 2,
            bytes_accessed=tiles * rows * lanes * heads * 4,
            transcendentals=tiles * rows * lanes * 80,
        ),
        name="edge_terms",
    )(lists, offsets, edges, mix, scale, shift)


def attend_kernel(
    lists,
    slopes,
    offsets,
    edge_ref,
    bias_ref,
    gate_ref,
    key_ref,
    value_ref,
    *rest,
):
    *query_refs, num_ref, query_pairs, acc, tops, totals = rest
    step = pl.program_id(0)
    heads, rows, lanes = bias_ref.shape[1:]
    head_dim = acc.shape[0] // heads

    @pl.when(lists[5, step] > 0)
    def _():
        acc[...] = jnp.zeros_like(acc)
        tops[...] = jnp.full_like(tops, NEG_FILL)
        totals[...] = jnp.zeros_like(totals)
        blank = jnp.zeros((head_dim, lanes), jnp.bfloat16)
        for pair in range(heads // 2):
            query_pairs[pair, :head_dim, lanes:] = blank
            query_pairs[pair, head_dim:, :lanes] = blank
        for place, query_ref in enumerate(query_refs):

            @pl.when(lists[7, step] == place)
            def _(query_ref=query_ref):
                for pair in range(heads // 2):
                    at = pair * 2 * head_dim
                    query_pairs[pair, :head_dim, :lanes] = query_ref[at : at + head_dim, :]
                    at += head_dim
                    query_pairs[pair, head_dim:, lanes:] = query_ref[at : at + head_dim, :]

    @pl.when(lists[4, step] > 0)
    def _():
        key_block = lists[3, step]
        edge_t = edge_ref[0].astype(jnp.float32).T
        for pair in range(heads // 2):
            width = 2 * head_dim
            keys = key_ref[key_block, :, pair * width : (pair + 1) * width]
            both = jnp.dot(keys, query_pairs[pair], preferred_element_type=jnp.float32)
            for side in range(2):
                head = pair * 2 + side
                span = slice(head * head_dim, (head + 1) * head_dim)
                scores = both[:, side * lanes : (side + 1) * lanes] + (
                    bias_ref[0, head].astype(jnp.float32) + (edge_t * slopes[head] + offsets[head])
                )
                old_top = tops[head : head + 1, :]
                new_top = jnp.maximum(old_top, jnp.max(scores, axis=0, keepdims=True))
                factor = jnp.exp(old_top - new_top)
                weights = jnp.exp(scores - new_top)
                totals[head : head + 1, :] = totals[head : head + 1, :] * factor + jnp.sum(
                    weights, axis=0, keepdims=True
                )
                tops[head : head + 1, :] = new_top
                gated = (weights * gate_ref[0, head].astype(jnp.float32)).astype(jnp.bfloat16)
                part = jnp.dot(
                    value_ref[key_block, span, :], gated, preferred_element_type=jnp.float32
                )
                acc[span, :] = acc[span, :] * factor + part

    @pl.when(lists[6, step] > 0)
    def _():
        for head in range(heads):
            span = slice(head * head_dim, (head + 1) * head_dim)
            total = totals[head : head + 1, :]
            inverse = jnp.where(total > 0.0, 1.0 / jnp.where(total > 0.0, total, 1.0), 0.0)
            num_ref[0, span, :] = (acc[span, :] * inverse).astype(num_ref.dtype)
        at = acc.shape[0]
        rest = tops[...]
        for _ in range(TOP_PIECES):
            piece = rest.astype(num_ref.dtype)
            num_ref[0, at : at + heads, :] = piece
            rest = rest - piece.astype(jnp.float32)
            at += heads
        rest = totals[...]
        for _ in range(TOTAL_PIECES):
            piece = rest.astype(num_ref.dtype)
            num_ref[0, at : at + heads, :] = piece
            rest = rest - piece.astype(jnp.float32)
            at += heads


def attend_stage(lists, slopes, offsets, edges, bias, gate, keys, values, queries):
    block_total = len(queries)
    width, lanes = queries[0].shape
    tiles, heads, rows, _ = bias.shape
    packed = width + heads * (TOP_PIECES + TOTAL_PIECES)
    whole = lambda array: pl.BlockSpec(
        array.shape, lambda s, *_: (0,) * array.ndim, pipeline_mode=pl.Buffered(1)
    )
    edge_block = pl.BlockSpec((1, heads, rows, lanes), lambda s, lists, *_: (lists[1, s], 0, 0, 0))
    grid_spec = pltpu.PrefetchScalarGridSpec(
        num_scalar_prefetch=3,
        grid=(tiles,),
        in_specs=[
            pl.BlockSpec((1, rows, lanes), lambda s, lists, *_: (lists[0, s], 0, 0)),
            edge_block,
            edge_block,
            whole(keys),
            whole(values),
        ]
        + [whole(query) for query in queries],
        out_specs=pl.BlockSpec((1, packed, lanes), lambda s, lists, *_: (lists[2, s], 0, 0)),
        scratch_shapes=[
            pltpu.VMEM((heads // 2, 2 * width // heads, 2 * lanes), jnp.bfloat16),
            pltpu.VMEM((width, lanes), jnp.float32),
            pltpu.VMEM((heads, lanes), jnp.float32),
            pltpu.VMEM((heads, lanes), jnp.float32),
        ],
    )
    return pl.pallas_call(
        attend_kernel,
        grid_spec=grid_spec,
        out_shape=jax.ShapeDtypeStruct((block_total, packed, lanes), jnp.bfloat16),
        compiler_params=pltpu.CompilerParams(vmem_limit_bytes=ATTEND_VMEM),
        cost_estimate=pl.CostEstimate(
            flops=tiles * 16 * rows * lanes * width,
            bytes_accessed=tiles * rows * lanes * heads * 4,
            transcendentals=tiles * rows * lanes * heads,
        ),
        name="attend",
    )(lists, slopes, offsets, edges, bias, gate, keys, values, *queries)


def join_kernel(parts_ref, embedded_ref, out_ref, residual, normed, attended):
    width = attended.shape[0]
    count = parts_ref.shape[0]
    heads = (parts_ref.shape[1] - width) // (TOP_PIECES + TOTAL_PIECES)
    head_dim = width // heads

    def rejoin(part, first, pieces):
        whole = jnp.zeros((heads, attended.shape[1]), jnp.float32)
        for piece in range(pieces):
            at = width + (first + piece) * heads
            whole = whole + parts_ref[part, at : at + heads, :].astype(jnp.float32)
        return whole

    tops = [rejoin(part, 0, TOP_PIECES) for part in range(count)]
    top = functools.reduce(jnp.maximum, tops)
    shares = [
        rejoin(part, TOP_PIECES, TOTAL_PIECES) * jnp.exp(tops[part] - top)
        for part in range(count)
    ]
    inverse = 1.0 / functools.reduce(jnp.add, shares)
    shares = [share * inverse for share in shares]
    for head in range(heads):
        span = slice(head * head_dim, (head + 1) * head_dim)
        merged = jnp.zeros((head_dim, attended.shape[1]), jnp.float32)
        for part in range(count):
            merged = merged + parts_ref[part, span, :].astype(jnp.float32) * (
                shares[part][head : head + 1]
            )
        attended[span, :] = merged
    rows = attended[...].T.astype(jnp.bfloat16)
    values = embedded_ref[...] + jnp.dot(
        rows, out_ref[...], preferred_element_type=jnp.float32
    )
    residual[...] = values
    normed[...] = layer_norm(values).astype(jnp.bfloat16)


def join_stage(parts, embedded, w_out):
    rows, width = embedded.shape
    return pl.pallas_call(
        join_kernel,
        out_shape=[
            jax.ShapeDtypeStruct((rows, width), jnp.float32),
            jax.ShapeDtypeStruct((rows, width), jnp.bfloat16),
        ],
        scratch_shapes=[pltpu.VMEM((width, parts.shape[2]), jnp.float32)],
        compiler_params=pltpu.CompilerParams(vmem_limit_bytes=TAIL_VMEM),
        name="join",
    )(parts, embedded, w_out)


def feed_kernel(own_ref, other_ref, weight_ref, own_sum, other_sum, normed, acc):
    step = pl.program_id(0)
    rows, width = own_ref.shape
    shards, depth, span = weight_ref.shape
    tall = depth // 2
    units = span // 2

    @pl.when(step == 0)
    def _():
        normed[:rows, :] = own_ref[...]
        normed[rows:, :] = other_ref[...]
        acc[...] = jnp.zeros_like(acc)

    pre = jnp.zeros((2 * rows, shards * units), jnp.float32)
    for piece in range(width // tall):
        up = jnp.concatenate(
            [
                weight_ref[shard, :tall, piece * units : (piece + 1) * units]
                for shard in range(shards)
            ],
            axis=1,
        )
        pre = pre + jnp.dot(
            normed[:, piece * tall : (piece + 1) * tall], up, preferred_element_type=jnp.float32
        )
    hidden = (0.5 * pre * (1.0 + lax.erf(pre * (0.5**0.5)))).astype(jnp.bfloat16)
    for piece in range(width // span):
        down = jnp.concatenate(
            [
                weight_ref[shard, tall + piece * units : tall + (piece + 1) * units, :]
                for shard in range(shards)
            ],
            axis=0,
        )
        acc[:, piece * span : (piece + 1) * span] += jnp.dot(
            hidden, down, preferred_element_type=jnp.float32
        )

    @pl.when(step == pl.num_programs(0) - 1)
    def _():
        own_sum[...] = acc[:rows, :]
        other_sum[...] = acc[rows:, :]


def feed_stage(own, other, weights):
    shards, depth, span = weights.shape
    rows, width = own.shape
    group = 2
    flat = pl.BlockSpec((rows, width), lambda s: (0, 0))
    return pl.pallas_call(
        feed_kernel,
        grid=(shards // group,),
        in_specs=[flat, flat, pl.BlockSpec((group, depth, span), lambda s: (s, 0, 0))],
        out_specs=[flat, flat],
        out_shape=[jax.ShapeDtypeStruct((rows, width), jnp.float32)] * 2,
        scratch_shapes=[
            pltpu.VMEM((2 * rows, width), jnp.bfloat16),
            pltpu.VMEM((2 * rows, width), jnp.float32),
        ],
        compiler_params=pltpu.CompilerParams(vmem_limit_bytes=TAIL_VMEM),
        name="feed",
    )(own, other, weights)


def half_kernel(core, up_ref, down_ref, out_ref):
    tall = up_ref.shape[0] // 2
    units, width = down_ref.shape
    span = 2 * units
    out_ref[:tall, :units] = up_ref[:tall, :]
    out_ref[:tall, units:] = up_ref[tall:, :]
    for piece in range(width // span):
        out_ref[tall + piece * units : tall + (piece + 1) * units, :] = down_ref[
            :, piece * span : (piece + 1) * span
        ]


def half_weights(w_up, w_down, core):
    width, span = w_up.shape
    units = span // 2
    grid_spec = pltpu.PrefetchScalarGridSpec(
        num_scalar_prefetch=1,
        grid=(1,),
        in_specs=[
            pl.BlockSpec((width, units), lambda s, core: (0, core[0])),
            pl.BlockSpec((units, width), lambda s, core: (core[0], 0)),
        ],
        out_specs=pl.BlockSpec((width, span), lambda s, core: (0, 0)),
    )
    return pl.pallas_call(
        half_kernel,
        grid_spec=grid_spec,
        out_shape=jax.ShapeDtypeStruct((width, span), w_up.dtype),
        name="half_weights",
    )(core.reshape(1), w_up, w_down)


def mix_matrix(edge_proj, heads):
    channel_count, outs = edge_proj.shape
    factors = jnp.where(jnp.arange(outs) < heads, 0.5, 0.25).astype(jnp.bfloat16)
    scaled = (edge_proj * factors[None, :]).T
    eye = jnp.eye(8, dtype=jnp.bfloat16)
    mixed = scaled[:, None, None, :] * eye[None, :, :, None]
    offsets = jnp.sum(scaled.astype(jnp.float32), axis=1)
    return mixed.reshape(outs * 8, 8 * channel_count), offsets


def shift_chip(value, by):
    return lax.ppermute(value, "kcol", [(i, (i + 2 * by) & 7) for i in range(8)])


def after(value, others):
    return lax.optimization_barrier((value, others))[0]


def swap_core(value):
    return lax.ppermute(value, "kcol", [(i, i ^ 1) for i in range(8)])


def local(
    features,
    node_ids,
    token_embed,
    w_query,
    w_key,
    w_value,
    w_out,
    slopes,
    chan_scale,
    chan_shift,
    edge_proj,
    edge_value,
    key_index,
    counts,
    w_up,
    w_down,
):
    node_dev, width = features.shape
    vocab_size = token_embed.shape[0]
    heads = slopes.shape[0]
    head_dim = width // heads
    rows = edge_value.shape[-1]
    col_at = lax.axis_index("kcol")
    core = col_at & 1
    one_hot = (
        node_ids[:, None] == lax.broadcasted_iota(jnp.int32, (node_dev, vocab_size), 1)
    ).astype(jnp.bfloat16)
    embedded = features.astype(jnp.float32) + jnp.dot(
        one_hot, token_embed, preferred_element_type=jnp.float32
    )
    normed = layer_norm(embedded).astype(jnp.bfloat16)

    column_nodes = lax.all_gather(normed, "qrow", axis=0)
    query_own = (
        jnp.einsum("kd,nk->dn", w_query, normed, preferred_element_type=jnp.float32).astype(
            jnp.bfloat16
        )
        * jnp.bfloat16(head_dim ** (-0.5))
    )
    weights = half_weights(w_up, w_down, core)
    queries = [query_own] + [shift_chip(query_own, by) for by in (1, -1, 2)]
    weights = lax.all_gather(after(weights, query_own), "qrow", axis=0)
    queries = queries + [swap_core(query) for query in queries]

    lists = list_stage(counts, key_index[:, 0], jnp.stack([col_at >> 1, core]))
    mix, offsets = mix_matrix(edge_proj, heads)
    spread = lambda vector: jnp.broadcast_to((0.5 * vector)[:, None], (vector.shape[0], rows))
    edges = edge_value.reshape(-1, rows, rows)
    bias, gate = edge_stage(
        after(lists, queries), offsets, edges, mix, spread(chan_scale), spread(chan_shift), heads
    )
    column_nodes, bias = lax.optimization_barrier((column_nodes, bias))
    keys = jnp.einsum(
        "gnk,kd->gnd", column_nodes, w_key, preferred_element_type=jnp.float32
    ).astype(jnp.bfloat16)
    values = jnp.einsum(
        "kd,gnk->gdn", w_value, column_nodes, preferred_element_type=jnp.float32
    ).astype(jnp.bfloat16)
    parts = attend_stage(lists, slopes, offsets, edges, bias, gate, keys, values, queries)
    parts = lax.all_to_all(parts, "kcol", 0, 0, tiled=True)
    residual, normed_two = join_stage(parts, embedded, w_out)
    weights, normed_two = lax.optimization_barrier((weights, normed_two))
    own_sum, other_sum = feed_stage(normed_two, swap_core(normed_two), weights)
    return (residual + (own_sum + swap_core(other_sum))).astype(jnp.bfloat16)


def solution(mesh):
    placed = (
        P(("qrow", "kcol"), None),
        P(("qrow", "kcol")),
        P(),
        P(),
        P(),
        P(),
        P(),
        P(),
        P(),
        P(),
        P(),
        P("qrow", "kcol", None, None, None),
        P("qrow", "kcol", None),
        P("qrow", "kcol"),
        P(None, "qrow"),
        P("qrow", None),
    )
    return jax.shard_map(
        local, mesh=mesh, in_specs=placed, out_specs=P(("qrow", "kcol"), None), check_vma=False
    )
```

```python
import functools

import jax
import jax.numpy as jnp
from jax import lax
from jax.experimental import pallas as pl
from jax.experimental.pallas import tpu as pltpu
from jax.sharding import PartitionSpec as P

NEG_FILL = -1e30
TOP_PIECES = 3
TOTAL_PIECES = 3
EDGE_VMEM = 56 * 1024 * 1024
ATTEND_VMEM = 20 * 1024 * 1024
JOIN_VMEM = 24 * 1024 * 1024
FEED_VMEM = 56 * 1024 * 1024


def layer_norm(values):
    average = jnp.mean(values, axis=-1, keepdims=True)
    centered = values - average
    spread = jnp.mean(centered * centered, axis=-1, keepdims=True)
    return centered * lax.rsqrt(spread + 1e-05)


def list_kernel(counts_ref, index_ref, place_ref, lists_ref):
    block_total, slot_count = index_ref.shape
    total = block_total * slot_count
    chip, core = place_ref[0], place_ref[1]

    def relative(theirs, ours):
        gap = (theirs - ours + 4) & 3
        return jnp.where(gap == 0, 0, jnp.where(gap == 3, 1, gap + 1))

    filled = jnp.int32(0)
    for block in range(block_total):
        count = counts_ref[block, 0]
        partner = jnp.where(core == block % 2, 0, 4) + relative(jnp.int32(block // 2), chip)
        visits = jnp.maximum(count, 1)
        for slot in range(slot_count):

            @pl.when(slot < visits)
            def _(at=filled, block=block, slot=slot, partner=partner, count=count, visits=visits):
                key_block = index_ref[block, slot]
                lists_ref[0, at] = jnp.int32(block * slot_count + slot)
                lists_ref[1, at] = at
                lists_ref[2, at] = jnp.int32(block)
                lists_ref[3, at] = key_block
                lists_ref[4, at] = (slot < count).astype(jnp.int32)
                lists_ref[5, at] = jnp.int32(slot == 0)
                lists_ref[6, at] = (visits == slot + 1).astype(jnp.int32)
                lists_ref[7, at] = partner

            filled = filled + (slot < visits).astype(jnp.int32)

    @pl.loop(0, total)
    def _(step):
        @pl.when(step >= filled)
        def _():
            for row in range(4):
                lists_ref[row, step] = lists_ref[row, filled - 1]
            for row in range(4, 7):
                lists_ref[row, step] = jnp.int32(0)
            lists_ref[7, step] = lists_ref[7, filled - 1]


def list_stage(counts, index, place):
    scalars = pl.BlockSpec(memory_space=pltpu.SMEM)
    return pl.pallas_call(
        list_kernel,
        in_specs=[scalars] * 3,
        out_specs=scalars,
        out_shape=jax.ShapeDtypeStruct((8, index.shape[0] * index.shape[1]), jnp.int32),
        name="lists",
    )(counts, index, place)


def edge_kernel(
    lists, offsets, edge_ref, mix_ref, scale_ref, shift_ref, bias_ref, gate_ref, edge_t
):
    step = pl.program_id(0)
    heads = bias_ref.shape[1]
    rows, lanes = edge_t.shape

    @pl.when(lists[4, step] > 0)
    def _():
        edge_t[...] = edge_ref[0].astype(jnp.float32).T
        scale = scale_ref[...]
        shift = shift_ref[...]

        def channels(row):
            line = jnp.broadcast_to(edge_t[row : row + 1, :], scale.shape)
            return jnp.tanh((line * scale + shift).astype(jnp.bfloat16))

        def build(part):
            return jnp.concatenate(
                [
                    jnp.concatenate(
                        [channels(part * 16 + half * 8 + within) for within in range(8)], axis=0
                    )
                    for half in range(2)
                ],
                axis=1,
            )

        for part in range(rows // 16):
            terms = jnp.dot(mix_ref[...], build(part), preferred_element_type=jnp.float32)
            span = slice(part * 16, part * 16 + 16)
            for head in range(heads):
                block = terms[head * 8 : head * 8 + 8]
                both = jnp.concatenate([block[:, :lanes], block[:, lanes:]], axis=0)
                bias_ref[0, head, span, :] = both.astype(jnp.bfloat16)
                block = terms[(heads + head) * 8 : (heads + head) * 8 + 8]
                both = jnp.concatenate([block[:, :lanes], block[:, lanes:]], axis=0)
                gate_ref[0, head, span, :] = (
                    0.5 + 0.5 * jnp.tanh(both + offsets[heads + head])
                ).astype(jnp.bfloat16)


def edge_stage(lists, offsets, edges, mix, scale, shift, heads):
    tiles, rows, lanes = edges.shape
    out = pl.BlockSpec((1, heads, rows, lanes), lambda s, lists, *_: (lists[1, s], 0, 0, 0))
    grid_spec = pltpu.PrefetchScalarGridSpec(
        num_scalar_prefetch=2,
        grid=(tiles,),
        in_specs=[
            pl.BlockSpec((1, rows, lanes), lambda s, lists, *_: (lists[0, s], 0, 0)),
            pl.BlockSpec(mix.shape, lambda s, *_: (0, 0)),
            pl.BlockSpec(scale.shape, lambda s, *_: (0, 0)),
            pl.BlockSpec(shift.shape, lambda s, *_: (0, 0)),
        ],
        out_specs=[out, out],
        scratch_shapes=[
            pltpu.VMEM((rows, lanes), jnp.float32),
        ],
    )
    return pl.pallas_call(
        edge_kernel,
        grid_spec=grid_spec,
        out_shape=[jax.ShapeDtypeStruct((tiles, heads, rows, lanes), jnp.bfloat16)] * 2,
        compiler_params=pltpu.CompilerParams(vmem_limit_bytes=EDGE_VMEM),
        cost_estimate=pl.CostEstimate(
            flops=tiles * 2 * rows * lanes * 64 * 256 * 2,
            bytes_accessed=tiles * rows * lanes * heads * 4,
            transcendentals=tiles * rows * lanes * 80,
        ),
        name="edge_terms",
    )(lists, offsets, edges, mix, scale, shift)


def attend_kernel(
    lists,
    slopes,
    offsets,
    edge_ref,
    bias_ref,
    gate_ref,
    key_ref,
    value_ref,
    *rest,
):
    *query_refs, num_ref, query_pairs, acc, tops, totals = rest
    step = pl.program_id(0)
    heads, rows, lanes = bias_ref.shape[1:]
    head_dim = acc.shape[0] // heads

    @pl.when(lists[5, step] > 0)
    def _():
        acc[...] = jnp.zeros_like(acc)
        tops[...] = jnp.full_like(tops, NEG_FILL)
        totals[...] = jnp.zeros_like(totals)
        blank = jnp.zeros((head_dim, lanes), jnp.bfloat16)
        for pair in range(heads // 2):
            query_pairs[pair, :head_dim, lanes:] = blank
            query_pairs[pair, head_dim:, :lanes] = blank
        for place, query_ref in enumerate(query_refs):

            @pl.when(lists[7, step] == place)
            def _(query_ref=query_ref):
                for pair in range(heads // 2):
                    at = pair * 2 * head_dim
                    query_pairs[pair, :head_dim, :lanes] = query_ref[at : at + head_dim, :]
                    at += head_dim
                    query_pairs[pair, head_dim:, lanes:] = query_ref[at : at + head_dim, :]

    @pl.when(lists[4, step] > 0)
    def _():
        key_block = lists[3, step]
        edge_t = edge_ref[0].astype(jnp.float32).T
        for pair in range(heads // 2):
            width = 2 * head_dim
            keys = key_ref[key_block, :, pair * width : (pair + 1) * width]
            both = jnp.dot(keys, query_pairs[pair], preferred_element_type=jnp.float32)
            for side in range(2):
                head = pair * 2 + side
                span = slice(head * head_dim, (head + 1) * head_dim)
                scores = both[:, side * lanes : (side + 1) * lanes] + (
                    bias_ref[0, head].astype(jnp.float32) + (edge_t * slopes[head] + offsets[head])
                )
                old_top = tops[head : head + 1, :]
                new_top = jnp.maximum(old_top, jnp.max(scores, axis=0, keepdims=True))
                factor = jnp.exp(old_top - new_top)
                weights = jnp.exp(scores - new_top)
                totals[head : head + 1, :] = totals[head : head + 1, :] * factor + jnp.sum(
                    weights, axis=0, keepdims=True
                )
                tops[head : head + 1, :] = new_top
                gated = (weights * gate_ref[0, head].astype(jnp.float32)).astype(jnp.bfloat16)
                part = jnp.dot(
                    value_ref[key_block, span, :], gated, preferred_element_type=jnp.float32
                )
                acc[span, :] = acc[span, :] * factor + part

    @pl.when(lists[6, step] > 0)
    def _():
        for head in range(heads):
            span = slice(head * head_dim, (head + 1) * head_dim)
            total = totals[head : head + 1, :]
            inverse = jnp.where(total > 0.0, 1.0 / jnp.where(total > 0.0, total, 1.0), 0.0)
            num_ref[0, span, :] = (acc[span, :] * inverse).astype(num_ref.dtype)
        at = acc.shape[0]
        rest = tops[...]
        for _ in range(TOP_PIECES):
            piece = rest.astype(num_ref.dtype)
            num_ref[0, at : at + heads, :] = piece
            rest = rest - piece.astype(jnp.float32)
            at += heads
        rest = totals[...]
        for _ in range(TOTAL_PIECES):
            piece = rest.astype(num_ref.dtype)
            num_ref[0, at : at + heads, :] = piece
            rest = rest - piece.astype(jnp.float32)
            at += heads


def attend_stage(lists, slopes, offsets, edges, bias, gate, keys, values, queries):
    block_total = len(queries)
    width, lanes = queries[0].shape
    tiles, heads, rows, _ = bias.shape
    packed = width + heads * (TOP_PIECES + TOTAL_PIECES)
    whole = lambda array: pl.BlockSpec(
        array.shape, lambda s, *_: (0,) * array.ndim, pipeline_mode=pl.Buffered(1)
    )
    edge_block = pl.BlockSpec((1, heads, rows, lanes), lambda s, lists, *_: (lists[1, s], 0, 0, 0))
    grid_spec = pltpu.PrefetchScalarGridSpec(
        num_scalar_prefetch=3,
        grid=(tiles,),
        in_specs=[
            pl.BlockSpec((1, rows, lanes), lambda s, lists, *_: (lists[0, s], 0, 0)),
            edge_block,
            edge_block,
            whole(keys),
            whole(values),
        ]
        + [whole(query) for query in queries],
        out_specs=pl.BlockSpec((1, packed, lanes), lambda s, lists, *_: (lists[2, s], 0, 0)),
        scratch_shapes=[
            pltpu.VMEM((heads // 2, 2 * width // heads, 2 * lanes), jnp.bfloat16),
            pltpu.VMEM((width, lanes), jnp.float32),
            pltpu.VMEM((heads, lanes), jnp.float32),
            pltpu.VMEM((heads, lanes), jnp.float32),
        ],
    )
    return pl.pallas_call(
        attend_kernel,
        grid_spec=grid_spec,
        out_shape=jax.ShapeDtypeStruct((block_total, packed, lanes), jnp.bfloat16),
        compiler_params=pltpu.CompilerParams(vmem_limit_bytes=ATTEND_VMEM),
        cost_estimate=pl.CostEstimate(
            flops=tiles * 16 * rows * lanes * width,
            bytes_accessed=tiles * rows * lanes * heads * 4,
            transcendentals=tiles * rows * lanes * heads,
        ),
        name="attend",
    )(lists, slopes, offsets, edges, bias, gate, keys, values, *queries)


def join_kernel(parts_ref, embedded_ref, out_ref, residual, normed, attended):
    width = attended.shape[0]
    count = parts_ref.shape[0]
    heads = (parts_ref.shape[1] - width) // (TOP_PIECES + TOTAL_PIECES)
    head_dim = width // heads

    def rejoin(part, first, pieces):
        whole = jnp.zeros((heads, attended.shape[1]), jnp.float32)
        for piece in range(pieces):
            at = width + (first + piece) * heads
            whole = whole + parts_ref[part, at : at + heads, :].astype(jnp.float32)
        return whole

    tops = [rejoin(part, 0, TOP_PIECES) for part in range(count)]
    top = functools.reduce(jnp.maximum, tops)
    shares = [
        rejoin(part, TOP_PIECES, TOTAL_PIECES) * jnp.exp(tops[part] - top)
        for part in range(count)
    ]
    inverse = 1.0 / functools.reduce(jnp.add, shares)
    shares = [share * inverse for share in shares]
    for head in range(heads):
        span = slice(head * head_dim, (head + 1) * head_dim)
        merged = jnp.zeros((head_dim, attended.shape[1]), jnp.float32)
        for part in range(count):
            merged = merged + parts_ref[part, span, :].astype(jnp.float32) * (
                shares[part][head : head + 1]
            )
        attended[span, :] = merged
    rows = attended[...].T.astype(jnp.bfloat16)
    values = embedded_ref[...] + jnp.dot(
        rows, out_ref[...], preferred_element_type=jnp.float32
    )
    residual[...] = values
    normed[...] = layer_norm(values).astype(jnp.bfloat16)


def join_stage(parts, embedded, w_out):
    rows, width = embedded.shape
    return pl.pallas_call(
        join_kernel,
        out_shape=[
            jax.ShapeDtypeStruct((rows, width), jnp.float32),
            jax.ShapeDtypeStruct((rows, width), jnp.bfloat16),
        ],
        scratch_shapes=[pltpu.VMEM((width, parts.shape[2]), jnp.float32)],
        compiler_params=pltpu.CompilerParams(vmem_limit_bytes=JOIN_VMEM),
        name="join",
    )(parts, embedded, w_out)


def feed_kernel(own_ref, other_ref, weight_ref, own_sum, other_sum, normed, acc):
    step = pl.program_id(0)
    rows, width = own_ref.shape
    shards, depth, span = weight_ref.shape
    tall = depth // 2
    units = span // 2

    @pl.when(step == 0)
    def _():
        normed[:rows, :] = own_ref[...]
        normed[rows:, :] = other_ref[...]
        acc[...] = jnp.zeros_like(acc)

    pre = jnp.zeros((2 * rows, shards * units), jnp.float32)
    for piece in range(width // tall):
        up = jnp.concatenate(
            [
                weight_ref[shard, :tall, piece * units : (piece + 1) * units]
                for shard in range(shards)
            ],
            axis=1,
        )
        pre = pre + jnp.dot(
            normed[:, piece * tall : (piece + 1) * tall], up, preferred_element_type=jnp.float32
        )
    hidden = (0.5 * pre * (1.0 + lax.erf(pre * (0.5**0.5)))).astype(jnp.bfloat16)
    for piece in range(width // span):
        down = jnp.concatenate(
            [
                weight_ref[shard, tall + piece * units : tall + (piece + 1) * units, :]
                for shard in range(shards)
            ],
            axis=0,
        )
        acc[:, piece * span : (piece + 1) * span] += jnp.dot(
            hidden, down, preferred_element_type=jnp.float32
        )

    @pl.when(step == pl.num_programs(0) - 1)
    def _():
        own_sum[...] = acc[:rows, :]
        other_sum[...] = acc[rows:, :]


def feed_stage(own, other, weights):
    shards, depth, span = weights.shape
    rows, width = own.shape
    group = 2
    flat = pl.BlockSpec((rows, width), lambda s: (0, 0))
    return pl.pallas_call(
        feed_kernel,
        grid=(shards // group,),
        in_specs=[flat, flat, pl.BlockSpec((group, depth, span), lambda s: (s, 0, 0))],
        out_specs=[flat, flat],
        out_shape=[jax.ShapeDtypeStruct((rows, width), jnp.float32)] * 2,
        scratch_shapes=[
            pltpu.VMEM((2 * rows, width), jnp.bfloat16),
            pltpu.VMEM((2 * rows, width), jnp.float32),
        ],
        compiler_params=pltpu.CompilerParams(vmem_limit_bytes=FEED_VMEM),
        name="feed",
    )(own, other, weights)


def half_kernel(core, up_ref, down_ref, out_ref):
    tall = up_ref.shape[0] // 2
    units, width = down_ref.shape
    span = 2 * units
    out_ref[:tall, :units] = up_ref[:tall, :]
    out_ref[:tall, units:] = up_ref[tall:, :]
    for piece in range(width // span):
        out_ref[tall + piece * units : tall + (piece + 1) * units, :] = down_ref[
            :, piece * span : (piece + 1) * span
        ]


def half_weights(w_up, w_down, core):
    width, span = w_up.shape
    units = span // 2
    grid_spec = pltpu.PrefetchScalarGridSpec(
        num_scalar_prefetch=1,
        grid=(1,),
        in_specs=[
            pl.BlockSpec((width, units), lambda s, core: (0, core[0])),
            pl.BlockSpec((units, width), lambda s, core: (core[0], 0)),
        ],
        out_specs=pl.BlockSpec((width, span), lambda s, core: (0, 0)),
    )
    return pl.pallas_call(
        half_kernel,
        grid_spec=grid_spec,
        out_shape=jax.ShapeDtypeStruct((width, span), w_up.dtype),
        name="half_weights",
    )(core.reshape(1), w_up, w_down)


def mix_matrix(edge_proj, heads):
    channel_count, outs = edge_proj.shape
    factors = jnp.where(jnp.arange(outs) < heads, 0.5, 0.25).astype(jnp.bfloat16)
    scaled = (edge_proj * factors[None, :]).T
    eye = jnp.eye(8, dtype=jnp.bfloat16)
    mixed = scaled[:, None, None, :] * eye[None, :, :, None]
    offsets = jnp.sum(scaled.astype(jnp.float32), axis=1)
    return mixed.reshape(outs * 8, 8 * channel_count), offsets


def shift_chip(value, by):
    return lax.ppermute(value, "kcol", [(i, (i + 2 * by) & 7) for i in range(8)])


def after(value, others):
    return lax.optimization_barrier((value, others))[0]


def swap_core(value):
    return lax.ppermute(value, "kcol", [(i, i ^ 1) for i in range(8)])


def local(
    features,
    node_ids,
    token_embed,
    w_query,
    w_key,
    w_value,
    w_out,
    slopes,
    chan_scale,
    chan_shift,
    edge_proj,
    edge_value,
    key_index,
    counts,
    w_up,
    w_down,
):
    node_dev, width = features.shape
    vocab_size = token_embed.shape[0]
    heads = slopes.shape[0]
    head_dim = width // heads
    rows = edge_value.shape[-1]
    col_at = lax.axis_index("kcol")
    core = col_at & 1
    one_hot = (
        node_ids[:, None] == lax.broadcasted_iota(jnp.int32, (node_dev, vocab_size), 1)
    ).astype(jnp.bfloat16)
    embedded = features.astype(jnp.float32) + jnp.dot(
        one_hot, token_embed, preferred_element_type=jnp.float32
    )
    normed = layer_norm(embedded).astype(jnp.bfloat16)

    column_nodes = lax.all_gather(normed, "qrow", axis=0)
    query_own = (
        jnp.einsum("kd,nk->dn", w_query, normed, preferred_element_type=jnp.float32).astype(
            jnp.bfloat16
        )
        * jnp.bfloat16(head_dim ** (-0.5))
    )
    weights = half_weights(w_up, w_down, core)
    queries = [query_own] + [shift_chip(query_own, by) for by in (1, -1, 2)]
    weights = lax.all_gather(after(weights, query_own), "qrow", axis=0)
    lists = list_stage(counts, key_index[:, 0], jnp.stack([col_at >> 1, core]))
    mix, offsets = mix_matrix(edge_proj, heads)
    spread = lambda vector: jnp.broadcast_to((0.5 * vector)[:, None], (vector.shape[0], rows))
    edges = edge_value.reshape(-1, rows, rows)
    scale, shift = spread(chan_scale), spread(chan_shift)
    *queries, lists, mix, offsets, scale, shift = lax.optimization_barrier(
        (*queries, lists, mix, offsets, scale, shift)
    )
    queries = queries + [swap_core(query) for query in queries]
    bias, gate = edge_stage(after(lists, queries), offsets, edges, mix, scale, shift, heads)
    column_nodes, bias = lax.optimization_barrier((column_nodes, bias))
    keys = jnp.einsum(
        "gnk,kd->gnd", column_nodes, w_key, preferred_element_type=jnp.float32
    ).astype(jnp.bfloat16)
    values = jnp.einsum(
        "kd,gnk->gdn", w_value, column_nodes, preferred_element_type=jnp.float32
    ).astype(jnp.bfloat16)
    parts = attend_stage(lists, slopes, offsets, edges, bias, gate, keys, values, queries)
    parts = lax.all_to_all(parts, "kcol", 0, 0, tiled=True)
    weights, parts = lax.optimization_barrier((weights, parts))
    residual, normed_two = join_stage(parts, embedded, w_out)
    own_sum, other_sum = feed_stage(normed_two, swap_core(normed_two), weights)
    return (residual + (own_sum + swap_core(other_sum))).astype(jnp.bfloat16)


def solution(mesh):
    placed = (
        P(("qrow", "kcol"), None),
        P(("qrow", "kcol")),
        P(),
        P(),
        P(),
        P(),
        P(),
        P(),
        P(),
        P(),
        P(),
        P("qrow", "kcol", None, None, None),
        P("qrow", "kcol", None),
        P("qrow", "kcol"),
        P(None, "qrow"),
        P("qrow", None),
    )
    return jax.shard_map(
        local, mesh=mesh, in_specs=placed, out_specs=P(("qrow", "kcol"), None), check_vma=False
    )
```

```python
import functools

import jax
import jax.numpy as jnp
from jax import lax
from jax.experimental import pallas as pl
from jax.experimental.pallas import tpu as pltpu
from jax.sharding import PartitionSpec as P

NEG_FILL = -1e30
HEAD_PARTS = 2
TOP_PIECES = 3
TOTAL_PIECES = 3
EDGE_VMEM = 56 * 1024 * 1024
ATTEND_VMEM = 44 * 1024 * 1024
JOIN_VMEM = 24 * 1024 * 1024
FEED_VMEM = 24 * 1024 * 1024


def layer_norm(values):
    average = jnp.mean(values, axis=-1, keepdims=True)
    centered = values - average
    spread = jnp.mean(centered * centered, axis=-1, keepdims=True)
    return centered * lax.rsqrt(spread + 1e-05)


def list_kernel(counts_ref, index_ref, place_ref, lists_ref):
    block_total, slot_count = index_ref.shape
    total = block_total * slot_count
    chip, core = place_ref[0], place_ref[1]

    def relative(theirs, ours):
        gap = (theirs - ours + 4) & 3
        return jnp.where(gap == 0, 0, jnp.where(gap == 3, 1, gap + 1))

    filled = jnp.int32(0)
    for block in range(block_total):
        count = counts_ref[block, 0]
        partner = jnp.where(core == block % 2, 0, 4) + relative(jnp.int32(block // 2), chip)
        visits = jnp.maximum(count, 1)
        for slot in range(slot_count):

            @pl.when(slot < visits)
            def _(at=filled, block=block, slot=slot, partner=partner, count=count, visits=visits):
                key_block = index_ref[block, slot]
                lists_ref[0, at] = jnp.int32(block * slot_count + slot)
                lists_ref[1, at] = at
                lists_ref[2, at] = jnp.int32(block)
                lists_ref[3, at] = key_block
                lists_ref[4, at] = (slot < count).astype(jnp.int32)
                lists_ref[5, at] = jnp.int32(slot == 0)
                lists_ref[6, at] = (visits == slot + 1).astype(jnp.int32)
                lists_ref[7, at] = partner

            filled = filled + (slot < visits).astype(jnp.int32)

    @pl.loop(0, total)
    def _(step):
        @pl.when(step >= filled)
        def _():
            for row in range(4):
                lists_ref[row, step] = lists_ref[row, filled - 1]
            for row in range(4, 7):
                lists_ref[row, step] = jnp.int32(0)
            lists_ref[7, step] = lists_ref[7, filled - 1]


def list_stage(counts, index, place):
    scalars = pl.BlockSpec(memory_space=pltpu.SMEM)
    return pl.pallas_call(
        list_kernel,
        in_specs=[scalars] * 3,
        out_specs=scalars,
        out_shape=jax.ShapeDtypeStruct((8, index.shape[0] * index.shape[1]), jnp.int32),
        name="lists",
    )(counts, index, place)


def edge_kernel(
    lists, offsets, edge_ref, mix_ref, scale_ref, shift_ref, bias_ref, gate_ref, edge_t
):
    step = pl.program_id(0)
    heads = bias_ref.shape[1]
    rows, lanes = edge_t.shape

    @pl.when(lists[4, step] > 0)
    def _():
        edge_t[...] = edge_ref[0].astype(jnp.float32).T
        scale = scale_ref[...]
        shift = shift_ref[...]

        def channels(row):
            line = jnp.broadcast_to(edge_t[row : row + 1, :], scale.shape)
            return jnp.tanh((line * scale + shift).astype(jnp.bfloat16))

        def build(part):
            return jnp.concatenate(
                [
                    jnp.concatenate(
                        [channels(part * 16 + half * 8 + within) for within in range(8)], axis=0
                    )
                    for half in range(2)
                ],
                axis=1,
            )

        for part in range(rows // 16):
            terms = jnp.dot(mix_ref[...], build(part), preferred_element_type=jnp.float32)
            span = slice(part * 16, part * 16 + 16)
            for head in range(heads):
                block = terms[head * 8 : head * 8 + 8]
                both = jnp.concatenate([block[:, :lanes], block[:, lanes:]], axis=0)
                bias_ref[0, head, span, :] = both.astype(jnp.bfloat16)
                block = terms[(heads + head) * 8 : (heads + head) * 8 + 8]
                both = jnp.concatenate([block[:, :lanes], block[:, lanes:]], axis=0)
                gate_ref[0, head, span, :] = (
                    0.5 + 0.5 * jnp.tanh(both + offsets[heads + head])
                ).astype(jnp.bfloat16)


def edge_stage(lists, offsets, edges, mix, scale, shift, heads):
    tiles, rows, lanes = edges.shape
    out = pl.BlockSpec((1, heads, rows, lanes), lambda s, lists, *_: (lists[1, s], 0, 0, 0))
    grid_spec = pltpu.PrefetchScalarGridSpec(
        num_scalar_prefetch=2,
        grid=(tiles,),
        in_specs=[
            pl.BlockSpec((1, rows, lanes), lambda s, lists, *_: (lists[0, s], 0, 0)),
            pl.BlockSpec(mix.shape, lambda s, *_: (0, 0)),
            pl.BlockSpec(scale.shape, lambda s, *_: (0, 0)),
            pl.BlockSpec(shift.shape, lambda s, *_: (0, 0)),
        ],
        out_specs=[out, out],
        scratch_shapes=[
            pltpu.VMEM((rows, lanes), jnp.float32),
        ],
    )
    return pl.pallas_call(
        edge_kernel,
        grid_spec=grid_spec,
        out_shape=[jax.ShapeDtypeStruct((tiles, heads, rows, lanes), jnp.bfloat16)] * 2,
        compiler_params=pltpu.CompilerParams(vmem_limit_bytes=EDGE_VMEM),
        cost_estimate=pl.CostEstimate(
            flops=tiles * 2 * rows * lanes * 64 * 256 * 2,
            bytes_accessed=tiles * rows * lanes * heads * 4,
            transcendentals=tiles * rows * lanes * 80,
        ),
        name="edge_terms",
    )(lists, offsets, edges, mix, scale, shift)


def attend_kernel(
    first_head,
    lists,
    slopes,
    offsets,
    edge_ref,
    bias_ref,
    gate_ref,
    key_ref,
    value_ref,
    *rest,
):
    *query_refs, num_ref, query_pairs, acc, tops, totals = rest
    step = pl.program_id(0)
    heads, rows, lanes = bias_ref.shape[1:]
    head_dim = acc.shape[0] // heads

    @pl.when(lists[5, step] > 0)
    def _():
        acc[...] = jnp.zeros_like(acc)
        tops[...] = jnp.full_like(tops, NEG_FILL)
        totals[...] = jnp.zeros_like(totals)
        blank = jnp.zeros((head_dim, lanes), jnp.bfloat16)
        for pair in range(heads // 2):
            query_pairs[pair, :head_dim, lanes:] = blank
            query_pairs[pair, head_dim:, :lanes] = blank
        for place, query_ref in enumerate(query_refs):

            @pl.when(lists[7, step] == place)
            def _(query_ref=query_ref):
                for pair in range(heads // 2):
                    at = pair * 2 * head_dim
                    query_pairs[pair, :head_dim, :lanes] = query_ref[at : at + head_dim, :]
                    at += head_dim
                    query_pairs[pair, head_dim:, lanes:] = query_ref[at : at + head_dim, :]

    @pl.when(lists[4, step] > 0)
    def _():
        key_block = lists[3, step]
        edge_t = edge_ref[0].astype(jnp.float32).T
        for pair in range(heads // 2):
            width = 2 * head_dim
            keys = key_ref[key_block, :, pair * width : (pair + 1) * width]
            both = jnp.dot(keys, query_pairs[pair], preferred_element_type=jnp.float32)
            for side in range(2):
                head = pair * 2 + side
                span = slice(head * head_dim, (head + 1) * head_dim)
                scores = both[:, side * lanes : (side + 1) * lanes] + (
                    bias_ref[0, head].astype(jnp.float32) + (
                        edge_t * slopes[first_head + head] + offsets[first_head + head]
                    )
                )
                old_top = tops[head : head + 1, :]
                new_top = jnp.maximum(old_top, jnp.max(scores, axis=0, keepdims=True))
                factor = jnp.exp(old_top - new_top)
                weights = jnp.exp(scores - new_top)
                totals[head : head + 1, :] = totals[head : head + 1, :] * factor + jnp.sum(
                    weights, axis=0, keepdims=True
                )
                tops[head : head + 1, :] = new_top
                gated = (weights * gate_ref[0, head].astype(jnp.float32)).astype(jnp.bfloat16)
                part = jnp.dot(
                    value_ref[key_block, span, :], gated, preferred_element_type=jnp.float32
                )
                acc[span, :] = acc[span, :] * factor + part

    @pl.when(lists[6, step] > 0)
    def _():
        for head in range(heads):
            span = slice(head * head_dim, (head + 1) * head_dim)
            total = totals[head : head + 1, :]
            inverse = jnp.where(total > 0.0, 1.0 / jnp.where(total > 0.0, total, 1.0), 0.0)
            num_ref[0, span, :] = (acc[span, :] * inverse).astype(num_ref.dtype)
        at = acc.shape[0]
        rest = tops[...]
        for _ in range(TOP_PIECES):
            piece = rest.astype(num_ref.dtype)
            num_ref[0, at : at + heads, :] = piece
            rest = rest - piece.astype(jnp.float32)
            at += heads
        rest = totals[...]
        for _ in range(TOTAL_PIECES):
            piece = rest.astype(num_ref.dtype)
            num_ref[0, at : at + heads, :] = piece
            rest = rest - piece.astype(jnp.float32)
            at += heads


def attend_stage(part, part_count, lists, slopes, offsets, edges, bias, gate, keys, values, queries):
    block_total = len(queries)
    tiles, heads, rows, lanes = bias.shape
    heads //= part_count
    width = queries[0].shape[0] // part_count
    packed = width + heads * (TOP_PIECES + TOTAL_PIECES)
    once = pl.Buffered(1)
    edge_block = pl.BlockSpec(
        (1, heads, rows, lanes), lambda s, lists, *_: (lists[1, s], part, 0, 0)
    )
    grid_spec = pltpu.PrefetchScalarGridSpec(
        num_scalar_prefetch=3,
        grid=(tiles,),
        in_specs=[
            pl.BlockSpec((1, rows, lanes), lambda s, lists, *_: (lists[0, s], 0, 0)),
            edge_block,
            edge_block,
            pl.BlockSpec(keys.shape, lambda s, *_: (0, 0, 0), pipeline_mode=once),
            pl.BlockSpec(values.shape, lambda s, *_: (0, 0, 0), pipeline_mode=once),
        ]
        + [pl.BlockSpec((width, lanes), lambda s, *_: (part, 0), pipeline_mode=once)] * block_total,
        out_specs=pl.BlockSpec((1, packed, lanes), lambda s, lists, *_: (lists[2, s], 0, 0)),
        scratch_shapes=[
            pltpu.VMEM((heads // 2, 2 * width // heads, 2 * lanes), jnp.bfloat16),
            pltpu.VMEM((width, lanes), jnp.float32),
            pltpu.VMEM((heads, lanes), jnp.float32),
            pltpu.VMEM((heads, lanes), jnp.float32),
        ],
    )
    return pl.pallas_call(
        functools.partial(attend_kernel, part * heads),
        grid_spec=grid_spec,
        out_shape=jax.ShapeDtypeStruct((block_total, packed, lanes), jnp.bfloat16),
        compiler_params=pltpu.CompilerParams(vmem_limit_bytes=ATTEND_VMEM),
        cost_estimate=pl.CostEstimate(
            flops=tiles * 16 * rows * lanes * width,
            bytes_accessed=tiles * rows * lanes * heads * 4,
            transcendentals=tiles * rows * lanes * heads,
        ),
        name="attend",
    )(lists, slopes, offsets, edges, bias, gate, keys, values, *queries)


def join_part(parts_ref, attended):
    width = attended.shape[0]
    count = parts_ref.shape[0]
    heads = (parts_ref.shape[1] - width) // (TOP_PIECES + TOTAL_PIECES)
    head_dim = width // heads

    def rejoin(part, first, pieces):
        whole = jnp.zeros((heads, attended.shape[1]), jnp.float32)
        for piece in range(pieces):
            at = width + (first + piece) * heads
            whole = whole + parts_ref[part, at : at + heads, :].astype(jnp.float32)
        return whole

    tops = [rejoin(part, 0, TOP_PIECES) for part in range(count)]
    top = functools.reduce(jnp.maximum, tops)
    shares = [
        rejoin(part, TOP_PIECES, TOTAL_PIECES) * jnp.exp(tops[part] - top)
        for part in range(count)
    ]
    inverse = 1.0 / functools.reduce(jnp.add, shares)
    shares = [share * inverse for share in shares]
    for head in range(heads):
        span = slice(head * head_dim, (head + 1) * head_dim)
        merged = jnp.zeros((head_dim, attended.shape[1]), jnp.float32)
        for part in range(count):
            merged = merged + parts_ref[part, span, :].astype(jnp.float32) * (
                shares[part][head : head + 1]
            )
        attended[span, :] = merged


def join_kernel(*refs):
    *parts, embedded_ref, out_ref, residual, normed, attended = refs
    width = attended.shape[0] // len(parts)
    for at, parts_ref in enumerate(parts):
        join_part(parts_ref, attended.at[at * width : (at + 1) * width])
    rows = attended[...].T.astype(jnp.bfloat16)
    values = embedded_ref[...] + jnp.dot(
        rows, out_ref[...], preferred_element_type=jnp.float32
    )
    residual[...] = values
    normed[...] = layer_norm(values).astype(jnp.bfloat16)


def join_stage(parts, embedded, w_out):
    rows, width = embedded.shape
    return pl.pallas_call(
        join_kernel,
        out_shape=[
            jax.ShapeDtypeStruct((rows, width), jnp.float32),
            jax.ShapeDtypeStruct((rows, width), jnp.bfloat16),
        ],
        scratch_shapes=[pltpu.VMEM((width, parts[0].shape[2]), jnp.float32)],
        compiler_params=pltpu.CompilerParams(vmem_limit_bytes=JOIN_VMEM),
        name="join",
    )(*parts, embedded, w_out)


def feed_kernel(own_ref, other_ref, weight_ref, own_sum, other_sum, normed, acc):
    step = pl.program_id(0)
    rows, width = own_ref.shape
    shards, depth, span = weight_ref.shape
    tall = depth // 2
    units = span // 2

    @pl.when(step == 0)
    def _():
        normed[:rows, :] = own_ref[...]
        normed[rows:, :] = other_ref[...]
        acc[...] = jnp.zeros_like(acc)

    pre = jnp.zeros((2 * rows, shards * units), jnp.float32)
    for piece in range(width // tall):
        up = jnp.concatenate(
            [
                weight_ref[shard, :tall, piece * units : (piece + 1) * units]
                for shard in range(shards)
            ],
            axis=1,
        )
        pre = pre + jnp.dot(
            normed[:, piece * tall : (piece + 1) * tall], up, preferred_element_type=jnp.float32
        )
    hidden = (0.5 * pre * (1.0 + lax.erf(pre * (0.5**0.5)))).astype(jnp.bfloat16)
    for piece in range(width // span):
        down = jnp.concatenate(
            [
                weight_ref[shard, tall + piece * units : tall + (piece + 1) * units, :]
                for shard in range(shards)
            ],
            axis=0,
        )
        acc[:, piece * span : (piece + 1) * span] += jnp.dot(
            hidden, down, preferred_element_type=jnp.float32
        )

    @pl.when(step == pl.num_programs(0) - 1)
    def _():
        own_sum[...] = acc[:rows, :]
        other_sum[...] = acc[rows:, :]


def feed_stage(own, other, weights):
    shards, depth, span = weights.shape
    rows, width = own.shape
    group = 2
    flat = pl.BlockSpec((rows, width), lambda s: (0, 0))
    return pl.pallas_call(
        feed_kernel,
        grid=(shards // group,),
        in_specs=[flat, flat, pl.BlockSpec((group, depth, span), lambda s: (s, 0, 0))],
        out_specs=[flat, flat],
        out_shape=[jax.ShapeDtypeStruct((rows, width), jnp.float32)] * 2,
        scratch_shapes=[
            pltpu.VMEM((2 * rows, width), jnp.bfloat16),
            pltpu.VMEM((2 * rows, width), jnp.float32),
        ],
        compiler_params=pltpu.CompilerParams(vmem_limit_bytes=FEED_VMEM),
        name="feed",
    )(own, other, weights)


def half_kernel(core, up_ref, down_ref, out_ref):
    tall = up_ref.shape[0] // 2
    units, width = down_ref.shape
    span = 2 * units
    out_ref[:tall, :units] = up_ref[:tall, :]
    out_ref[:tall, units:] = up_ref[tall:, :]
    for piece in range(width // span):
        out_ref[tall + piece * units : tall + (piece + 1) * units, :] = down_ref[
            :, piece * span : (piece + 1) * span
        ]


def half_weights(w_up, w_down, core):
    width, span = w_up.shape
    units = span // 2
    grid_spec = pltpu.PrefetchScalarGridSpec(
        num_scalar_prefetch=1,
        grid=(1,),
        in_specs=[
            pl.BlockSpec((width, units), lambda s, core: (0, core[0])),
            pl.BlockSpec((units, width), lambda s, core: (core[0], 0)),
        ],
        out_specs=pl.BlockSpec((width, span), lambda s, core: (0, 0)),
    )
    return pl.pallas_call(
        half_kernel,
        grid_spec=grid_spec,
        out_shape=jax.ShapeDtypeStruct((width, span), w_up.dtype),
        name="half_weights",
    )(core.reshape(1), w_up, w_down)


def mix_matrix(edge_proj, heads):
    channel_count, outs = edge_proj.shape
    factors = jnp.where(jnp.arange(outs) < heads, 0.5, 0.25).astype(jnp.bfloat16)
    scaled = (edge_proj * factors[None, :]).T
    eye = jnp.eye(8, dtype=jnp.bfloat16)
    mixed = scaled[:, None, None, :] * eye[None, :, :, None]
    offsets = jnp.sum(scaled.astype(jnp.float32), axis=1)
    return mixed.reshape(outs * 8, 8 * channel_count), offsets


def shift_chip(value, by):
    return lax.ppermute(value, "kcol", [(i, (i + 2 * by) & 7) for i in range(8)])


def after(value, others):
    return lax.optimization_barrier((value, others))[0]


def swap_core(value):
    return lax.ppermute(value, "kcol", [(i, i ^ 1) for i in range(8)])


def local(
    features,
    node_ids,
    token_embed,
    w_query,
    w_key,
    w_value,
    w_out,
    slopes,
    chan_scale,
    chan_shift,
    edge_proj,
    edge_value,
    key_index,
    counts,
    w_up,
    w_down,
):
    node_dev, width = features.shape
    vocab_size = token_embed.shape[0]
    heads = slopes.shape[0]
    head_dim = width // heads
    rows = edge_value.shape[-1]
    col_at = lax.axis_index("kcol")
    core = col_at & 1
    one_hot = (
        node_ids[:, None] == lax.broadcasted_iota(jnp.int32, (node_dev, vocab_size), 1)
    ).astype(jnp.bfloat16)
    embedded = features.astype(jnp.float32) + jnp.dot(
        one_hot, token_embed, preferred_element_type=jnp.float32
    )
    normed = layer_norm(embedded).astype(jnp.bfloat16)

    column_nodes = lax.all_gather(normed, "qrow", axis=0)
    query_own = (
        jnp.einsum("kd,nk->dn", w_query, normed, preferred_element_type=jnp.float32).astype(
            jnp.bfloat16
        )
        * jnp.bfloat16(head_dim ** (-0.5))
    )
    weights = half_weights(w_up, w_down, core)
    queries = [query_own] + [shift_chip(query_own, by) for by in (1, -1, 2)]
    weights = lax.all_gather(after(weights, query_own), "qrow", axis=0)
    lists = list_stage(counts, key_index[:, 0], jnp.stack([col_at >> 1, core]))
    mix, offsets = mix_matrix(edge_proj, heads)
    spread = lambda vector: jnp.broadcast_to((0.5 * vector)[:, None], (vector.shape[0], rows))
    edges = edge_value.reshape(-1, rows, rows)
    scale, shift = spread(chan_scale), spread(chan_shift)
    *queries, lists, mix, offsets, scale, shift = lax.optimization_barrier(
        (*queries, lists, mix, offsets, scale, shift)
    )
    queries = queries + [swap_core(query) for query in queries]
    bias, gate = edge_stage(after(lists, queries), offsets, edges, mix, scale, shift, heads)
    column_nodes, bias = lax.optimization_barrier((column_nodes, bias))
    parts = []
    for part in range(HEAD_PARTS):
        span = slice(part * width // HEAD_PARTS, (part + 1) * width // HEAD_PARTS)
        keys = jnp.einsum(
            "gnk,kd->gnd", column_nodes, w_key[:, span], preferred_element_type=jnp.float32
        ).astype(jnp.bfloat16)
        values = jnp.einsum(
            "kd,gnk->gdn", w_value[:, span], column_nodes, preferred_element_type=jnp.float32
        ).astype(jnp.bfloat16)
        piece = attend_stage(
            part, HEAD_PARTS, lists, slopes, offsets, edges, bias, gate, keys, values, queries
        )
        column_nodes = after(column_nodes, piece)
        parts.append(lax.all_to_all(after(piece, parts), "kcol", 0, 0, tiled=True))
    weights, parts = lax.optimization_barrier((weights, parts))
    residual, normed_two = join_stage(parts, embedded, w_out)
    own_sum, other_sum = feed_stage(normed_two, swap_core(normed_two), weights)
    return (residual + (own_sum + swap_core(other_sum))).astype(jnp.bfloat16)


def solution(mesh):
    placed = (
        P(("qrow", "kcol"), None),
        P(("qrow", "kcol")),
        P(),
        P(),
        P(),
        P(),
        P(),
        P(),
        P(),
        P(),
        P(),
        P("qrow", "kcol", None, None, None),
        P("qrow", "kcol", None),
        P("qrow", "kcol"),
        P(None, "qrow"),
        P("qrow", None),
    )
    return jax.shard_map(
        local, mesh=mesh, in_specs=placed, out_specs=P(("qrow", "kcol"), None), check_vma=False
    )
```

```python
import functools

import jax
import jax.numpy as jnp
from jax import lax
from jax.experimental import pallas as pl
from jax.experimental.pallas import tpu as pltpu
from jax.sharding import PartitionSpec as P

NEG_FILL = -1e30
HEAD_PARTS = 1
TOP_PIECES = 3
TOTAL_PIECES = 3
EDGE_VMEM = 56 * 1024 * 1024
ATTEND_VMEM = 36 * 1024 * 1024
JOIN_VMEM = 24 * 1024 * 1024
FEED_VMEM = 24 * 1024 * 1024


def layer_norm(values):
    average = jnp.mean(values, axis=-1, keepdims=True)
    centered = values - average
    spread = jnp.mean(centered * centered, axis=-1, keepdims=True)
    return centered * lax.rsqrt(spread + 1e-05)


def list_kernel(counts_ref, index_ref, place_ref, lists_ref):
    block_total, slot_count = index_ref.shape
    total = block_total * slot_count
    chip, core = place_ref[0], place_ref[1]

    def relative(theirs, ours):
        gap = (theirs - ours + 4) & 3
        return jnp.where(gap == 0, 0, jnp.where(gap == 3, 1, gap + 1))

    filled = jnp.int32(0)
    for block in range(block_total):
        count = counts_ref[block, 0]
        partner = jnp.where(core == block % 2, 0, 4) + relative(jnp.int32(block // 2), chip)
        visits = jnp.maximum(count, 1)
        for slot in range(slot_count):

            @pl.when(slot < visits)
            def _(at=filled, block=block, slot=slot, partner=partner, count=count, visits=visits):
                key_block = index_ref[block, slot]
                lists_ref[0, at] = jnp.int32(block * slot_count + slot)
                lists_ref[1, at] = at
                lists_ref[2, at] = jnp.int32(block)
                lists_ref[3, at] = key_block
                lists_ref[4, at] = (slot < count).astype(jnp.int32)
                lists_ref[5, at] = jnp.int32(slot == 0)
                lists_ref[6, at] = (visits == slot + 1).astype(jnp.int32)
                lists_ref[7, at] = partner

            filled = filled + (slot < visits).astype(jnp.int32)

    @pl.loop(0, total)
    def _(step):
        lists_ref[8, step] = filled

        @pl.when(step >= filled)
        def _():
            for row in range(8):
                lists_ref[row, step] = jnp.int32(0)


def list_stage(counts, index, place):
    scalars = pl.BlockSpec(memory_space=pltpu.SMEM)
    return pl.pallas_call(
        list_kernel,
        in_specs=[scalars] * 3,
        out_specs=scalars,
        out_shape=jax.ShapeDtypeStruct((9, index.shape[0] * index.shape[1]), jnp.int32),
        name="lists",
    )(counts, index, place)


def edge_kernel(
    lists,
    offsets,
    edge_ref,
    mix_ref,
    scale_ref,
    shift_ref,
    bias_out,
    gate_out,
    edge_t,
    bias_ref,
    gate_ref,
    sems,
):
    heads = bias_ref.shape[1]
    rows, lanes = edge_t.shape

    steps = lists[8, 0]

    def copies(step, slot):
        return (
            pltpu.make_async_copy(bias_ref.at[slot], bias_out.at[step], sems.at[0, slot]),
            pltpu.make_async_copy(gate_ref.at[slot], gate_out.at[step], sems.at[1, slot]),
        )

    @pl.loop(0, steps)
    def _(step):
        slot = step & 1

        @pl.when(step >= 2)
        def _():
            for copy in copies(step - 2, slot):
                copy.wait()

        edge_t[...] = edge_ref[lists[0, step]].astype(jnp.float32)
        scale = scale_ref[...]
        shift = shift_ref[...]

        def channels(row):
            line = jnp.broadcast_to(edge_t[row : row + 1, :], scale.shape)
            return jnp.tanh((line * scale + shift).astype(jnp.bfloat16))

        def build(part):
            return jnp.concatenate(
                [
                    jnp.concatenate(
                        [channels(part * 16 + half * 8 + within) for within in range(8)], axis=0
                    )
                    for half in range(2)
                ],
                axis=1,
            )

        for part in range(rows // 16):
            terms = jnp.dot(mix_ref[...], build(part), preferred_element_type=jnp.float32)
            span = slice(part * 16, part * 16 + 16)
            for head in range(heads):
                block = terms[head * 8 : head * 8 + 8]
                both = jnp.concatenate([block[:, :lanes], block[:, lanes:]], axis=0)
                bias_ref[slot, head, span, :] = both.astype(jnp.bfloat16)
                block = terms[(heads + head) * 8 : (heads + head) * 8 + 8]
                both = jnp.concatenate([block[:, :lanes], block[:, lanes:]], axis=0)
                gate_ref[slot, head, span, :] = (
                    0.5 + 0.5 * jnp.tanh(both + offsets[heads + head])
                ).astype(jnp.bfloat16)

        for copy in copies(step, slot):
            copy.start()

    @pl.when(steps >= 2)
    def _():
        for copy in copies(steps - 2, steps & 1):
            copy.wait()

    for copy in copies(steps - 1, (steps - 1) & 1):
        copy.wait()


def edge_stage(lists, offsets, edges, mix, scale, shift, heads):
    tiles, rows, lanes = edges.shape
    scalars = pl.BlockSpec(memory_space=pltpu.SMEM)
    held = pl.BlockSpec(memory_space=pltpu.VMEM)
    return pl.pallas_call(
        edge_kernel,
        in_specs=[scalars, scalars, held, held, held, held],
        out_specs=[pl.BlockSpec(memory_space=pl.ANY)] * 2,
        out_shape=[jax.ShapeDtypeStruct((tiles, heads, rows, lanes), jnp.bfloat16)] * 2,
        scratch_shapes=[
            pltpu.VMEM((rows, lanes), jnp.float32),
            pltpu.VMEM((2, heads, rows, lanes), jnp.bfloat16),
            pltpu.VMEM((2, heads, rows, lanes), jnp.bfloat16),
            pltpu.SemaphoreType.DMA((2, 2)),
        ],
        compiler_params=pltpu.CompilerParams(vmem_limit_bytes=EDGE_VMEM),
        cost_estimate=pl.CostEstimate(
            flops=tiles * 2 * rows * lanes * 64 * 256 * 2,
            bytes_accessed=tiles * rows * lanes * heads * 4,
            transcendentals=tiles * rows * lanes * 80,
        ),
        name="edge_terms",
    )(lists, offsets, edges, mix, scale, shift)


def attend_kernel(
    first_head,
    lists,
    slopes,
    offsets,
    edge_ref,
    bias_in,
    gate_in,
    key_ref,
    value_ref,
    *rest,
):
    *query_refs, num_ref, query_pairs, acc, tops, totals, bias_ref, gate_ref, sems = rest
    heads, rows, lanes = bias_ref.shape[1:]
    head_dim = acc.shape[0] // heads
    steps = lists[8, 0]

    def copies(step, slot):
        span = slice(first_head, first_head + heads)
        return (
            pltpu.make_async_copy(bias_in.at[step, span], bias_ref.at[slot], sems.at[0, slot]),
            pltpu.make_async_copy(gate_in.at[step, span], gate_ref.at[slot], sems.at[1, slot]),
        )

    for copy in copies(0, 0):
        copy.start()

    @pl.loop(0, steps)
    def _(step):
        slot = step & 1

        @pl.when(step + 1 < steps)
        def _():
            for copy in copies(step + 1, 1 - slot):
                copy.start()

        for copy in copies(step, slot):
            copy.wait()

        @pl.when(lists[5, step] > 0)
        def _():
            acc[...] = jnp.zeros_like(acc)
            tops[...] = jnp.full_like(tops, NEG_FILL)
            totals[...] = jnp.zeros_like(totals)
            blank = jnp.zeros((head_dim, lanes), jnp.bfloat16)
            for pair in range(heads // 2):
                query_pairs[pair, :head_dim, lanes:] = blank
                query_pairs[pair, head_dim:, :lanes] = blank
            for place, query_ref in enumerate(query_refs):

                @pl.when(lists[7, step] == place)
                def _(query_ref=query_ref):
                    for pair in range(heads // 2):
                        at = (first_head + pair * 2) * head_dim
                        query_pairs[pair, :head_dim, :lanes] = query_ref[at : at + head_dim, :]
                        at += head_dim
                        query_pairs[pair, head_dim:, lanes:] = query_ref[at : at + head_dim, :]

        @pl.when(lists[4, step] > 0)
        def _():
            key_block = lists[3, step]
            edge_t = edge_ref[lists[0, step]].astype(jnp.float32)
            for pair in range(heads // 2):
                width = 2 * head_dim
                keys = key_ref[key_block, :, pair * width : (pair + 1) * width]
                both = jnp.dot(keys, query_pairs[pair], preferred_element_type=jnp.float32)
                for side in range(2):
                    head = pair * 2 + side
                    span = slice(head * head_dim, (head + 1) * head_dim)
                    scores = both[:, side * lanes : (side + 1) * lanes] + (
                        bias_ref[slot, head].astype(jnp.float32) + (
                            edge_t * slopes[first_head + head] + offsets[first_head + head]
                        )
                    )
                    old_top = tops[head : head + 1, :]
                    new_top = jnp.maximum(old_top, jnp.max(scores, axis=0, keepdims=True))
                    factor = jnp.exp(old_top - new_top)
                    weights = jnp.exp(scores - new_top)
                    totals[head : head + 1, :] = totals[head : head + 1, :] * factor + jnp.sum(
                        weights, axis=0, keepdims=True
                    )
                    tops[head : head + 1, :] = new_top
                    gated = (weights * gate_ref[slot, head].astype(jnp.float32)).astype(jnp.bfloat16)
                    part = jnp.dot(
                        value_ref[key_block, span, :], gated, preferred_element_type=jnp.float32
                    )
                    acc[span, :] = acc[span, :] * factor + part

        @pl.when(lists[6, step] > 0)
        def _():
            for head in range(heads):
                span = slice(head * head_dim, (head + 1) * head_dim)
                total = totals[head : head + 1, :]
                inverse = jnp.where(total > 0.0, 1.0 / jnp.where(total > 0.0, total, 1.0), 0.0)
                num_ref[lists[2, step], span, :] = (acc[span, :] * inverse).astype(num_ref.dtype)
            at = acc.shape[0]
            rest = tops[...]
            for _ in range(TOP_PIECES):
                piece = rest.astype(num_ref.dtype)
                num_ref[lists[2, step], at : at + heads, :] = piece
                rest = rest - piece.astype(jnp.float32)
                at += heads
            rest = totals[...]
            for _ in range(TOTAL_PIECES):
                piece = rest.astype(num_ref.dtype)
                num_ref[lists[2, step], at : at + heads, :] = piece
                rest = rest - piece.astype(jnp.float32)
                at += heads


def attend_stage(part, part_count, lists, slopes, offsets, edges, bias, gate, keys, values, queries):
    block_total = len(queries)
    tiles, heads, rows, lanes = bias.shape
    heads //= part_count
    width = queries[0].shape[0] // part_count
    packed = width + heads * (TOP_PIECES + TOTAL_PIECES)
    scalars = pl.BlockSpec(memory_space=pltpu.SMEM)
    held = pl.BlockSpec(memory_space=pltpu.VMEM)
    far = pl.BlockSpec(memory_space=pl.ANY)
    return pl.pallas_call(
        functools.partial(attend_kernel, part * heads),
        in_specs=[scalars] * 3 + [held, far, far] + [held] * (2 + block_total),
        out_specs=held,
        out_shape=jax.ShapeDtypeStruct((block_total, packed, lanes), jnp.bfloat16),
        scratch_shapes=[
            pltpu.VMEM((heads // 2, 2 * width // heads, 2 * lanes), jnp.bfloat16),
            pltpu.VMEM((width, lanes), jnp.float32),
            pltpu.VMEM((heads, lanes), jnp.float32),
            pltpu.VMEM((heads, lanes), jnp.float32),
            pltpu.VMEM((2, heads, rows, lanes), jnp.bfloat16),
            pltpu.VMEM((2, heads, rows, lanes), jnp.bfloat16),
            pltpu.SemaphoreType.DMA((2, 2)),
        ],
        compiler_params=pltpu.CompilerParams(vmem_limit_bytes=ATTEND_VMEM),
        cost_estimate=pl.CostEstimate(
            flops=tiles * 16 * rows * lanes * width,
            bytes_accessed=tiles * rows * lanes * heads * 4,
            transcendentals=tiles * rows * lanes * heads,
        ),
        name="attend",
    )(lists, slopes, offsets, edges, bias, gate, keys, values, *queries)


def join_part(parts_ref, attended):
    width = attended.shape[0]
    count = parts_ref.shape[0]
    heads = (parts_ref.shape[1] - width) // (TOP_PIECES + TOTAL_PIECES)
    head_dim = width // heads

    def rejoin(part, first, pieces):
        whole = jnp.zeros((heads, attended.shape[1]), jnp.float32)
        for piece in range(pieces):
            at = width + (first + piece) * heads
            whole = whole + parts_ref[part, at : at + heads, :].astype(jnp.float32)
        return whole

    tops = [rejoin(part, 0, TOP_PIECES) for part in range(count)]
    top = functools.reduce(jnp.maximum, tops)
    shares = [
        rejoin(part, TOP_PIECES, TOTAL_PIECES) * jnp.exp(tops[part] - top)
        for part in range(count)
    ]
    inverse = 1.0 / functools.reduce(jnp.add, shares)
    shares = [share * inverse for share in shares]
    for head in range(heads):
        span = slice(head * head_dim, (head + 1) * head_dim)
        merged = jnp.zeros((head_dim, attended.shape[1]), jnp.float32)
        for part in range(count):
            merged = merged + parts_ref[part, span, :].astype(jnp.float32) * (
                shares[part][head : head + 1]
            )
        attended[span, :] = merged


def join_kernel(*refs):
    *parts, embedded_ref, out_ref, residual, normed, attended = refs
    width = attended.shape[0] // len(parts)
    for at, parts_ref in enumerate(parts):
        join_part(parts_ref, attended.at[at * width : (at + 1) * width])
    rows = attended[...].T.astype(jnp.bfloat16)
    values = embedded_ref[...] + jnp.dot(
        rows, out_ref[...], preferred_element_type=jnp.float32
    )
    residual[...] = values
    normed[...] = layer_norm(values).astype(jnp.bfloat16)


def join_stage(parts, embedded, w_out):
    rows, width = embedded.shape
    return pl.pallas_call(
        join_kernel,
        out_shape=[
            jax.ShapeDtypeStruct((rows, width), jnp.float32),
            jax.ShapeDtypeStruct((rows, width), jnp.bfloat16),
        ],
        scratch_shapes=[pltpu.VMEM((width, parts[0].shape[2]), jnp.float32)],
        compiler_params=pltpu.CompilerParams(vmem_limit_bytes=JOIN_VMEM),
        name="join",
    )(*parts, embedded, w_out)


def feed_kernel(own_ref, other_ref, weight_ref, own_sum, other_sum, normed, acc):
    step = pl.program_id(0)
    rows, width = own_ref.shape
    shards, depth, span = weight_ref.shape
    tall = depth // 2
    units = span // 2

    @pl.when(step == 0)
    def _():
        normed[:rows, :] = own_ref[...]
        normed[rows:, :] = other_ref[...]
        acc[...] = jnp.zeros_like(acc)

    pre = jnp.zeros((2 * rows, shards * units), jnp.float32)
    for piece in range(width // tall):
        up = jnp.concatenate(
            [
                weight_ref[shard, :tall, piece * units : (piece + 1) * units]
                for shard in range(shards)
            ],
            axis=1,
        )
        pre = pre + jnp.dot(
            normed[:, piece * tall : (piece + 1) * tall], up, preferred_element_type=jnp.float32
        )
    hidden = (0.5 * pre * (1.0 + lax.erf(pre * (0.5**0.5)))).astype(jnp.bfloat16)
    for piece in range(width // span):
        down = jnp.concatenate(
            [
                weight_ref[shard, tall + piece * units : tall + (piece + 1) * units, :]
                for shard in range(shards)
            ],
            axis=0,
        )
        acc[:, piece * span : (piece + 1) * span] += jnp.dot(
            hidden, down, preferred_element_type=jnp.float32
        )

    @pl.when(step == pl.num_programs(0) - 1)
    def _():
        own_sum[...] = acc[:rows, :]
        other_sum[...] = acc[rows:, :]


def feed_stage(own, other, weights):
    shards, depth, span = weights.shape
    rows, width = own.shape
    group = 2
    flat = pl.BlockSpec((rows, width), lambda s: (0, 0))
    return pl.pallas_call(
        feed_kernel,
        grid=(shards // group,),
        in_specs=[flat, flat, pl.BlockSpec((group, depth, span), lambda s: (s, 0, 0))],
        out_specs=[flat, flat],
        out_shape=[jax.ShapeDtypeStruct((rows, width), jnp.float32)] * 2,
        scratch_shapes=[
            pltpu.VMEM((2 * rows, width), jnp.bfloat16),
            pltpu.VMEM((2 * rows, width), jnp.float32),
        ],
        compiler_params=pltpu.CompilerParams(vmem_limit_bytes=FEED_VMEM),
        name="feed",
    )(own, other, weights)


def half_kernel(core, up_ref, down_ref, out_ref):
    tall = up_ref.shape[0] // 2
    units, width = down_ref.shape
    span = 2 * units
    out_ref[:tall, :units] = up_ref[:tall, :]
    out_ref[:tall, units:] = up_ref[tall:, :]
    for piece in range(width // span):
        out_ref[tall + piece * units : tall + (piece + 1) * units, :] = down_ref[
            :, piece * span : (piece + 1) * span
        ]


def half_weights(w_up, w_down, core):
    width, span = w_up.shape
    units = span // 2
    grid_spec = pltpu.PrefetchScalarGridSpec(
        num_scalar_prefetch=1,
        grid=(1,),
        in_specs=[
            pl.BlockSpec((width, units), lambda s, core: (0, core[0])),
            pl.BlockSpec((units, width), lambda s, core: (core[0], 0)),
        ],
        out_specs=pl.BlockSpec((width, span), lambda s, core: (0, 0)),
    )
    return pl.pallas_call(
        half_kernel,
        grid_spec=grid_spec,
        out_shape=jax.ShapeDtypeStruct((width, span), w_up.dtype),
        name="half_weights",
    )(core.reshape(1), w_up, w_down)


def mix_matrix(edge_proj, heads):
    channel_count, outs = edge_proj.shape
    factors = jnp.where(jnp.arange(outs) < heads, 0.5, 0.25).astype(jnp.bfloat16)
    scaled = (edge_proj * factors[None, :]).T
    eye = jnp.eye(8, dtype=jnp.bfloat16)
    mixed = scaled[:, None, None, :] * eye[None, :, :, None]
    offsets = jnp.sum(scaled.astype(jnp.float32), axis=1)
    return mixed.reshape(outs * 8, 8 * channel_count), offsets


def shift_chip(value, by):
    return lax.ppermute(value, "kcol", [(i, (i + 2 * by) & 7) for i in range(8)])


def after(value, others):
    return lax.optimization_barrier((value, others))[0]


def swap_core(value):
    return lax.ppermute(value, "kcol", [(i, i ^ 1) for i in range(8)])


def local(
    features,
    node_ids,
    token_embed,
    w_query,
    w_key,
    w_value,
    w_out,
    slopes,
    chan_scale,
    chan_shift,
    edge_proj,
    edge_value,
    key_index,
    counts,
    w_up,
    w_down,
):
    node_dev, width = features.shape
    vocab_size = token_embed.shape[0]
    heads = slopes.shape[0]
    head_dim = width // heads
    rows = edge_value.shape[-1]
    col_at = lax.axis_index("kcol")
    core = col_at & 1
    one_hot = (
        node_ids[:, None] == lax.broadcasted_iota(jnp.int32, (node_dev, vocab_size), 1)
    ).astype(jnp.bfloat16)
    embedded = features.astype(jnp.float32) + jnp.dot(
        one_hot, token_embed, preferred_element_type=jnp.float32
    )
    normed = layer_norm(embedded).astype(jnp.bfloat16)

    column_nodes = lax.all_gather(normed, "qrow", axis=0)
    query_own = (
        jnp.einsum("kd,nk->dn", w_query, normed, preferred_element_type=jnp.float32).astype(
            jnp.bfloat16
        )
        * jnp.bfloat16(head_dim ** (-0.5))
    )
    weights = half_weights(w_up, w_down, core)
    queries = [query_own] + [shift_chip(query_own, by) for by in (1, -1, 2)]
    weights = lax.all_gather(after(weights, query_own), "qrow", axis=0)
    lists = list_stage(counts, key_index[:, 0], jnp.stack([col_at >> 1, core]))
    mix, offsets = mix_matrix(edge_proj, heads)
    spread = lambda vector: jnp.broadcast_to((0.5 * vector)[:, None], (vector.shape[0], rows))
    edges = jnp.swapaxes(edge_value.reshape(-1, rows, rows), 1, 2)
    scale, shift = spread(chan_scale), spread(chan_shift)
    *queries, lists, mix, offsets, scale, shift, edges = lax.optimization_barrier(
        (*queries, lists, mix, offsets, scale, shift, edges)
    )
    queries = queries + [swap_core(query) for query in queries]
    bias, gate = edge_stage(after(lists, queries), offsets, edges, mix, scale, shift, heads)
    column_nodes, bias = lax.optimization_barrier((column_nodes, bias))
    parts = []
    for part in range(HEAD_PARTS):
        span = slice(part * width // HEAD_PARTS, (part + 1) * width // HEAD_PARTS)
        keys = jnp.einsum(
            "gnk,kd->gnd", column_nodes, w_key[:, span], preferred_element_type=jnp.float32
        ).astype(jnp.bfloat16)
        values = jnp.einsum(
            "kd,gnk->gdn", w_value[:, span], column_nodes, preferred_element_type=jnp.float32
        ).astype(jnp.bfloat16)
        piece = attend_stage(
            part, HEAD_PARTS, lists, slopes, offsets, edges, bias, gate, keys, values, queries
        )
        column_nodes = after(column_nodes, piece)
        parts.append(lax.all_to_all(after(piece, parts), "kcol", 0, 0, tiled=True))
    weights, parts = lax.optimization_barrier((weights, parts))
    residual, normed_two = join_stage(parts, embedded, w_out)
    own_sum, other_sum = feed_stage(normed_two, swap_core(normed_two), weights)
    return (residual + (own_sum + swap_core(other_sum))).astype(jnp.bfloat16)


def solution(mesh):
    placed = (
        P(("qrow", "kcol"), None),
        P(("qrow", "kcol")),
        P(),
        P(),
        P(),
        P(),
        P(),
        P(),
        P(),
        P(),
        P(),
        P("qrow", "kcol", None, None, None),
        P("qrow", "kcol", None),
        P("qrow", "kcol"),
        P(None, "qrow"),
        P("qrow", None),
    )
    return jax.shard_map(
        local, mesh=mesh, in_specs=placed, out_specs=P(("qrow", "kcol"), None), check_vma=False
    )
```

```python
import functools

import jax
import jax.numpy as jnp
from jax import lax
from jax.experimental import pallas as pl
from jax.experimental.pallas import tpu as pltpu
from jax.sharding import PartitionSpec as P

NEG_FILL = -1e30
HEAD_PARTS = 1
TOP_PIECES = 3
TOTAL_PIECES = 3
EDGE_VMEM = 56 * 1024 * 1024
ATTEND_VMEM = 36 * 1024 * 1024
JOIN_VMEM = 24 * 1024 * 1024
FEED_VMEM = 52 * 1024 * 1024


def layer_norm(values):
    average = jnp.mean(values, axis=-1, keepdims=True)
    centered = values - average
    spread = jnp.mean(centered * centered, axis=-1, keepdims=True)
    return centered * lax.rsqrt(spread + 1e-05)


def list_kernel(counts_ref, index_ref, place_ref, lists_ref):
    block_total, slot_count = index_ref.shape
    total = block_total * slot_count
    chip, core = place_ref[0], place_ref[1]

    def relative(theirs, ours):
        gap = (theirs - ours + 4) & 3
        return jnp.where(gap == 0, 0, jnp.where(gap == 3, 1, gap + 1))

    filled = jnp.int32(0)
    for block in range(block_total):
        count = counts_ref[block, 0]
        partner = jnp.where(core == block % 2, 0, 4) + relative(jnp.int32(block // 2), chip)
        visits = jnp.maximum(count, 1)
        for slot in range(slot_count):

            @pl.when(slot < visits)
            def _(at=filled, block=block, slot=slot, partner=partner, count=count, visits=visits):
                key_block = index_ref[block, slot]
                lists_ref[0, at] = jnp.int32(block * slot_count + slot)
                lists_ref[1, at] = at
                lists_ref[2, at] = jnp.int32(block)
                lists_ref[3, at] = key_block
                lists_ref[4, at] = (slot < count).astype(jnp.int32)
                lists_ref[5, at] = jnp.int32(slot == 0)
                lists_ref[6, at] = (visits == slot + 1).astype(jnp.int32)
                lists_ref[7, at] = partner

            filled = filled + (slot < visits).astype(jnp.int32)

    @pl.loop(0, total)
    def _(step):
        lists_ref[8, step] = filled

        @pl.when(step >= filled)
        def _():
            for row in range(8):
                lists_ref[row, step] = jnp.int32(0)


def list_stage(counts, index, place):
    scalars = pl.BlockSpec(memory_space=pltpu.SMEM)
    return pl.pallas_call(
        list_kernel,
        in_specs=[scalars] * 3,
        out_specs=scalars,
        out_shape=jax.ShapeDtypeStruct((9, index.shape[0] * index.shape[1]), jnp.int32),
        name="lists",
    )(counts, index, place)


def edge_kernel(
    lists,
    offsets,
    edge_ref,
    mix_ref,
    scale_ref,
    shift_ref,
    bias_out,
    gate_out,
    edge_t,
    bias_ref,
    gate_ref,
    sems,
):
    heads = bias_ref.shape[1]
    rows, lanes = edge_t.shape

    steps = lists[8, 0]

    def copies(step, slot):
        return (
            pltpu.make_async_copy(bias_ref.at[slot], bias_out.at[step], sems.at[0, slot]),
            pltpu.make_async_copy(gate_ref.at[slot], gate_out.at[step], sems.at[1, slot]),
        )

    @pl.loop(0, steps)
    def _(step):
        slot = step & 1

        @pl.when(step >= 2)
        def _():
            for copy in copies(step - 2, slot):
                copy.wait()

        edge_t[...] = edge_ref[lists[0, step]].astype(jnp.float32)
        scale = scale_ref[...]
        shift = shift_ref[...]

        def channels(row):
            line = jnp.broadcast_to(edge_t[row : row + 1, :], scale.shape)
            return jnp.tanh((line * scale + shift).astype(jnp.bfloat16))

        def build(part):
            return jnp.concatenate(
                [
                    jnp.concatenate(
                        [channels(part * 16 + half * 8 + within) for within in range(8)], axis=0
                    )
                    for half in range(2)
                ],
                axis=1,
            )

        for part in range(rows // 16):
            terms = jnp.dot(mix_ref[...], build(part), preferred_element_type=jnp.float32)
            span = slice(part * 16, part * 16 + 16)
            for head in range(heads):
                block = terms[head * 8 : head * 8 + 8]
                both = jnp.concatenate([block[:, :lanes], block[:, lanes:]], axis=0)
                bias_ref[slot, head, span, :] = both.astype(jnp.bfloat16)
                block = terms[(heads + head) * 8 : (heads + head) * 8 + 8]
                both = jnp.concatenate([block[:, :lanes], block[:, lanes:]], axis=0)
                gate_ref[slot, head, span, :] = (
                    0.5 + 0.5 * jnp.tanh(both + offsets[heads + head])
                ).astype(jnp.bfloat16)

        for copy in copies(step, slot):
            copy.start()

    @pl.when(steps >= 2)
    def _():
        for copy in copies(steps - 2, steps & 1):
            copy.wait()

    for copy in copies(steps - 1, (steps - 1) & 1):
        copy.wait()


def edge_stage(lists, offsets, edges, mix, scale, shift, heads):
    tiles, rows, lanes = edges.shape
    scalars = pl.BlockSpec(memory_space=pltpu.SMEM)
    held = pl.BlockSpec(memory_space=pltpu.VMEM)
    return pl.pallas_call(
        edge_kernel,
        in_specs=[scalars, scalars, held, held, held, held],
        out_specs=[pl.BlockSpec(memory_space=pl.ANY)] * 2,
        out_shape=[jax.ShapeDtypeStruct((tiles, heads, rows, lanes), jnp.bfloat16)] * 2,
        scratch_shapes=[
            pltpu.VMEM((rows, lanes), jnp.float32),
            pltpu.VMEM((2, heads, rows, lanes), jnp.bfloat16),
            pltpu.VMEM((2, heads, rows, lanes), jnp.bfloat16),
            pltpu.SemaphoreType.DMA((2, 2)),
        ],
        compiler_params=pltpu.CompilerParams(vmem_limit_bytes=EDGE_VMEM),
        cost_estimate=pl.CostEstimate(
            flops=tiles * 2 * rows * lanes * 64 * 256 * 2,
            bytes_accessed=tiles * rows * lanes * heads * 4,
            transcendentals=tiles * rows * lanes * 80,
        ),
        name="edge_terms",
    )(lists, offsets, edges, mix, scale, shift)


def attend_kernel(
    first_head,
    lists,
    slopes,
    offsets,
    edge_ref,
    bias_in,
    gate_in,
    key_ref,
    value_ref,
    *rest,
):
    *query_refs, num_ref, query_pairs, acc, tops, totals, bias_ref, gate_ref, sems = rest
    heads, rows, lanes = bias_ref.shape[1:]
    head_dim = acc.shape[0] // heads
    steps = lists[8, 0]

    def copies(step, slot):
        span = slice(first_head, first_head + heads)
        return (
            pltpu.make_async_copy(bias_in.at[step, span], bias_ref.at[slot], sems.at[0, slot]),
            pltpu.make_async_copy(gate_in.at[step, span], gate_ref.at[slot], sems.at[1, slot]),
        )

    for copy in copies(0, 0):
        copy.start()

    @pl.loop(0, steps)
    def _(step):
        slot = step & 1

        @pl.when(step + 1 < steps)
        def _():
            for copy in copies(step + 1, 1 - slot):
                copy.start()

        for copy in copies(step, slot):
            copy.wait()

        @pl.when(lists[5, step] > 0)
        def _():
            acc[...] = jnp.zeros_like(acc)
            tops[...] = jnp.full_like(tops, NEG_FILL)
            totals[...] = jnp.zeros_like(totals)
            blank = jnp.zeros((head_dim, lanes), jnp.bfloat16)
            for pair in range(heads // 2):
                query_pairs[pair, :head_dim, lanes:] = blank
                query_pairs[pair, head_dim:, :lanes] = blank
            for place, query_ref in enumerate(query_refs):

                @pl.when(lists[7, step] == place)
                def _(query_ref=query_ref):
                    for pair in range(heads // 2):
                        at = (first_head + pair * 2) * head_dim
                        query_pairs[pair, :head_dim, :lanes] = query_ref[at : at + head_dim, :]
                        at += head_dim
                        query_pairs[pair, head_dim:, lanes:] = query_ref[at : at + head_dim, :]

        @pl.when(lists[4, step] > 0)
        def _():
            key_block = lists[3, step]
            edge_t = edge_ref[lists[0, step]].astype(jnp.float32)
            for pair in range(heads // 2):
                width = 2 * head_dim
                keys = key_ref[key_block, :, pair * width : (pair + 1) * width]
                both = jnp.dot(keys, query_pairs[pair], preferred_element_type=jnp.float32)
                for side in range(2):
                    head = pair * 2 + side
                    span = slice(head * head_dim, (head + 1) * head_dim)
                    scores = both[:, side * lanes : (side + 1) * lanes] + (
                        bias_ref[slot, head].astype(jnp.float32) + (
                            edge_t * slopes[first_head + head] + offsets[first_head + head]
                        )
                    )
                    old_top = tops[head : head + 1, :]
                    new_top = jnp.maximum(old_top, jnp.max(scores, axis=0, keepdims=True))
                    factor = jnp.exp(old_top - new_top)
                    weights = jnp.exp(scores - new_top)
                    totals[head : head + 1, :] = totals[head : head + 1, :] * factor + jnp.sum(
                        weights, axis=0, keepdims=True
                    )
                    tops[head : head + 1, :] = new_top
                    gated = (weights * gate_ref[slot, head].astype(jnp.float32)).astype(jnp.bfloat16)
                    part = jnp.dot(
                        value_ref[key_block, span, :], gated, preferred_element_type=jnp.float32
                    )
                    acc[span, :] = acc[span, :] * factor + part

        @pl.when(lists[6, step] > 0)
        def _():
            for head in range(heads):
                span = slice(head * head_dim, (head + 1) * head_dim)
                total = totals[head : head + 1, :]
                inverse = jnp.where(total > 0.0, 1.0 / jnp.where(total > 0.0, total, 1.0), 0.0)
                num_ref[lists[2, step], span, :] = (acc[span, :] * inverse).astype(num_ref.dtype)
            at = acc.shape[0]
            rest = tops[...]
            for _ in range(TOP_PIECES):
                piece = rest.astype(num_ref.dtype)
                num_ref[lists[2, step], at : at + heads, :] = piece
                rest = rest - piece.astype(jnp.float32)
                at += heads
            rest = totals[...]
            for _ in range(TOTAL_PIECES):
                piece = rest.astype(num_ref.dtype)
                num_ref[lists[2, step], at : at + heads, :] = piece
                rest = rest - piece.astype(jnp.float32)
                at += heads


def attend_stage(part, part_count, lists, slopes, offsets, edges, bias, gate, keys, values, queries):
    block_total = len(queries)
    tiles, heads, rows, lanes = bias.shape
    heads //= part_count
    width = queries[0].shape[0] // part_count
    packed = width + heads * (TOP_PIECES + TOTAL_PIECES)
    scalars = pl.BlockSpec(memory_space=pltpu.SMEM)
    held = pl.BlockSpec(memory_space=pltpu.VMEM)
    far = pl.BlockSpec(memory_space=pl.ANY)
    return pl.pallas_call(
        functools.partial(attend_kernel, part * heads),
        in_specs=[scalars] * 3 + [held, far, far] + [held] * (2 + block_total),
        out_specs=held,
        out_shape=jax.ShapeDtypeStruct((block_total, packed, lanes), jnp.bfloat16),
        scratch_shapes=[
            pltpu.VMEM((heads // 2, 2 * width // heads, 2 * lanes), jnp.bfloat16),
            pltpu.VMEM((width, lanes), jnp.float32),
            pltpu.VMEM((heads, lanes), jnp.float32),
            pltpu.VMEM((heads, lanes), jnp.float32),
            pltpu.VMEM((2, heads, rows, lanes), jnp.bfloat16),
            pltpu.VMEM((2, heads, rows, lanes), jnp.bfloat16),
            pltpu.SemaphoreType.DMA((2, 2)),
        ],
        compiler_params=pltpu.CompilerParams(vmem_limit_bytes=ATTEND_VMEM),
        cost_estimate=pl.CostEstimate(
            flops=tiles * 16 * rows * lanes * width,
            bytes_accessed=tiles * rows * lanes * heads * 4,
            transcendentals=tiles * rows * lanes * heads,
        ),
        name="attend",
    )(lists, slopes, offsets, edges, bias, gate, keys, values, *queries)


def join_part(parts_ref, attended):
    width = attended.shape[0]
    count = parts_ref.shape[0]
    heads = (parts_ref.shape[1] - width) // (TOP_PIECES + TOTAL_PIECES)
    head_dim = width // heads

    def rejoin(part, first, pieces):
        whole = jnp.zeros((heads, attended.shape[1]), jnp.float32)
        for piece in range(pieces):
            at = width + (first + piece) * heads
            whole = whole + parts_ref[part, at : at + heads, :].astype(jnp.float32)
        return whole

    tops = [rejoin(part, 0, TOP_PIECES) for part in range(count)]
    top = functools.reduce(jnp.maximum, tops)
    shares = [
        rejoin(part, TOP_PIECES, TOTAL_PIECES) * jnp.exp(tops[part] - top)
        for part in range(count)
    ]
    inverse = 1.0 / functools.reduce(jnp.add, shares)
    shares = [share * inverse for share in shares]
    for head in range(heads):
        span = slice(head * head_dim, (head + 1) * head_dim)
        merged = jnp.zeros((head_dim, attended.shape[1]), jnp.float32)
        for part in range(count):
            merged = merged + parts_ref[part, span, :].astype(jnp.float32) * (
                shares[part][head : head + 1]
            )
        attended[span, :] = merged


def join_kernel(*refs):
    *parts, embedded_ref, out_ref, residual, normed, attended = refs
    width = attended.shape[0] // len(parts)
    for at, parts_ref in enumerate(parts):
        join_part(parts_ref, attended.at[at * width : (at + 1) * width])
    rows = attended[...].T.astype(jnp.bfloat16)
    values = embedded_ref[...] + jnp.dot(
        rows, out_ref[...], preferred_element_type=jnp.float32
    )
    residual[...] = values
    normed[...] = layer_norm(values).astype(jnp.bfloat16)


def join_stage(parts, embedded, w_out):
    rows, width = embedded.shape
    return pl.pallas_call(
        join_kernel,
        out_shape=[
            jax.ShapeDtypeStruct((rows, width), jnp.float32),
            jax.ShapeDtypeStruct((rows, width), jnp.bfloat16),
        ],
        scratch_shapes=[pltpu.VMEM((width, parts[0].shape[2]), jnp.float32)],
        compiler_params=pltpu.CompilerParams(vmem_limit_bytes=JOIN_VMEM),
        name="join",
    )(*parts, embedded, w_out)


def feed_kernel(own_ref, other_ref, weight_in, own_sum, other_sum, normed, acc, weight_ref, sems):
    rows, width = own_ref.shape
    shards, depth, span = weight_ref.shape
    group = shards // sems.shape[0]
    tall = depth // 2
    units = span // 2

    def fetch(step):
        part = pl.ds(step * group, group)
        return pltpu.make_async_copy(weight_in.at[part], weight_ref.at[part], sems.at[step])

    for step in range(shards // group):
        fetch(step).start()
    normed[:rows, :] = own_ref[...]
    normed[rows:, :] = other_ref[...]
    acc[...] = jnp.zeros_like(acc)

    @pl.loop(0, shards // group)
    def _(step):
        fetch(step).wait()
        pre = jnp.zeros((2 * rows, group * units), jnp.float32)
        for piece in range(width // tall):
            up = jnp.concatenate(
                [
                    weight_ref[step * group + at, :tall, piece * units : (piece + 1) * units]
                    for at in range(group)
                ],
                axis=1,
            )
            pre = pre + jnp.dot(
                normed[:, piece * tall : (piece + 1) * tall],
                up,
                preferred_element_type=jnp.float32,
            )
        hidden = (0.5 * pre * (1.0 + lax.erf(pre * (0.5**0.5)))).astype(jnp.bfloat16)
        for piece in range(width // span):
            down = jnp.concatenate(
                [
                    weight_ref[
                        step * group + at, tall + piece * units : tall + (piece + 1) * units, :
                    ]
                    for at in range(group)
                ],
                axis=0,
            )
            acc[:, piece * span : (piece + 1) * span] += jnp.dot(
                hidden, down, preferred_element_type=jnp.float32
            )

    own_sum[...] = acc[:rows, :]
    other_sum[...] = acc[rows:, :]


def feed_stage(own, other, weights):
    shards = weights.shape[0]
    rows, width = own.shape
    group = 2
    held = pl.BlockSpec(memory_space=pltpu.VMEM)
    return pl.pallas_call(
        feed_kernel,
        in_specs=[held, held, pl.BlockSpec(memory_space=pl.ANY)],
        out_specs=[held, held],
        out_shape=[jax.ShapeDtypeStruct((rows, width), jnp.float32)] * 2,
        scratch_shapes=[
            pltpu.VMEM((2 * rows, width), jnp.bfloat16),
            pltpu.VMEM((2 * rows, width), jnp.float32),
            pltpu.VMEM(weights.shape, weights.dtype),
            pltpu.SemaphoreType.DMA((shards // group,)),
        ],
        compiler_params=pltpu.CompilerParams(vmem_limit_bytes=FEED_VMEM),
        name="feed",
    )(own, other, weights)


def half_kernel(core, up_ref, down_ref, out_ref):
    tall = up_ref.shape[0] // 2
    units, width = down_ref.shape
    span = 2 * units
    out_ref[:tall, :units] = up_ref[:tall, :]
    out_ref[:tall, units:] = up_ref[tall:, :]
    for piece in range(width // span):
        out_ref[tall + piece * units : tall + (piece + 1) * units, :] = down_ref[
            :, piece * span : (piece + 1) * span
        ]


def half_weights(w_up, w_down, core):
    width, span = w_up.shape
    units = span // 2
    grid_spec = pltpu.PrefetchScalarGridSpec(
        num_scalar_prefetch=1,
        grid=(1,),
        in_specs=[
            pl.BlockSpec((width, units), lambda s, core: (0, core[0])),
            pl.BlockSpec((units, width), lambda s, core: (core[0], 0)),
        ],
        out_specs=pl.BlockSpec((width, span), lambda s, core: (0, 0)),
    )
    return pl.pallas_call(
        half_kernel,
        grid_spec=grid_spec,
        out_shape=jax.ShapeDtypeStruct((width, span), w_up.dtype),
        name="half_weights",
    )(core.reshape(1), w_up, w_down)


def mix_matrix(edge_proj, heads):
    channel_count, outs = edge_proj.shape
    factors = jnp.where(jnp.arange(outs) < heads, 0.5, 0.25).astype(jnp.bfloat16)
    scaled = (edge_proj * factors[None, :]).T
    eye = jnp.eye(8, dtype=jnp.bfloat16)
    mixed = scaled[:, None, None, :] * eye[None, :, :, None]
    offsets = jnp.sum(scaled.astype(jnp.float32), axis=1)
    return mixed.reshape(outs * 8, 8 * channel_count), offsets


def shift_chip(value, by):
    return lax.ppermute(value, "kcol", [(i, (i + 2 * by) & 7) for i in range(8)])


def after(value, others):
    return lax.optimization_barrier((value, others))[0]


def swap_core(value):
    return lax.ppermute(value, "kcol", [(i, i ^ 1) for i in range(8)])


def local(
    features,
    node_ids,
    token_embed,
    w_query,
    w_key,
    w_value,
    w_out,
    slopes,
    chan_scale,
    chan_shift,
    edge_proj,
    edge_value,
    key_index,
    counts,
    w_up,
    w_down,
):
    node_dev, width = features.shape
    vocab_size = token_embed.shape[0]
    heads = slopes.shape[0]
    head_dim = width // heads
    rows = edge_value.shape[-1]
    col_at = lax.axis_index("kcol")
    core = col_at & 1
    one_hot = (
        node_ids[:, None] == lax.broadcasted_iota(jnp.int32, (node_dev, vocab_size), 1)
    ).astype(jnp.bfloat16)
    embedded = features.astype(jnp.float32) + jnp.dot(
        one_hot, token_embed, preferred_element_type=jnp.float32
    )
    normed = layer_norm(embedded).astype(jnp.bfloat16)

    column_nodes = lax.all_gather(normed, "qrow", axis=0)
    query_own = (
        jnp.einsum("kd,nk->dn", w_query, normed, preferred_element_type=jnp.float32).astype(
            jnp.bfloat16
        )
        * jnp.bfloat16(head_dim ** (-0.5))
    )
    weights = half_weights(w_up, w_down, core)
    queries = [query_own] + [shift_chip(query_own, by) for by in (1, -1, 2)]
    weights = lax.all_gather(after(weights, query_own), "qrow", axis=0)
    lists = list_stage(counts, key_index[:, 0], jnp.stack([col_at >> 1, core]))
    mix, offsets = mix_matrix(edge_proj, heads)
    spread = lambda vector: jnp.broadcast_to((0.5 * vector)[:, None], (vector.shape[0], rows))
    edges = jnp.swapaxes(edge_value.reshape(-1, rows, rows), 1, 2)
    scale, shift = spread(chan_scale), spread(chan_shift)
    *queries, lists, mix, offsets, scale, shift, edges = lax.optimization_barrier(
        (*queries, lists, mix, offsets, scale, shift, edges)
    )
    queries = queries + [swap_core(query) for query in queries]
    bias, gate = edge_stage(after(lists, queries), offsets, edges, mix, scale, shift, heads)
    column_nodes, bias = lax.optimization_barrier((column_nodes, bias))
    parts = []
    for part in range(HEAD_PARTS):
        span = slice(part * width // HEAD_PARTS, (part + 1) * width // HEAD_PARTS)
        keys = jnp.einsum(
            "gnk,kd->gnd", column_nodes, w_key[:, span], preferred_element_type=jnp.float32
        ).astype(jnp.bfloat16)
        values = jnp.einsum(
            "kd,gnk->gdn", w_value[:, span], column_nodes, preferred_element_type=jnp.float32
        ).astype(jnp.bfloat16)
        piece = attend_stage(
            part, HEAD_PARTS, lists, slopes, offsets, edges, bias, gate, keys, values, queries
        )
        column_nodes = after(column_nodes, piece)
        parts.append(lax.all_to_all(after(piece, parts), "kcol", 0, 0, tiled=True))
    weights, parts = lax.optimization_barrier((weights, parts))
    residual, normed_two = join_stage(parts, embedded, w_out)
    own_sum, other_sum = feed_stage(normed_two, swap_core(normed_two), weights)
    return (residual + (own_sum + swap_core(other_sum))).astype(jnp.bfloat16)


def solution(mesh):
    placed = (
        P(("qrow", "kcol"), None),
        P(("qrow", "kcol")),
        P(),
        P(),
        P(),
        P(),
        P(),
        P(),
        P(),
        P(),
        P(),
        P("qrow", "kcol", None, None, None),
        P("qrow", "kcol", None),
        P("qrow", "kcol"),
        P(None, "qrow"),
        P("qrow", None),
    )
    return jax.shard_map(
        local, mesh=mesh, in_specs=placed, out_specs=P(("qrow", "kcol"), None), check_vma=False
    )
```

```python
import functools

import jax
import jax.numpy as jnp
from jax import lax
from jax.experimental import pallas as pl
from jax.experimental.pallas import tpu as pltpu
from jax.sharding import PartitionSpec as P

NEG_FILL = -1e30
HEAD_PARTS = 1
TOP_PIECES = 3
TOTAL_PIECES = 3
EDGE_VMEM = 56 * 1024 * 1024
ATTEND_VMEM = 36 * 1024 * 1024
JOIN_VMEM = 24 * 1024 * 1024
FEED_VMEM = 52 * 1024 * 1024


def layer_norm(values):
    average = jnp.mean(values, axis=-1, keepdims=True)
    centered = values - average
    spread = jnp.mean(centered * centered, axis=-1, keepdims=True)
    return centered * lax.rsqrt(spread + 1e-05)


def list_kernel(counts_ref, index_ref, place_ref, tiles_ref, pairs_ref):
    block_total, slot_count = index_ref.shape
    chip, core = place_ref[0], place_ref[1]
    filled = jnp.int32(0)
    paired = jnp.int32(0)
    for block in range(block_total):
        count = counts_ref[block, 0]
        gap = (jnp.int32(block // 2) - chip + 4) & 3
        partner = jnp.where(core == block % 2, 0, 4) + jnp.where(
            gap == 0, 0, jnp.where(gap == 3, 1, gap + 1)
        )
        visits = jnp.maximum(count, 1)
        for slot in range(slot_count):

            @pl.when(slot < visits)
            def _(at=filled + slot, tile=block * slot_count + slot):
                tiles_ref[0, at] = jnp.int32(tile)

        for pair in range(slot_count // 2):
            slot = 2 * pair

            @pl.when(slot < visits)
            def _(
                step=paired + pair,
                at=filled + slot,
                block=block,
                slot=slot,
                partner=partner,
                count=count,
                visits=visits,
            ):
                pairs_ref[0, step] = jnp.int32(block)
                pairs_ref[1, step] = partner
                pairs_ref[2, step] = jnp.int32(block * slot_count + slot)
                pairs_ref[3, step] = at
                pairs_ref[4, step] = index_ref[block, slot]
                pairs_ref[5, step] = index_ref[block, slot + 1]
                pairs_ref[6, step] = (slot < count).astype(jnp.int32)
                pairs_ref[7, step] = (slot + 1 < count).astype(jnp.int32)
                pairs_ref[8, step] = jnp.int32(slot == 0)
                pairs_ref[9, step] = (slot + 2 >= visits).astype(jnp.int32)

        filled = filled + visits
        paired = paired + ((visits + 1) >> 1)
    tiles_ref[1, 0] = filled
    pairs_ref[10, 0] = paired


def list_stage(counts, index, place):
    scalars = pl.BlockSpec(memory_space=pltpu.SMEM)
    total = index.shape[0] * index.shape[1]
    return pl.pallas_call(
        list_kernel,
        in_specs=[scalars] * 3,
        out_specs=[scalars] * 2,
        out_shape=[
            jax.ShapeDtypeStruct((2, total), jnp.int32),
            jax.ShapeDtypeStruct((11, total // 2), jnp.int32),
        ],
        name="lists",
    )(counts, index, place)


def edge_kernel(
    lists,
    offsets,
    edge_ref,
    mix_ref,
    scale_ref,
    shift_ref,
    bias_out,
    gate_out,
    edge_t,
    bias_ref,
    gate_ref,
    sems,
):
    heads = bias_ref.shape[1]
    rows, lanes = edge_t.shape

    steps = lists[1, 0]

    def copies(step, slot):
        return (
            pltpu.make_async_copy(bias_ref.at[slot], bias_out.at[step], sems.at[0, slot]),
            pltpu.make_async_copy(gate_ref.at[slot], gate_out.at[step], sems.at[1, slot]),
        )

    @pl.loop(0, steps)
    def _(step):
        slot = step & 1

        @pl.when(step >= 2)
        def _():
            for copy in copies(step - 2, slot):
                copy.wait()

        edge_t[...] = edge_ref[lists[0, step]].astype(jnp.float32)
        scale = scale_ref[...]
        shift = shift_ref[...]

        def channels(row):
            line = jnp.broadcast_to(edge_t[row : row + 1, :], scale.shape)
            return jnp.tanh((line * scale + shift).astype(jnp.bfloat16))

        def build(part):
            return jnp.concatenate(
                [
                    jnp.concatenate(
                        [channels(part * 16 + half * 8 + within) for within in range(8)], axis=0
                    )
                    for half in range(2)
                ],
                axis=1,
            )

        for part in range(rows // 16):
            terms = jnp.dot(mix_ref[...], build(part), preferred_element_type=jnp.float32)
            span = slice(part * 16, part * 16 + 16)
            for head in range(heads):
                block = terms[head * 8 : head * 8 + 8]
                both = jnp.concatenate([block[:, :lanes], block[:, lanes:]], axis=0)
                bias_ref[slot, head, span, :] = both.astype(jnp.bfloat16)
                block = terms[(heads + head) * 8 : (heads + head) * 8 + 8]
                both = jnp.concatenate([block[:, :lanes], block[:, lanes:]], axis=0)
                gate_ref[slot, head, span, :] = (
                    0.5 + 0.5 * jnp.tanh(both + offsets[heads + head])
                ).astype(jnp.bfloat16)

        for copy in copies(step, slot):
            copy.start()

    @pl.when(steps >= 2)
    def _():
        for copy in copies(steps - 2, steps & 1):
            copy.wait()

    for copy in copies(steps - 1, (steps - 1) & 1):
        copy.wait()


def edge_stage(lists, offsets, edges, mix, scale, shift, heads):
    tiles, rows, lanes = edges.shape
    scalars = pl.BlockSpec(memory_space=pltpu.SMEM)
    held = pl.BlockSpec(memory_space=pltpu.VMEM)
    return pl.pallas_call(
        edge_kernel,
        in_specs=[scalars, scalars, held, held, held, held],
        out_specs=[pl.BlockSpec(memory_space=pl.ANY)] * 2,
        out_shape=[jax.ShapeDtypeStruct((tiles, heads, rows, lanes), jnp.bfloat16)] * 2,
        scratch_shapes=[
            pltpu.VMEM((rows, lanes), jnp.float32),
            pltpu.VMEM((2, heads, rows, lanes), jnp.bfloat16),
            pltpu.VMEM((2, heads, rows, lanes), jnp.bfloat16),
            pltpu.SemaphoreType.DMA((2, 2)),
        ],
        compiler_params=pltpu.CompilerParams(vmem_limit_bytes=EDGE_VMEM),
        cost_estimate=pl.CostEstimate(
            flops=tiles * 2 * rows * lanes * 64 * 256 * 2,
            bytes_accessed=tiles * rows * lanes * heads * 4,
            transcendentals=tiles * rows * lanes * 80,
        ),
        name="edge_terms",
    )(lists, offsets, edges, mix, scale, shift)


def attend_kernel(
    first_head,
    pairs,
    slopes,
    offsets,
    edge_ref,
    bias_in,
    gate_in,
    key_ref,
    value_ref,
    *rest,
):
    *query_refs, num_ref, query_pairs, acc, tops, totals, bias_ref, gate_ref, sems = rest
    heads, rows, lanes = bias_ref.shape[2:]
    head_dim = acc.shape[0] // heads
    steps = pairs[10, 0]

    def copies(step, slot, side):
        span = slice(first_head, first_head + heads)
        at = pairs[3, step] + side
        return (
            pltpu.make_async_copy(
                bias_in.at[at, span], bias_ref.at[slot, side], sems.at[0, slot, side]
            ),
            pltpu.make_async_copy(
                gate_in.at[at, span], gate_ref.at[slot, side], sems.at[1, slot, side]
            ),
        )

    def fetch(step, slot):
        for copy in copies(step, slot, 0):
            copy.start()

        @pl.when(pairs[7, step] > 0)
        def _():
            for copy in copies(step, slot, 1):
                copy.start()

    fetch(0, 0)

    @pl.loop(0, steps)
    def _(step):
        slot = step & 1

        @pl.when(step + 1 < steps)
        def _():
            fetch(step + 1, 1 - slot)

        for copy in copies(step, slot, 0):
            copy.wait()

        @pl.when(pairs[7, step] > 0)
        def _():
            for copy in copies(step, slot, 1):
                copy.wait()

        @pl.when(pairs[8, step] > 0)
        def _():
            acc[...] = jnp.zeros_like(acc)
            tops[...] = jnp.full_like(tops, NEG_FILL)
            totals[...] = jnp.zeros_like(totals)
            blank = jnp.zeros((head_dim, lanes), jnp.bfloat16)
            for pair in range(heads // 2):
                query_pairs[pair, :head_dim, lanes:] = blank
                query_pairs[pair, head_dim:, :lanes] = blank
            for place, query_ref in enumerate(query_refs):

                @pl.when(pairs[1, step] == place)
                def _(query_ref=query_ref):
                    for pair in range(heads // 2):
                        at = (first_head + pair * 2) * head_dim
                        query_pairs[pair, :head_dim, :lanes] = query_ref[at : at + head_dim, :]
                        at += head_dim
                        query_pairs[pair, head_dim:, lanes:] = query_ref[at : at + head_dim, :]

        @pl.when(pairs[6, step] > 0)
        def _():
            tile = pairs[2, step]
            key_blocks = (pairs[4, step], pairs[5, step])
            second = pairs[7, step]
            penalty = jnp.where(second > 0, 0.0, NEG_FILL)
            sides = ((0, 0.0), (second, penalty))
            for pair in range(heads // 2):
                width = 2 * head_dim
                keys = jnp.concatenate(
                    [key_ref[block, :, pair * width : (pair + 1) * width] for block in key_blocks],
                    axis=0,
                )
                both = jnp.dot(keys, query_pairs[pair], preferred_element_type=jnp.float32)
                for half in range(2):
                    head = pair * 2 + half
                    span = slice(head * head_dim, (head + 1) * head_dim)
                    slope = slopes[first_head + head]
                    offset = offsets[first_head + head]
                    scores = [
                        both[at * rows : (at + 1) * rows, half * lanes : (half + 1) * lanes]
                        + (
                            bias_ref[slot, side, head].astype(jnp.float32)
                            + (edge_ref[tile + at].astype(jnp.float32) * slope + (offset + mask))
                        )
                        for at, (side, mask) in enumerate(sides)
                    ]
                    old_top = tops[head : head + 1, :]
                    new_top = jnp.maximum(
                        old_top, jnp.max(jnp.maximum(*scores), axis=0, keepdims=True)
                    )
                    factor = jnp.exp(old_top - new_top)
                    weights = [jnp.exp(score - new_top) for score in scores]
                    totals[head : head + 1, :] = totals[head : head + 1, :] * factor + jnp.sum(
                        weights[0] + weights[1], axis=0, keepdims=True
                    )
                    tops[head : head + 1, :] = new_top
                    gated = jnp.concatenate(
                        [
                            (weight * gate_ref[slot, side, head].astype(jnp.float32)).astype(
                                jnp.bfloat16
                            )
                            for weight, (side, _) in zip(weights, sides)
                        ],
                        axis=0,
                    )
                    values = jnp.concatenate(
                        [value_ref[block, span, :] for block in key_blocks], axis=1
                    )
                    part = jnp.dot(values, gated, preferred_element_type=jnp.float32)
                    acc[span, :] = acc[span, :] * factor + part

        @pl.when(pairs[9, step] > 0)
        def _():
            for head in range(heads):
                span = slice(head * head_dim, (head + 1) * head_dim)
                total = totals[head : head + 1, :]
                inverse = jnp.where(total > 0.0, 1.0 / jnp.where(total > 0.0, total, 1.0), 0.0)
                num_ref[pairs[0, step], span, :] = (acc[span, :] * inverse).astype(num_ref.dtype)
            at = acc.shape[0]
            rest = tops[...]
            for _ in range(TOP_PIECES):
                piece = rest.astype(num_ref.dtype)
                num_ref[pairs[0, step], at : at + heads, :] = piece
                rest = rest - piece.astype(jnp.float32)
                at += heads
            rest = totals[...]
            for _ in range(TOTAL_PIECES):
                piece = rest.astype(num_ref.dtype)
                num_ref[pairs[0, step], at : at + heads, :] = piece
                rest = rest - piece.astype(jnp.float32)
                at += heads


def attend_stage(part, part_count, pairs, slopes, offsets, edges, bias, gate, keys, values, queries):
    block_total = len(queries)
    tiles, heads, rows, lanes = bias.shape
    heads //= part_count
    width = queries[0].shape[0] // part_count
    packed = width + heads * (TOP_PIECES + TOTAL_PIECES)
    scalars = pl.BlockSpec(memory_space=pltpu.SMEM)
    held = pl.BlockSpec(memory_space=pltpu.VMEM)
    far = pl.BlockSpec(memory_space=pl.ANY)
    return pl.pallas_call(
        functools.partial(attend_kernel, part * heads),
        in_specs=[scalars] * 3 + [held, far, far] + [held] * (2 + block_total),
        out_specs=held,
        out_shape=jax.ShapeDtypeStruct((block_total, packed, lanes), jnp.bfloat16),
        scratch_shapes=[
            pltpu.VMEM((heads // 2, 2 * width // heads, 2 * lanes), jnp.bfloat16),
            pltpu.VMEM((width, lanes), jnp.float32),
            pltpu.VMEM((heads, lanes), jnp.float32),
            pltpu.VMEM((heads, lanes), jnp.float32),
            pltpu.VMEM((2, 2, heads, rows, lanes), jnp.bfloat16),
            pltpu.VMEM((2, 2, heads, rows, lanes), jnp.bfloat16),
            pltpu.SemaphoreType.DMA((2, 2, 2)),
        ],
        compiler_params=pltpu.CompilerParams(vmem_limit_bytes=ATTEND_VMEM),
        cost_estimate=pl.CostEstimate(
            flops=tiles * 16 * rows * lanes * width,
            bytes_accessed=tiles * rows * lanes * heads * 4,
            transcendentals=tiles * rows * lanes * heads,
        ),
        name="attend",
    )(pairs, slopes, offsets, edges, bias, gate, keys, values, *queries)


def join_part(parts_ref, attended):
    width = attended.shape[0]
    count = parts_ref.shape[0]
    heads = (parts_ref.shape[1] - width) // (TOP_PIECES + TOTAL_PIECES)
    head_dim = width // heads

    def rejoin(part, first, pieces):
        whole = jnp.zeros((heads, attended.shape[1]), jnp.float32)
        for piece in range(pieces):
            at = width + (first + piece) * heads
            whole = whole + parts_ref[part, at : at + heads, :].astype(jnp.float32)
        return whole

    tops = [rejoin(part, 0, TOP_PIECES) for part in range(count)]
    top = functools.reduce(jnp.maximum, tops)
    shares = [
        rejoin(part, TOP_PIECES, TOTAL_PIECES) * jnp.exp(tops[part] - top)
        for part in range(count)
    ]
    inverse = 1.0 / functools.reduce(jnp.add, shares)
    shares = [share * inverse for share in shares]
    for head in range(heads):
        span = slice(head * head_dim, (head + 1) * head_dim)
        merged = jnp.zeros((head_dim, attended.shape[1]), jnp.float32)
        for part in range(count):
            merged = merged + parts_ref[part, span, :].astype(jnp.float32) * (
                shares[part][head : head + 1]
            )
        attended[span, :] = merged


def join_kernel(*refs):
    *parts, embedded_ref, out_ref, residual, normed, attended = refs
    width = attended.shape[0] // len(parts)
    for at, parts_ref in enumerate(parts):
        join_part(parts_ref, attended.at[at * width : (at + 1) * width])
    rows = attended[...].T.astype(jnp.bfloat16)
    values = embedded_ref[...] + jnp.dot(
        rows, out_ref[...], preferred_element_type=jnp.float32
    )
    residual[...] = values
    normed[...] = layer_norm(values).astype(jnp.bfloat16)


def join_stage(parts, embedded, w_out):
    rows, width = embedded.shape
    return pl.pallas_call(
        join_kernel,
        out_shape=[
            jax.ShapeDtypeStruct((rows, width), jnp.float32),
            jax.ShapeDtypeStruct((rows, width), jnp.bfloat16),
        ],
        scratch_shapes=[pltpu.VMEM((width, parts[0].shape[2]), jnp.float32)],
        compiler_params=pltpu.CompilerParams(vmem_limit_bytes=JOIN_VMEM),
        name="join",
    )(*parts, embedded, w_out)


def feed_kernel(own_ref, other_ref, weight_in, own_sum, other_sum, normed, acc, weight_ref, sems):
    rows, width = own_ref.shape
    shards, depth, span = weight_ref.shape
    group = shards // sems.shape[0]
    tall = depth // 2
    units = span // 2

    def fetch(step):
        part = pl.ds(step * group, group)
        return pltpu.make_async_copy(weight_in.at[part], weight_ref.at[part], sems.at[step])

    for step in range(shards // group):
        fetch(step).start()
    normed[:rows, :] = own_ref[...]
    normed[rows:, :] = other_ref[...]
    acc[...] = jnp.zeros_like(acc)

    @pl.loop(0, shards // group)
    def _(step):
        fetch(step).wait()
        pre = jnp.zeros((2 * rows, group * units), jnp.float32)
        for piece in range(width // tall):
            up = jnp.concatenate(
                [
                    weight_ref[step * group + at, :tall, piece * units : (piece + 1) * units]
                    for at in range(group)
                ],
                axis=1,
            )
            pre = pre + jnp.dot(
                normed[:, piece * tall : (piece + 1) * tall],
                up,
                preferred_element_type=jnp.float32,
            )
        hidden = (0.5 * pre * (1.0 + lax.erf(pre * (0.5**0.5)))).astype(jnp.bfloat16)
        for piece in range(width // span):
            down = jnp.concatenate(
                [
                    weight_ref[
                        step * group + at, tall + piece * units : tall + (piece + 1) * units, :
                    ]
                    for at in range(group)
                ],
                axis=0,
            )
            acc[:, piece * span : (piece + 1) * span] += jnp.dot(
                hidden, down, preferred_element_type=jnp.float32
            )

    own_sum[...] = acc[:rows, :]
    other_sum[...] = acc[rows:, :]


def feed_stage(own, other, weights):
    shards = weights.shape[0]
    rows, width = own.shape
    group = 2
    held = pl.BlockSpec(memory_space=pltpu.VMEM)
    return pl.pallas_call(
        feed_kernel,
        in_specs=[held, held, pl.BlockSpec(memory_space=pl.ANY)],
        out_specs=[held, held],
        out_shape=[jax.ShapeDtypeStruct((rows, width), jnp.float32)] * 2,
        scratch_shapes=[
            pltpu.VMEM((2 * rows, width), jnp.bfloat16),
            pltpu.VMEM((2 * rows, width), jnp.float32),
            pltpu.VMEM(weights.shape, weights.dtype),
            pltpu.SemaphoreType.DMA((shards // group,)),
        ],
        compiler_params=pltpu.CompilerParams(vmem_limit_bytes=FEED_VMEM),
        name="feed",
    )(own, other, weights)


def half_kernel(core, up_ref, down_ref, out_ref):
    tall = up_ref.shape[0] // 2
    units, width = down_ref.shape
    span = 2 * units
    out_ref[:tall, :units] = up_ref[:tall, :]
    out_ref[:tall, units:] = up_ref[tall:, :]
    for piece in range(width // span):
        out_ref[tall + piece * units : tall + (piece + 1) * units, :] = down_ref[
            :, piece * span : (piece + 1) * span
        ]


def half_weights(w_up, w_down, core):
    width, span = w_up.shape
    units = span // 2
    grid_spec = pltpu.PrefetchScalarGridSpec(
        num_scalar_prefetch=1,
        grid=(1,),
        in_specs=[
            pl.BlockSpec((width, units), lambda s, core: (0, core[0])),
            pl.BlockSpec((units, width), lambda s, core: (core[0], 0)),
        ],
        out_specs=pl.BlockSpec((width, span), lambda s, core: (0, 0)),
    )
    return pl.pallas_call(
        half_kernel,
        grid_spec=grid_spec,
        out_shape=jax.ShapeDtypeStruct((width, span), w_up.dtype),
        name="half_weights",
    )(core.reshape(1), w_up, w_down)


def mix_matrix(edge_proj, heads):
    channel_count, outs = edge_proj.shape
    factors = jnp.where(jnp.arange(outs) < heads, 0.5, 0.25).astype(jnp.bfloat16)
    scaled = (edge_proj * factors[None, :]).T
    eye = jnp.eye(8, dtype=jnp.bfloat16)
    mixed = scaled[:, None, None, :] * eye[None, :, :, None]
    offsets = jnp.sum(scaled.astype(jnp.float32), axis=1)
    return mixed.reshape(outs * 8, 8 * channel_count), offsets


def shift_chip(value, by):
    return lax.ppermute(value, "kcol", [(i, (i + 2 * by) & 7) for i in range(8)])


def after(value, others):
    return lax.optimization_barrier((value, others))[0]


def swap_core(value):
    return lax.ppermute(value, "kcol", [(i, i ^ 1) for i in range(8)])


def local(
    features,
    node_ids,
    token_embed,
    w_query,
    w_key,
    w_value,
    w_out,
    slopes,
    chan_scale,
    chan_shift,
    edge_proj,
    edge_value,
    key_index,
    counts,
    w_up,
    w_down,
):
    node_dev, width = features.shape
    vocab_size = token_embed.shape[0]
    heads = slopes.shape[0]
    head_dim = width // heads
    rows = edge_value.shape[-1]
    col_at = lax.axis_index("kcol")
    core = col_at & 1
    one_hot = (
        node_ids[:, None] == lax.broadcasted_iota(jnp.int32, (node_dev, vocab_size), 1)
    ).astype(jnp.bfloat16)
    embedded = features.astype(jnp.float32) + jnp.dot(
        one_hot, token_embed, preferred_element_type=jnp.float32
    )
    normed = layer_norm(embedded).astype(jnp.bfloat16)

    column_nodes = lax.all_gather(normed, "qrow", axis=0)
    query_own = (
        jnp.einsum("kd,nk->dn", w_query, normed, preferred_element_type=jnp.float32).astype(
            jnp.bfloat16
        )
        * jnp.bfloat16(head_dim ** (-0.5))
    )
    weights = half_weights(w_up, w_down, core)
    queries = [query_own] + [shift_chip(query_own, by) for by in (1, -1, 2)]
    weights = lax.all_gather(after(weights, query_own), "qrow", axis=0)
    lists, pairs = list_stage(counts, key_index[:, 0], jnp.stack([col_at >> 1, core]))
    mix, offsets = mix_matrix(edge_proj, heads)
    spread = lambda vector: jnp.broadcast_to((0.5 * vector)[:, None], (vector.shape[0], rows))
    edges = jnp.swapaxes(edge_value.reshape(-1, rows, rows), 1, 2)
    scale, shift = spread(chan_scale), spread(chan_shift)
    *queries, lists, mix, offsets, scale, shift, edges = lax.optimization_barrier(
        (*queries, lists, mix, offsets, scale, shift, edges)
    )
    queries = queries + [swap_core(query) for query in queries]
    bias, gate = edge_stage(after(lists, queries), offsets, edges, mix, scale, shift, heads)
    column_nodes, bias = lax.optimization_barrier((column_nodes, bias))
    parts = []
    for part in range(HEAD_PARTS):
        span = slice(part * width // HEAD_PARTS, (part + 1) * width // HEAD_PARTS)
        keys = jnp.einsum(
            "gnk,kd->gnd", column_nodes, w_key[:, span], preferred_element_type=jnp.float32
        ).astype(jnp.bfloat16)
        values = jnp.einsum(
            "kd,gnk->gdn", w_value[:, span], column_nodes, preferred_element_type=jnp.float32
        ).astype(jnp.bfloat16)
        piece = attend_stage(
            part, HEAD_PARTS, pairs, slopes, offsets, edges, bias, gate, keys, values, queries
        )
        column_nodes = after(column_nodes, piece)
        parts.append(lax.all_to_all(after(piece, parts), "kcol", 0, 0, tiled=True))
    residual, normed_two = join_stage(parts, embedded, w_out)
    normed_other = swap_core(normed_two)
    weights, normed_other = lax.optimization_barrier((weights, normed_other))
    own_sum, other_sum = feed_stage(normed_two, normed_other, weights)
    return (residual + (own_sum + swap_core(other_sum))).astype(jnp.bfloat16)


def solution(mesh):
    placed = (
        P(("qrow", "kcol"), None),
        P(("qrow", "kcol")),
        P(),
        P(),
        P(),
        P(),
        P(),
        P(),
        P(),
        P(),
        P(),
        P("qrow", "kcol", None, None, None),
        P("qrow", "kcol", None),
        P("qrow", "kcol"),
        P(None, "qrow"),
        P("qrow", None),
    )
    return jax.shard_map(
        local, mesh=mesh, in_specs=placed, out_specs=P(("qrow", "kcol"), None), check_vma=False
    )
```

```python
import functools

import jax
import jax.numpy as jnp
from jax import lax
from jax.experimental import pallas as pl
from jax.experimental.pallas import tpu as pltpu
from jax.sharding import PartitionSpec as P

NEG_FILL = -1e30
HEAD_PARTS = 1
TOP_PIECES = 3
TOTAL_PIECES = 3
EDGE_VMEM = 56 * 1024 * 1024
ATTEND_VMEM = 36 * 1024 * 1024
JOIN_VMEM = 24 * 1024 * 1024
FEED_VMEM = 52 * 1024 * 1024


def layer_norm(values):
    average = jnp.mean(values, axis=-1, keepdims=True)
    centered = values - average
    spread = jnp.mean(centered * centered, axis=-1, keepdims=True)
    return centered * lax.rsqrt(spread + 1e-05)


def list_kernel(counts_ref, index_ref, place_ref, lists_ref):
    block_total, slot_count = index_ref.shape
    total = block_total * slot_count
    chip, core = place_ref[0], place_ref[1]

    def relative(theirs, ours):
        gap = (theirs - ours + 4) & 3
        return jnp.where(gap == 0, 0, jnp.where(gap == 3, 1, gap + 1))

    filled = jnp.int32(0)
    for block in range(block_total):
        count = counts_ref[block, 0]
        partner = jnp.where(core == block % 2, 0, 4) + relative(jnp.int32(block // 2), chip)
        visits = jnp.maximum(count, 1)
        for slot in range(slot_count):

            @pl.when(slot < visits)
            def _(at=filled, block=block, slot=slot, partner=partner, count=count, visits=visits):
                key_block = index_ref[block, slot]
                lists_ref[0, at] = jnp.int32(block * slot_count + slot)
                lists_ref[1, at] = at
                lists_ref[2, at] = jnp.int32(block)
                lists_ref[3, at] = key_block
                lists_ref[4, at] = (slot < count).astype(jnp.int32)
                lists_ref[5, at] = jnp.int32(slot == 0)
                lists_ref[6, at] = (visits == slot + 1).astype(jnp.int32)
                lists_ref[7, at] = partner

            filled = filled + (slot < visits).astype(jnp.int32)

    @pl.loop(0, total)
    def _(step):
        lists_ref[8, step] = filled

        @pl.when(step >= filled)
        def _():
            for row in range(8):
                lists_ref[row, step] = jnp.int32(0)


def list_stage(counts, index, place):
    scalars = pl.BlockSpec(memory_space=pltpu.SMEM)
    return pl.pallas_call(
        list_kernel,
        in_specs=[scalars] * 3,
        out_specs=scalars,
        out_shape=jax.ShapeDtypeStruct((9, index.shape[0] * index.shape[1]), jnp.int32),
        name="lists",
    )(counts, index, place)


def edge_kernel(
    lists,
    offsets,
    edge_ref,
    proj_ref,
    scale_ref,
    shift_ref,
    bias_out,
    gate_out,
    edge_t,
    bias_ref,
    gate_ref,
    mix_ref,
    sems,
):
    heads = bias_ref.shape[1]
    rows, lanes = edge_t.shape

    steps = lists[8, 0]

    outs, columns = proj_ref.shape
    spread = jnp.broadcast_to(proj_ref[...][:, None, :], (outs, 8, columns)).reshape(
        8 * outs, columns
    )
    node = lax.broadcasted_iota(jnp.int32, spread.shape, 0) & 7
    second = (lax.broadcasted_iota(jnp.int32, spread.shape, 1) >= columns // 2).astype(jnp.int32)
    for piece in range(4):
        mix_ref[:, piece * columns : (piece + 1) * columns] = jnp.where(
            node == 2 * piece + second, spread, 0.0
        ).astype(jnp.bfloat16)

    def copies(step, slot):
        return (
            pltpu.make_async_copy(bias_ref.at[slot], bias_out.at[step], sems.at[0, slot]),
            pltpu.make_async_copy(gate_ref.at[slot], gate_out.at[step], sems.at[1, slot]),
        )

    @pl.loop(0, steps)
    def _(step):
        slot = step & 1

        @pl.when(step >= 2)
        def _():
            for copy in copies(step - 2, slot):
                copy.wait()

        edge_t[...] = edge_ref[lists[0, step]].astype(jnp.float32)
        scale = scale_ref[...]
        shift = shift_ref[...]

        def channels(row):
            line = jnp.broadcast_to(edge_t[row : row + 1, :], scale.shape)
            return jnp.tanh((line * scale + shift).astype(jnp.bfloat16))

        def build(part):
            return jnp.concatenate(
                [
                    jnp.concatenate(
                        [channels(part * 16 + half * 8 + within) for within in range(8)], axis=0
                    )
                    for half in range(2)
                ],
                axis=1,
            )

        for part in range(rows // 16):
            terms = jnp.dot(mix_ref[...], build(part), preferred_element_type=jnp.float32)
            span = slice(part * 16, part * 16 + 16)
            for head in range(heads):
                block = terms[head * 8 : head * 8 + 8]
                both = jnp.concatenate([block[:, :lanes], block[:, lanes:]], axis=0)
                bias_ref[slot, head, span, :] = both.astype(jnp.bfloat16)
                block = terms[(heads + head) * 8 : (heads + head) * 8 + 8]
                both = jnp.concatenate([block[:, :lanes], block[:, lanes:]], axis=0)
                gate_ref[slot, head, span, :] = (
                    0.5 + 0.5 * jnp.tanh(both + offsets[heads + head])
                ).astype(jnp.bfloat16)

        for copy in copies(step, slot):
            copy.start()

    @pl.when(steps >= 2)
    def _():
        for copy in copies(steps - 2, steps & 1):
            copy.wait()

    for copy in copies(steps - 1, (steps - 1) & 1):
        copy.wait()


def edge_stage(lists, offsets, edges, mix, scale, shift, heads):
    tiles, rows, lanes = edges.shape
    scalars = pl.BlockSpec(memory_space=pltpu.SMEM)
    held = pl.BlockSpec(memory_space=pltpu.VMEM)
    return pl.pallas_call(
        edge_kernel,
        in_specs=[scalars, scalars, held, held, held, held],
        out_specs=[pl.BlockSpec(memory_space=pl.ANY)] * 2,
        out_shape=[jax.ShapeDtypeStruct((tiles, heads, rows, lanes), jnp.bfloat16)] * 2,
        scratch_shapes=[
            pltpu.VMEM((rows, lanes), jnp.float32),
            pltpu.VMEM((2, heads, rows, lanes), jnp.bfloat16),
            pltpu.VMEM((2, heads, rows, lanes), jnp.bfloat16),
            pltpu.VMEM((8 * mix.shape[0], 4 * mix.shape[1]), jnp.bfloat16),
            pltpu.SemaphoreType.DMA((2, 2)),
        ],
        compiler_params=pltpu.CompilerParams(vmem_limit_bytes=EDGE_VMEM),
        cost_estimate=pl.CostEstimate(
            flops=tiles * 2 * rows * lanes * 64 * 256 * 2,
            bytes_accessed=tiles * rows * lanes * heads * 4,
            transcendentals=tiles * rows * lanes * 80,
        ),
        name="edge_terms",
    )(lists, offsets, edges, mix, scale, shift)


def attend_kernel(
    first_head,
    lists,
    slopes,
    offsets,
    edge_ref,
    bias_in,
    gate_in,
    key_ref,
    value_ref,
    *rest,
):
    *query_refs, num_ref, query_pairs, acc, tops, totals, bias_ref, gate_ref, sems = rest
    heads, rows, lanes = bias_ref.shape[1:]
    head_dim = acc.shape[0] // heads
    steps = lists[8, 0]

    def copies(step, slot):
        span = slice(first_head, first_head + heads)
        return (
            pltpu.make_async_copy(bias_in.at[step, span], bias_ref.at[slot], sems.at[0, slot]),
            pltpu.make_async_copy(gate_in.at[step, span], gate_ref.at[slot], sems.at[1, slot]),
        )

    for copy in copies(0, 0):
        copy.start()

    @pl.loop(0, steps)
    def _(step):
        slot = step & 1

        @pl.when(step + 1 < steps)
        def _():
            for copy in copies(step + 1, 1 - slot):
                copy.start()

        for copy in copies(step, slot):
            copy.wait()

        @pl.when(lists[5, step] > 0)
        def _():
            acc[...] = jnp.zeros_like(acc)
            tops[...] = jnp.full_like(tops, NEG_FILL)
            totals[...] = jnp.zeros_like(totals)
            blank = jnp.zeros((head_dim, lanes), jnp.bfloat16)
            for pair in range(heads // 2):
                query_pairs[pair, :head_dim, lanes:] = blank
                query_pairs[pair, head_dim:, :lanes] = blank
            for place, query_ref in enumerate(query_refs):

                @pl.when(lists[7, step] == place)
                def _(query_ref=query_ref):
                    for pair in range(heads // 2):
                        at = (first_head + pair * 2) * head_dim
                        query_pairs[pair, :head_dim, :lanes] = query_ref[at : at + head_dim, :]
                        at += head_dim
                        query_pairs[pair, head_dim:, lanes:] = query_ref[at : at + head_dim, :]

        @pl.when(lists[4, step] > 0)
        def _():
            key_block = lists[3, step]
            edge_t = edge_ref[lists[0, step]].astype(jnp.float32)
            for pair in range(heads // 2):
                width = 2 * head_dim
                keys = key_ref[key_block, :, pair * width : (pair + 1) * width]
                both = jnp.dot(keys, query_pairs[pair], preferred_element_type=jnp.float32)
                for side in range(2):
                    head = pair * 2 + side
                    span = slice(head * head_dim, (head + 1) * head_dim)
                    scores = both[:, side * lanes : (side + 1) * lanes] + (
                        bias_ref[slot, head].astype(jnp.float32) + (
                            edge_t * slopes[first_head + head] + offsets[first_head + head]
                        )
                    )
                    old_top = tops[head : head + 1, :]
                    new_top = jnp.maximum(old_top, jnp.max(scores, axis=0, keepdims=True))
                    factor = jnp.exp(old_top - new_top)
                    weights = jnp.exp(scores - new_top)
                    totals[head : head + 1, :] = totals[head : head + 1, :] * factor + jnp.sum(
                        weights, axis=0, keepdims=True
                    )
                    tops[head : head + 1, :] = new_top
                    gated = (weights * gate_ref[slot, head].astype(jnp.float32)).astype(jnp.bfloat16)
                    part = jnp.dot(
                        value_ref[key_block, span, :], gated, preferred_element_type=jnp.float32
                    )
                    acc[span, :] = acc[span, :] * factor + part

        @pl.when(lists[6, step] > 0)
        def _():
            for head in range(heads):
                span = slice(head * head_dim, (head + 1) * head_dim)
                total = totals[head : head + 1, :]
                inverse = jnp.where(total > 0.0, 1.0 / jnp.where(total > 0.0, total, 1.0), 0.0)
                num_ref[lists[2, step], span, :] = (acc[span, :] * inverse).astype(num_ref.dtype)
            at = acc.shape[0]
            rest = tops[...]
            for _ in range(TOP_PIECES):
                piece = rest.astype(num_ref.dtype)
                num_ref[lists[2, step], at : at + heads, :] = piece
                rest = rest - piece.astype(jnp.float32)
                at += heads
            rest = totals[...]
            for _ in range(TOTAL_PIECES):
                piece = rest.astype(num_ref.dtype)
                num_ref[lists[2, step], at : at + heads, :] = piece
                rest = rest - piece.astype(jnp.float32)
                at += heads


def attend_stage(part, part_count, lists, slopes, offsets, edges, bias, gate, keys, values, queries):
    block_total = len(queries)
    tiles, heads, rows, lanes = bias.shape
    heads //= part_count
    width = queries[0].shape[0] // part_count
    packed = width + heads * (TOP_PIECES + TOTAL_PIECES)
    scalars = pl.BlockSpec(memory_space=pltpu.SMEM)
    held = pl.BlockSpec(memory_space=pltpu.VMEM)
    far = pl.BlockSpec(memory_space=pl.ANY)
    return pl.pallas_call(
        functools.partial(attend_kernel, part * heads),
        in_specs=[scalars] * 3 + [held, far, far] + [held] * (2 + block_total),
        out_specs=held,
        out_shape=jax.ShapeDtypeStruct((block_total, packed, lanes), jnp.bfloat16),
        scratch_shapes=[
            pltpu.VMEM((heads // 2, 2 * width // heads, 2 * lanes), jnp.bfloat16),
            pltpu.VMEM((width, lanes), jnp.float32),
            pltpu.VMEM((heads, lanes), jnp.float32),
            pltpu.VMEM((heads, lanes), jnp.float32),
            pltpu.VMEM((2, heads, rows, lanes), jnp.bfloat16),
            pltpu.VMEM((2, heads, rows, lanes), jnp.bfloat16),
            pltpu.SemaphoreType.DMA((2, 2)),
        ],
        compiler_params=pltpu.CompilerParams(vmem_limit_bytes=ATTEND_VMEM),
        cost_estimate=pl.CostEstimate(
            flops=tiles * 16 * rows * lanes * width,
            bytes_accessed=tiles * rows * lanes * heads * 4,
            transcendentals=tiles * rows * lanes * heads,
        ),
        name="attend",
    )(lists, slopes, offsets, edges, bias, gate, keys, values, *queries)


def join_part(parts_ref, attended):
    width = attended.shape[0]
    count = parts_ref.shape[0]
    heads = (parts_ref.shape[1] - width) // (TOP_PIECES + TOTAL_PIECES)
    head_dim = width // heads

    def rejoin(part, first, pieces):
        whole = jnp.zeros((heads, attended.shape[1]), jnp.float32)
        for piece in range(pieces):
            at = width + (first + piece) * heads
            whole = whole + parts_ref[part, at : at + heads, :].astype(jnp.float32)
        return whole

    tops = [rejoin(part, 0, TOP_PIECES) for part in range(count)]
    top = functools.reduce(jnp.maximum, tops)
    shares = [
        rejoin(part, TOP_PIECES, TOTAL_PIECES) * jnp.exp(tops[part] - top)
        for part in range(count)
    ]
    inverse = 1.0 / functools.reduce(jnp.add, shares)
    shares = [share * inverse for share in shares]
    for head in range(heads):
        span = slice(head * head_dim, (head + 1) * head_dim)
        merged = jnp.zeros((head_dim, attended.shape[1]), jnp.float32)
        for part in range(count):
            merged = merged + parts_ref[part, span, :].astype(jnp.float32) * (
                shares[part][head : head + 1]
            )
        attended[span, :] = merged


def join_kernel(*refs):
    *parts, embedded_ref, out_ref, residual, normed, attended = refs
    width = attended.shape[0] // len(parts)
    for at, parts_ref in enumerate(parts):
        join_part(parts_ref, attended.at[at * width : (at + 1) * width])
    rows = attended[...].T.astype(jnp.bfloat16)
    values = embedded_ref[...] + jnp.dot(
        rows, out_ref[...], preferred_element_type=jnp.float32
    )
    residual[...] = values
    normed[...] = layer_norm(values).astype(jnp.bfloat16)


def join_stage(parts, embedded, w_out):
    rows, width = embedded.shape
    return pl.pallas_call(
        join_kernel,
        out_shape=[
            jax.ShapeDtypeStruct((rows, width), jnp.float32),
            jax.ShapeDtypeStruct((rows, width), jnp.bfloat16),
        ],
        scratch_shapes=[pltpu.VMEM((width, parts[0].shape[2]), jnp.float32)],
        compiler_params=pltpu.CompilerParams(vmem_limit_bytes=JOIN_VMEM),
        name="join",
    )(*parts, embedded, w_out)


def feed_kernel(own_ref, other_ref, weight_in, own_sum, other_sum, normed, acc, weight_ref, sems):
    rows, width = own_ref.shape
    shards, depth, span = weight_ref.shape
    group = shards // sems.shape[0]
    tall = depth // 2
    units = span // 2

    def fetch(step):
        part = pl.ds(step * group, group)
        return pltpu.make_async_copy(weight_in.at[part], weight_ref.at[part], sems.at[step])

    for step in range(shards // group):
        fetch(step).start()
    normed[:rows, :] = own_ref[...]
    normed[rows:, :] = other_ref[...]
    acc[...] = jnp.zeros_like(acc)

    @pl.loop(0, shards // group)
    def _(step):
        fetch(step).wait()
        pre = jnp.zeros((2 * rows, group * units), jnp.float32)
        for piece in range(width // tall):
            up = jnp.concatenate(
                [
                    weight_ref[step * group + at, :tall, piece * units : (piece + 1) * units]
                    for at in range(group)
                ],
                axis=1,
            )
            pre = pre + jnp.dot(
                normed[:, piece * tall : (piece + 1) * tall],
                up,
                preferred_element_type=jnp.float32,
            )
        hidden = (0.5 * pre * (1.0 + lax.erf(pre * (0.5**0.5)))).astype(jnp.bfloat16)
        for piece in range(width // span):
            down = jnp.concatenate(
                [
                    weight_ref[
                        step * group + at, tall + piece * units : tall + (piece + 1) * units, :
                    ]
                    for at in range(group)
                ],
                axis=0,
            )
            acc[:, piece * span : (piece + 1) * span] += jnp.dot(
                hidden, down, preferred_element_type=jnp.float32
            )

    own_sum[...] = acc[:rows, :]
    other_sum[...] = acc[rows:, :]


def feed_stage(own, other, weights):
    shards = weights.shape[0]
    rows, width = own.shape
    group = 2
    held = pl.BlockSpec(memory_space=pltpu.VMEM)
    return pl.pallas_call(
        feed_kernel,
        in_specs=[held, held, pl.BlockSpec(memory_space=pl.ANY)],
        out_specs=[held, held],
        out_shape=[jax.ShapeDtypeStruct((rows, width), jnp.float32)] * 2,
        scratch_shapes=[
            pltpu.VMEM((2 * rows, width), jnp.bfloat16),
            pltpu.VMEM((2 * rows, width), jnp.float32),
            pltpu.VMEM(weights.shape, weights.dtype),
            pltpu.SemaphoreType.DMA((shards // group,)),
        ],
        compiler_params=pltpu.CompilerParams(vmem_limit_bytes=FEED_VMEM),
        name="feed",
    )(own, other, weights)


def half_kernel(core, up_ref, down_ref, out_ref):
    tall = up_ref.shape[0] // 2
    units, width = down_ref.shape
    span = 2 * units
    out_ref[:tall, :units] = up_ref[:tall, :]
    out_ref[:tall, units:] = up_ref[tall:, :]
    for piece in range(width // span):
        out_ref[tall + piece * units : tall + (piece + 1) * units, :] = down_ref[
            :, piece * span : (piece + 1) * span
        ]


def half_weights(w_up, w_down, core):
    width, span = w_up.shape
    units = span // 2
    grid_spec = pltpu.PrefetchScalarGridSpec(
        num_scalar_prefetch=1,
        grid=(1,),
        in_specs=[
            pl.BlockSpec((width, units), lambda s, core: (0, core[0])),
            pl.BlockSpec((units, width), lambda s, core: (core[0], 0)),
        ],
        out_specs=pl.BlockSpec((width, span), lambda s, core: (0, 0)),
    )
    return pl.pallas_call(
        half_kernel,
        grid_spec=grid_spec,
        out_shape=jax.ShapeDtypeStruct((width, span), w_up.dtype),
        name="half_weights",
    )(core.reshape(1), w_up, w_down)


def scaled_projection(edge_proj, heads):
    outs = edge_proj.shape[1]
    factors = jnp.where(jnp.arange(outs) < heads, 0.5, 0.25)
    scaled = (edge_proj.astype(jnp.float32) * factors[None, :]).T
    return jnp.concatenate([scaled, scaled], axis=1), jnp.sum(scaled, axis=1)


def shift_chip(value, by):
    return lax.ppermute(value, "kcol", [(i, (i + 2 * by) & 7) for i in range(8)])


def after(value, others):
    return lax.optimization_barrier((value, others))[0]


def swap_core(value):
    return lax.ppermute(value, "kcol", [(i, i ^ 1) for i in range(8)])


def local(
    features,
    node_ids,
    token_embed,
    w_query,
    w_key,
    w_value,
    w_out,
    slopes,
    chan_scale,
    chan_shift,
    edge_proj,
    edge_value,
    key_index,
    counts,
    w_up,
    w_down,
):
    node_dev, width = features.shape
    vocab_size = token_embed.shape[0]
    heads = slopes.shape[0]
    head_dim = width // heads
    rows = edge_value.shape[-1]
    col_at = lax.axis_index("kcol")
    core = col_at & 1
    one_hot = (
        node_ids[:, None] == lax.broadcasted_iota(jnp.int32, (node_dev, vocab_size), 1)
    ).astype(jnp.bfloat16)
    embedded = features.astype(jnp.float32) + jnp.dot(
        one_hot, token_embed, preferred_element_type=jnp.float32
    )
    normed = layer_norm(embedded).astype(jnp.bfloat16)

    column_nodes = lax.all_gather(normed, "qrow", axis=0)
    query_own = (
        jnp.einsum("kd,nk->dn", w_query, normed, preferred_element_type=jnp.float32).astype(
            jnp.bfloat16
        )
        * jnp.bfloat16(head_dim ** (-0.5))
    )
    weights = half_weights(w_up, w_down, core)
    queries = [query_own] + [shift_chip(query_own, by) for by in (1, -1, 2)]
    weights = lax.all_gather(after(weights, query_own), "qrow", axis=0)
    lists = list_stage(counts, key_index[:, 0], jnp.stack([col_at >> 1, core]))
    mix, offsets = scaled_projection(edge_proj, heads)
    spread = lambda vector: jnp.broadcast_to((0.5 * vector)[:, None], (vector.shape[0], rows))
    edges = jnp.swapaxes(edge_value.reshape(-1, rows, rows), 1, 2)
    scale, shift = spread(chan_scale), spread(chan_shift)
    *queries, lists, mix, offsets, scale, shift, edges = lax.optimization_barrier(
        (*queries, lists, mix, offsets, scale, shift, edges)
    )
    queries = queries + [swap_core(query) for query in queries]
    bias, gate = edge_stage(after(lists, queries), offsets, edges, mix, scale, shift, heads)
    column_nodes, bias = lax.optimization_barrier((column_nodes, bias))
    parts = []
    for part in range(HEAD_PARTS):
        span = slice(part * width // HEAD_PARTS, (part + 1) * width // HEAD_PARTS)
        keys = jnp.einsum(
            "gnk,kd->gnd", column_nodes, w_key[:, span], preferred_element_type=jnp.float32
        ).astype(jnp.bfloat16)
        values = jnp.einsum(
            "kd,gnk->gdn", w_value[:, span], column_nodes, preferred_element_type=jnp.float32
        ).astype(jnp.bfloat16)
        piece = attend_stage(
            part, HEAD_PARTS, lists, slopes, offsets, edges, bias, gate, keys, values, queries
        )
        column_nodes = after(column_nodes, piece)
        parts.append(lax.all_to_all(after(piece, parts), "kcol", 0, 0, tiled=True))
    residual, normed_two = join_stage(parts, embedded, w_out)
    normed_other = swap_core(normed_two)
    weights, normed_other = lax.optimization_barrier((weights, normed_other))
    own_sum, other_sum = feed_stage(normed_two, normed_other, weights)
    return (residual + (own_sum + swap_core(other_sum))).astype(jnp.bfloat16)


def solution(mesh):
    placed = (
        P(("qrow", "kcol"), None),
        P(("qrow", "kcol")),
        P(),
        P(),
        P(),
        P(),
        P(),
        P(),
        P(),
        P(),
        P(),
        P("qrow", "kcol", None, None, None),
        P("qrow", "kcol", None),
        P("qrow", "kcol"),
        P(None, "qrow"),
        P("qrow", None),
    )
    return jax.shard_map(
        local, mesh=mesh, in_specs=placed, out_specs=P(("qrow", "kcol"), None), check_vma=False
    )
```

```python
import functools

import jax
import jax.numpy as jnp
from jax import lax
from jax.experimental import pallas as pl
from jax.experimental.pallas import tpu as pltpu
from jax.sharding import PartitionSpec as P

NEG_FILL = -1e30
HEAD_PARTS = 1
TOP_PIECES = 3
TOTAL_PIECES = 3
EDGE_VMEM = 56 * 1024 * 1024
ATTEND_VMEM = 36 * 1024 * 1024
JOIN_VMEM = 24 * 1024 * 1024
FEED_VMEM = 52 * 1024 * 1024


def layer_norm(values):
    average = jnp.mean(values, axis=-1, keepdims=True)
    centered = values - average
    spread = jnp.mean(centered * centered, axis=-1, keepdims=True)
    return centered * lax.rsqrt(spread + 1e-05)


def list_kernel(counts_ref, index_ref, place_ref, lists_ref):
    block_total, slot_count = index_ref.shape
    total = block_total * slot_count
    chip, core = place_ref[0], place_ref[1]

    def relative(theirs, ours):
        gap = (theirs - ours + 4) & 3
        return jnp.where(gap == 0, 0, jnp.where(gap == 3, 1, gap + 1))

    filled = jnp.int32(0)
    for block in range(block_total):
        count = counts_ref[block, 0]
        partner = jnp.where(core == block % 2, 0, 4) + relative(jnp.int32(block // 2), chip)
        visits = jnp.maximum(count, 1)
        for slot in range(slot_count):

            @pl.when(slot < visits)
            def _(at=filled, block=block, slot=slot, partner=partner, count=count, visits=visits):
                key_block = index_ref[block, slot]
                lists_ref[0, at] = jnp.int32(block * slot_count + slot)
                lists_ref[1, at] = at
                lists_ref[2, at] = jnp.int32(block)
                lists_ref[3, at] = key_block
                lists_ref[4, at] = (slot < count).astype(jnp.int32)
                lists_ref[5, at] = jnp.int32(slot == 0)
                lists_ref[6, at] = (visits == slot + 1).astype(jnp.int32)
                lists_ref[7, at] = partner

            filled = filled + (slot < visits).astype(jnp.int32)

    @pl.loop(0, total)
    def _(step):
        lists_ref[8, step] = filled

        @pl.when(step >= filled)
        def _():
            for row in range(8):
                lists_ref[row, step] = jnp.int32(0)


def list_stage(counts, index, place):
    scalars = pl.BlockSpec(memory_space=pltpu.SMEM)
    return pl.pallas_call(
        list_kernel,
        in_specs=[scalars] * 3,
        out_specs=scalars,
        out_shape=jax.ShapeDtypeStruct((9, index.shape[0] * index.shape[1]), jnp.int32),
        name="lists",
    )(counts, index, place)


def edge_kernel(
    lists,
    offsets,
    edge_ref,
    proj_ref,
    scales,
    shifts,
    bias_out,
    gate_out,
    edge_t,
    bias_ref,
    gate_ref,
    mix_ref,
    scale_ref,
    shift_ref,
    sems,
):
    heads = bias_ref.shape[1]
    rows, lanes = edge_t.shape

    steps = lists[8, 0]

    for channel in range(scale_ref.shape[0]):
        line = (1, scale_ref.shape[1])
        scale_ref[channel : channel + 1, :] = jnp.full(line, 0.5 * scales[channel], jnp.float32)
        shift_ref[channel : channel + 1, :] = jnp.full(line, 0.5 * shifts[channel], jnp.float32)

    outs, columns = proj_ref.shape
    spread = jnp.broadcast_to(proj_ref[...][:, None, :], (outs, 8, columns)).reshape(
        8 * outs, columns
    )
    node = lax.broadcasted_iota(jnp.int32, spread.shape, 0) & 7
    second = (lax.broadcasted_iota(jnp.int32, spread.shape, 1) >= columns // 2).astype(jnp.int32)
    for piece in range(4):
        mix_ref[:, piece * columns : (piece + 1) * columns] = jnp.where(
            node == 2 * piece + second, spread, 0.0
        ).astype(jnp.bfloat16)

    def copies(step, slot):
        return (
            pltpu.make_async_copy(bias_ref.at[slot], bias_out.at[step], sems.at[0, slot]),
            pltpu.make_async_copy(gate_ref.at[slot], gate_out.at[step], sems.at[1, slot]),
        )

    @pl.loop(0, steps)
    def _(step):
        slot = step & 1

        @pl.when(step >= 2)
        def _():
            for copy in copies(step - 2, slot):
                copy.wait()

        edge_t[...] = edge_ref[lists[0, step]].astype(jnp.float32)
        scale = scale_ref[...]
        shift = shift_ref[...]

        def channels(row):
            line = jnp.broadcast_to(edge_t[row : row + 1, :], scale.shape)
            return jnp.tanh((line * scale + shift).astype(jnp.bfloat16))

        def build(part):
            return jnp.concatenate(
                [
                    jnp.concatenate(
                        [channels(part * 16 + half * 8 + within) for within in range(8)], axis=0
                    )
                    for half in range(2)
                ],
                axis=1,
            )

        for part in range(rows // 16):
            terms = jnp.dot(mix_ref[...], build(part), preferred_element_type=jnp.float32)
            span = slice(part * 16, part * 16 + 16)
            for head in range(heads):
                block = terms[head * 8 : head * 8 + 8]
                both = jnp.concatenate([block[:, :lanes], block[:, lanes:]], axis=0)
                bias_ref[slot, head, span, :] = both.astype(jnp.bfloat16)
                block = terms[(heads + head) * 8 : (heads + head) * 8 + 8]
                both = jnp.concatenate([block[:, :lanes], block[:, lanes:]], axis=0)
                gate_ref[slot, head, span, :] = (
                    0.5 + 0.5 * jnp.tanh(both + offsets[heads + head])
                ).astype(jnp.bfloat16)

        for copy in copies(step, slot):
            copy.start()

    @pl.when(steps >= 2)
    def _():
        for copy in copies(steps - 2, steps & 1):
            copy.wait()

    for copy in copies(steps - 1, (steps - 1) & 1):
        copy.wait()


def edge_stage(lists, offsets, edges, mix, scale, shift, heads):
    tiles, rows, lanes = edges.shape
    scalars = pl.BlockSpec(memory_space=pltpu.SMEM)
    held = pl.BlockSpec(memory_space=pltpu.VMEM)
    return pl.pallas_call(
        edge_kernel,
        in_specs=[scalars, scalars, held, held, scalars, scalars],
        out_specs=[pl.BlockSpec(memory_space=pl.ANY)] * 2,
        out_shape=[jax.ShapeDtypeStruct((tiles, heads, rows, lanes), jnp.bfloat16)] * 2,
        scratch_shapes=[
            pltpu.VMEM((rows, lanes), jnp.float32),
            pltpu.VMEM((2, heads, rows, lanes), jnp.bfloat16),
            pltpu.VMEM((2, heads, rows, lanes), jnp.bfloat16),
            pltpu.VMEM((8 * mix.shape[0], 4 * mix.shape[1]), jnp.bfloat16),
            pltpu.VMEM((scale.shape[0], lanes), jnp.float32),
            pltpu.VMEM((shift.shape[0], lanes), jnp.float32),
            pltpu.SemaphoreType.DMA((2, 2)),
        ],
        compiler_params=pltpu.CompilerParams(vmem_limit_bytes=EDGE_VMEM),
        cost_estimate=pl.CostEstimate(
            flops=tiles * 2 * rows * lanes * 64 * 256 * 2,
            bytes_accessed=tiles * rows * lanes * heads * 4,
            transcendentals=tiles * rows * lanes * 80,
        ),
        name="edge_terms",
    )(lists, offsets, edges, mix, scale, shift)


def attend_kernel(
    first_head,
    lists,
    slopes,
    offsets,
    edge_ref,
    bias_in,
    gate_in,
    key_ref,
    value_ref,
    *rest,
):
    *query_refs, num_ref, query_pairs, acc, tops, totals, bias_ref, gate_ref, sems = rest
    heads, rows, lanes = bias_ref.shape[1:]
    head_dim = acc.shape[0] // heads
    steps = lists[8, 0]

    def copies(step, slot):
        span = slice(first_head, first_head + heads)
        return (
            pltpu.make_async_copy(bias_in.at[step, span], bias_ref.at[slot], sems.at[0, slot]),
            pltpu.make_async_copy(gate_in.at[step, span], gate_ref.at[slot], sems.at[1, slot]),
        )

    for copy in copies(0, 0):
        copy.start()

    @pl.loop(0, steps)
    def _(step):
        slot = step & 1

        @pl.when(step + 1 < steps)
        def _():
            for copy in copies(step + 1, 1 - slot):
                copy.start()

        for copy in copies(step, slot):
            copy.wait()

        @pl.when(lists[5, step] > 0)
        def _():
            acc[...] = jnp.zeros_like(acc)
            tops[...] = jnp.full_like(tops, NEG_FILL)
            totals[...] = jnp.zeros_like(totals)
            blank = jnp.zeros((head_dim, lanes), jnp.bfloat16)
            for pair in range(heads // 2):
                query_pairs[pair, :head_dim, lanes:] = blank
                query_pairs[pair, head_dim:, :lanes] = blank
            for place, query_ref in enumerate(query_refs):

                @pl.when(lists[7, step] == place)
                def _(query_ref=query_ref):
                    for pair in range(heads // 2):
                        at = (first_head + pair * 2) * head_dim
                        query_pairs[pair, :head_dim, :lanes] = query_ref[at : at + head_dim, :]
                        at += head_dim
                        query_pairs[pair, head_dim:, lanes:] = query_ref[at : at + head_dim, :]

        @pl.when(lists[4, step] > 0)
        def _():
            key_block = lists[3, step]
            edge_t = edge_ref[lists[0, step]].astype(jnp.float32)
            for pair in range(heads // 2):
                width = 2 * head_dim
                keys = key_ref[key_block, :, pair * width : (pair + 1) * width]
                both = jnp.dot(keys, query_pairs[pair], preferred_element_type=jnp.float32)
                for side in range(2):
                    head = pair * 2 + side
                    span = slice(head * head_dim, (head + 1) * head_dim)
                    scores = both[:, side * lanes : (side + 1) * lanes] + (
                        bias_ref[slot, head].astype(jnp.float32) + (
                            edge_t * slopes[first_head + head] + offsets[first_head + head]
                        )
                    )
                    old_top = tops[head : head + 1, :]
                    new_top = jnp.maximum(old_top, jnp.max(scores, axis=0, keepdims=True))
                    factor = jnp.exp(old_top - new_top)
                    weights = jnp.exp(scores - new_top)
                    totals[head : head + 1, :] = totals[head : head + 1, :] * factor + jnp.sum(
                        weights, axis=0, keepdims=True
                    )
                    tops[head : head + 1, :] = new_top
                    gated = (weights * gate_ref[slot, head].astype(jnp.float32)).astype(jnp.bfloat16)
                    part = jnp.dot(
                        value_ref[key_block, span, :], gated, preferred_element_type=jnp.float32
                    )
                    acc[span, :] = acc[span, :] * factor + part

        @pl.when(lists[6, step] > 0)
        def _():
            for head in range(heads):
                span = slice(head * head_dim, (head + 1) * head_dim)
                total = totals[head : head + 1, :]
                inverse = jnp.where(total > 0.0, 1.0 / jnp.where(total > 0.0, total, 1.0), 0.0)
                num_ref[lists[2, step], span, :] = (acc[span, :] * inverse).astype(num_ref.dtype)
            at = acc.shape[0]
            rest = tops[...]
            for _ in range(TOP_PIECES):
                piece = rest.astype(num_ref.dtype)
                num_ref[lists[2, step], at : at + heads, :] = piece
                rest = rest - piece.astype(jnp.float32)
                at += heads
            rest = totals[...]
            for _ in range(TOTAL_PIECES):
                piece = rest.astype(num_ref.dtype)
                num_ref[lists[2, step], at : at + heads, :] = piece
                rest = rest - piece.astype(jnp.float32)
                at += heads


def attend_stage(part, part_count, lists, slopes, offsets, edges, bias, gate, keys, values, queries):
    block_total = len(queries)
    tiles, heads, rows, lanes = bias.shape
    heads //= part_count
    width = queries[0].shape[0] // part_count
    packed = width + heads * (TOP_PIECES + TOTAL_PIECES)
    scalars = pl.BlockSpec(memory_space=pltpu.SMEM)
    held = pl.BlockSpec(memory_space=pltpu.VMEM)
    far = pl.BlockSpec(memory_space=pl.ANY)
    return pl.pallas_call(
        functools.partial(attend_kernel, part * heads),
        in_specs=[scalars] * 3 + [held, far, far] + [held] * (2 + block_total),
        out_specs=held,
        out_shape=jax.ShapeDtypeStruct((block_total, packed, lanes), jnp.bfloat16),
        scratch_shapes=[
            pltpu.VMEM((heads // 2, 2 * width // heads, 2 * lanes), jnp.bfloat16),
            pltpu.VMEM((width, lanes), jnp.float32),
            pltpu.VMEM((heads, lanes), jnp.float32),
            pltpu.VMEM((heads, lanes), jnp.float32),
            pltpu.VMEM((2, heads, rows, lanes), jnp.bfloat16),
            pltpu.VMEM((2, heads, rows, lanes), jnp.bfloat16),
            pltpu.SemaphoreType.DMA((2, 2)),
        ],
        compiler_params=pltpu.CompilerParams(vmem_limit_bytes=ATTEND_VMEM),
        cost_estimate=pl.CostEstimate(
            flops=tiles * 16 * rows * lanes * width,
            bytes_accessed=tiles * rows * lanes * heads * 4,
            transcendentals=tiles * rows * lanes * heads,
        ),
        name="attend",
    )(lists, slopes, offsets, edges, bias, gate, keys, values, *queries)


def join_part(parts_ref, attended):
    width = attended.shape[0]
    count = parts_ref.shape[0]
    heads = (parts_ref.shape[1] - width) // (TOP_PIECES + TOTAL_PIECES)
    head_dim = width // heads

    def rejoin(part, first, pieces):
        whole = jnp.zeros((heads, attended.shape[1]), jnp.float32)
        for piece in range(pieces):
            at = width + (first + piece) * heads
            whole = whole + parts_ref[part, at : at + heads, :].astype(jnp.float32)
        return whole

    tops = [rejoin(part, 0, TOP_PIECES) for part in range(count)]
    top = functools.reduce(jnp.maximum, tops)
    shares = [
        rejoin(part, TOP_PIECES, TOTAL_PIECES) * jnp.exp(tops[part] - top)
        for part in range(count)
    ]
    inverse = 1.0 / functools.reduce(jnp.add, shares)
    shares = [share * inverse for share in shares]
    for head in range(heads):
        span = slice(head * head_dim, (head + 1) * head_dim)
        merged = jnp.zeros((head_dim, attended.shape[1]), jnp.float32)
        for part in range(count):
            merged = merged + parts_ref[part, span, :].astype(jnp.float32) * (
                shares[part][head : head + 1]
            )
        attended[span, :] = merged


def join_kernel(*refs):
    *parts, embedded_ref, out_ref, residual, normed, attended = refs
    width = attended.shape[0] // len(parts)
    for at, parts_ref in enumerate(parts):
        join_part(parts_ref, attended.at[at * width : (at + 1) * width])
    rows = attended[...].T.astype(jnp.bfloat16)
    values = embedded_ref[...] + jnp.dot(
        rows, out_ref[...], preferred_element_type=jnp.float32
    )
    residual[...] = values
    normed[...] = layer_norm(values).astype(jnp.bfloat16)


def join_stage(parts, embedded, w_out):
    rows, width = embedded.shape
    return pl.pallas_call(
        join_kernel,
        out_shape=[
            jax.ShapeDtypeStruct((rows, width), jnp.float32),
            jax.ShapeDtypeStruct((rows, width), jnp.bfloat16),
        ],
        scratch_shapes=[pltpu.VMEM((width, parts[0].shape[2]), jnp.float32)],
        compiler_params=pltpu.CompilerParams(vmem_limit_bytes=JOIN_VMEM),
        name="join",
    )(*parts, embedded, w_out)


def feed_kernel(own_ref, other_ref, weight_in, own_sum, other_sum, normed, acc, weight_ref, sems):
    rows, width = own_ref.shape
    shards, depth, span = weight_ref.shape
    group = shards // sems.shape[0]
    tall = depth // 2
    units = span // 2

    def fetch(step):
        part = pl.ds(step * group, group)
        return pltpu.make_async_copy(weight_in.at[part], weight_ref.at[part], sems.at[step])

    for step in range(shards // group):
        fetch(step).start()
    normed[:rows, :] = own_ref[...]
    normed[rows:, :] = other_ref[...]
    acc[...] = jnp.zeros_like(acc)

    @pl.loop(0, shards // group)
    def _(step):
        fetch(step).wait()
        pre = jnp.zeros((2 * rows, group * units), jnp.float32)
        for piece in range(width // tall):
            up = jnp.concatenate(
                [
                    weight_ref[step * group + at, :tall, piece * units : (piece + 1) * units]
                    for at in range(group)
                ],
                axis=1,
            )
            pre = pre + jnp.dot(
                normed[:, piece * tall : (piece + 1) * tall],
                up,
                preferred_element_type=jnp.float32,
            )
        hidden = (0.5 * pre * (1.0 + lax.erf(pre * (0.5**0.5)))).astype(jnp.bfloat16)
        for piece in range(width // span):
            down = jnp.concatenate(
                [
                    weight_ref[
                        step * group + at, tall + piece * units : tall + (piece + 1) * units, :
                    ]
                    for at in range(group)
                ],
                axis=0,
            )
            acc[:, piece * span : (piece + 1) * span] += jnp.dot(
                hidden, down, preferred_element_type=jnp.float32
            )

    own_sum[...] = acc[:rows, :]
    other_sum[...] = acc[rows:, :]


def feed_stage(own, other, weights):
    shards = weights.shape[0]
    rows, width = own.shape
    group = 2
    held = pl.BlockSpec(memory_space=pltpu.VMEM)
    return pl.pallas_call(
        feed_kernel,
        in_specs=[held, held, pl.BlockSpec(memory_space=pl.ANY)],
        out_specs=[held, held],
        out_shape=[jax.ShapeDtypeStruct((rows, width), jnp.float32)] * 2,
        scratch_shapes=[
            pltpu.VMEM((2 * rows, width), jnp.bfloat16),
            pltpu.VMEM((2 * rows, width), jnp.float32),
            pltpu.VMEM(weights.shape, weights.dtype),
            pltpu.SemaphoreType.DMA((shards // group,)),
        ],
        compiler_params=pltpu.CompilerParams(vmem_limit_bytes=FEED_VMEM),
        name="feed",
    )(own, other, weights)


def half_kernel(core, up_ref, down_ref, out_ref):
    tall = up_ref.shape[0] // 2
    units, width = down_ref.shape
    span = 2 * units
    out_ref[:tall, :units] = up_ref[:tall, :]
    out_ref[:tall, units:] = up_ref[tall:, :]
    for piece in range(width // span):
        out_ref[tall + piece * units : tall + (piece + 1) * units, :] = down_ref[
            :, piece * span : (piece + 1) * span
        ]


def half_weights(w_up, w_down, core):
    width, span = w_up.shape
    units = span // 2
    grid_spec = pltpu.PrefetchScalarGridSpec(
        num_scalar_prefetch=1,
        grid=(1,),
        in_specs=[
            pl.BlockSpec((width, units), lambda s, core: (0, core[0])),
            pl.BlockSpec((units, width), lambda s, core: (core[0], 0)),
        ],
        out_specs=pl.BlockSpec((width, span), lambda s, core: (0, 0)),
    )
    return pl.pallas_call(
        half_kernel,
        grid_spec=grid_spec,
        out_shape=jax.ShapeDtypeStruct((width, span), w_up.dtype),
        name="half_weights",
    )(core.reshape(1), w_up, w_down)


def scaled_projection(edge_proj, heads):
    outs = edge_proj.shape[1]
    factors = jnp.where(jnp.arange(outs) < heads, 0.5, 0.25)
    scaled = (edge_proj.astype(jnp.float32) * factors[None, :]).T
    return jnp.concatenate([scaled, scaled], axis=1), jnp.sum(scaled, axis=1)


def shift_chip(value, by):
    return lax.ppermute(value, "kcol", [(i, (i + 2 * by) & 7) for i in range(8)])


def after(value, others):
    return lax.optimization_barrier((value, others))[0]


def swap_core(value):
    return lax.ppermute(value, "kcol", [(i, i ^ 1) for i in range(8)])


def local(
    features,
    node_ids,
    token_embed,
    w_query,
    w_key,
    w_value,
    w_out,
    slopes,
    chan_scale,
    chan_shift,
    edge_proj,
    edge_value,
    key_index,
    counts,
    w_up,
    w_down,
):
    node_dev, width = features.shape
    vocab_size = token_embed.shape[0]
    heads = slopes.shape[0]
    head_dim = width // heads
    rows = edge_value.shape[-1]
    col_at = lax.axis_index("kcol")
    core = col_at & 1
    one_hot = (
        node_ids[:, None] == lax.broadcasted_iota(jnp.int32, (node_dev, vocab_size), 1)
    ).astype(jnp.bfloat16)
    embedded = features.astype(jnp.float32) + jnp.dot(
        one_hot, token_embed, preferred_element_type=jnp.float32
    )
    normed = layer_norm(embedded).astype(jnp.bfloat16)

    column_nodes = lax.all_gather(normed, "qrow", axis=0)
    query_own = (
        jnp.einsum("kd,nk->dn", w_query, normed, preferred_element_type=jnp.float32).astype(
            jnp.bfloat16
        )
        * jnp.bfloat16(head_dim ** (-0.5))
    )
    weights = half_weights(w_up, w_down, core)
    queries = [query_own] + [shift_chip(query_own, by) for by in (1, -1, 2)]
    weights = lax.all_gather(after(weights, query_own), "qrow", axis=0)
    lists = list_stage(counts, key_index[:, 0], jnp.stack([col_at >> 1, core]))
    mix, offsets = scaled_projection(edge_proj, heads)
    edges = jnp.swapaxes(edge_value.reshape(-1, rows, rows), 1, 2)
    *queries, lists, mix, offsets, edges = lax.optimization_barrier(
        (*queries, lists, mix, offsets, edges)
    )
    queries = queries + [swap_core(query) for query in queries]
    bias, gate = edge_stage(after(lists, queries), offsets, edges, mix, chan_scale, chan_shift, heads)
    column_nodes, bias = lax.optimization_barrier((column_nodes, bias))
    parts = []
    for part in range(HEAD_PARTS):
        span = slice(part * width // HEAD_PARTS, (part + 1) * width // HEAD_PARTS)
        keys = jnp.einsum(
            "gnk,kd->gnd", column_nodes, w_key[:, span], preferred_element_type=jnp.float32
        ).astype(jnp.bfloat16)
        values = jnp.einsum(
            "kd,gnk->gdn", w_value[:, span], column_nodes, preferred_element_type=jnp.float32
        ).astype(jnp.bfloat16)
        piece = attend_stage(
            part, HEAD_PARTS, lists, slopes, offsets, edges, bias, gate, keys, values, queries
        )
        column_nodes = after(column_nodes, piece)
        parts.append(lax.all_to_all(after(piece, parts), "kcol", 0, 0, tiled=True))
    residual, normed_two = join_stage(parts, embedded, w_out)
    normed_other = swap_core(normed_two)
    weights, normed_other = lax.optimization_barrier((weights, normed_other))
    own_sum, other_sum = feed_stage(normed_two, normed_other, weights)
    return (residual + (own_sum + swap_core(other_sum))).astype(jnp.bfloat16)


def solution(mesh):
    placed = (
        P(("qrow", "kcol"), None),
        P(("qrow", "kcol")),
        P(),
        P(),
        P(),
        P(),
        P(),
        P(),
        P(),
        P(),
        P(),
        P("qrow", "kcol", None, None, None),
        P("qrow", "kcol", None),
        P("qrow", "kcol"),
        P(None, "qrow"),
        P("qrow", None),
    )
    return jax.shard_map(
        local, mesh=mesh, in_specs=placed, out_specs=P(("qrow", "kcol"), None), check_vma=False
    )
```
